32 devices in a mesh: fsdp: 8 (over z, x), sp: 4 (over y, core).
Axes of the slice: x: 2, y: 2, z: 4, core: 2. Of those that a mesh axis runs over, the one named last changes fastest.
Arguments:
- tokens: bfloat16 [2, 12288, 768], P(None, ('fsdp', 'sp')), may hold values from -6 to 6
- cotangent: bfloat16 [2, 12288, 768], P(None, ('fsdp', 'sp')), may hold values from -6 to 6
- lengths: int32 [2, 8, 3], P(None, 'fsdp'), may hold values from 1 to 1024, 1536 in all within a row
- dealing: int32 [2, 8, 1536], P(None, 'fsdp'), may hold values from 0 to 1535, each once within a row
- gain_attn: bfloat16 [768], P('fsdp'), may hold values from 0.099609375 to 1.8984375
- w_query: bfloat16 [768, 768], P('fsdp'), may hold values from -0.0546875 to 0.0546875
- w_key: bfloat16 [768, 768], P('fsdp'), may hold values from -0.21875 to 0.21875
- w_value: bfloat16 [768, 768], P('fsdp'), may hold values from -0.21875 to 0.21875
- w_out: bfloat16 [768, 768], P('fsdp'), may hold values from -0.875 to 0.875
- bias_table: bfloat16 [32, 12], P(None, 'sp'), may hold values from -4 to 4
- gain_ff: bfloat16 [768], P('fsdp'), may hold values from 0.099609375 to 1.8984375
- w_gate: bfloat16 [768, 2048], P('fsdp'), may hold values from -0.21875 to 0.21875
- w_up: bfloat16 [768, 2048], P('fsdp'), may hold values from -0.21875 to 0.21875
- w_down: bfloat16 [2048, 768], P('fsdp'), may hold values from -0.25 to 0.25
Outputs:
- output: bfloat16 [2, 12288, 768], P(None, ('fsdp', 'sp'))
- grad_tokens: bfloat16 [2, 12288, 768], P(None, ('fsdp', 'sp'))
- grad_gain_attn: float32 [768], P('fsdp')
- grad_query: float32 [768, 768], P('fsdp')
- grad_key: float32 [768, 768], P('fsdp')
- grad_value: float32 [768, 768], P('fsdp')
- grad_out: float32 [768, 768], P('fsdp')
- grad_bias: float32 [32, 12], P(None, 'sp')
- grad_gain_ff: float32 [768], P('fsdp')
- grad_gate: float32 [768, 2048], P('fsdp')
- grad_up: float32 [768, 2048], P('fsdp')
- grad_down: float32 [2048, 768], P('fsdp')
The draws below stay inside these ranges and needn't reach their ends.
Inputs may be any that keep to these rules, and one draw needn't show every extreme that they name: In every micro-batch and group the 3 lengths sum to 1536, and the longest is exactly 1024. Each row dealing[m, g] is a permutation of the 1536 arrival indices.
All inputs are finite; a program needn't handle non-finite values.
Results may differ from the reference program's by a relative error of at most 0.018.
Values may be sent and summed in bfloat16 or wider, within the bound.
A program may use at most 192 MiB of HBM per device.

```python
import math
import jax
import jax.numpy as jnp
import numpy as np
from jax import lax

D = 768
HEADS = 12
DH = 64
FF = 2048
BUCKETS = 32
MICRO = 2
SEQ_GRP = 3
GROUP = 1536
MAXLEN = 1024
PIECE = 48
TOKENS = 12288
N_FSDP = 8
N_SP = 4


def block_levels(key, shape, split, low, high):
    def one(dim, parts):
        draws = jax.random.uniform(jax.random.fold_in(jax.random.fold_in(key, 6), dim), (parts,), jnp.float32, low / len(split), high / len(split))
        return jnp.repeat(jnp.exp(draws), shape[dim] // parts).reshape((-1,) + (1,) * (len(shape) - dim - 1))

    loudness = one(*split[0])
    for cut in split[1:]:
        loudness = loudness * one(*cut)
    return loudness


def length_profile(number_of, total, reach, lean):
    weights = [(1 << 20) // math.isqrt(rank ** lean) + 1 for rank in range(2, number_of + 1)]
    rest, holding = total - reach - (number_of - 1), [1] * (number_of - 1)
    while rest > 0:
        movable = [i for i in range(number_of - 1) if holding[i] < reach]
        mass, remaining = sum([weights[i] for i in movable]), rest
        for i in movable:
            more = min(reach - holding[i], max(1, remaining * weights[i] // mass), rest)
            holding[i] = holding[i] + more
            rest = rest - more
    return np.array([reach] + holding)


def ragged(own_key, count, total, reach, skew):
    if count == 2:
        one = jax.random.randint(own_key, (), max(1, total - reach), min(reach, total - 1) + 1)
        return jnp.stack([one, total - one])
    sizes = jnp.asarray(length_profile(count, total, reach, skew), jnp.int32)
    twos = (count - 1) // 2
    giver, receiver = sizes[1:1 + 2 * twos:2], sizes[2:2 + 2 * twos:2]
    room = jnp.minimum(giver - 1, reach - receiver)
    shifted = jax.random.randint(jax.random.fold_in(own_key, 1), (twos,), 0, 1 << 20) % (room + 1)
    sizes = sizes.at[1:1 + 2 * twos:2].set(giver - shifted).at[2:2 + 2 * twos:2].set(receiver + shifted)
    return sizes[jax.random.permutation(jax.random.fold_in(own_key, 2), count)]


def noise(rng, extent, width, bound, split=(), held_as=jnp.bfloat16):
    values = jax.random.normal(rng, extent, jnp.float32) * width
    if len(split) > 0:
        values = block_levels(rng, extent, split, -0.22, 0.18) * values
    return jnp.clip(values, min=-bound, max=bound).astype(held_as)


def setup_inputs(seed: int = 0) -> dict:
    keys = jax.random.split(jax.random.key(seed), 15)
    tokens = noise(keys[0], (MICRO, TOKENS, D), 1.0, 6.0, ((1, 32),))
    cotangent = noise(keys[1], (MICRO, TOKENS, D), 1.0, 6.0, ((1, 32),))
    lengths = jax.vmap(lambda own: ragged(own, SEQ_GRP, GROUP, MAXLEN, 2))(jax.random.split(keys[2], MICRO * N_FSDP)).reshape((MICRO, N_FSDP, SEQ_GRP)).astype(jnp.int32)
    dealing = jax.vmap(lambda own: jax.random.permutation(own, GROUP))(jax.random.split(keys[3], MICRO * N_FSDP)).reshape((MICRO, N_FSDP, GROUP)).astype(jnp.int32)
    gain_attn = jnp.clip(1.0 + 0.18 * jax.random.normal(keys[4], (D,), jnp.float32), 0.099609375, 1.8984375).astype(jnp.bfloat16)
    w_query = noise(keys[5], (D, D), (16 * D) ** -0.5, 0.0546875, ((0, 8),))
    w_key = noise(keys[6], (D, D), D ** -0.5, 0.21875, ((0, 8),))
    w_value = noise(keys[7], (D, D), D ** -0.5, 0.21875, ((0, 8),))
    w_out = noise(keys[8], (D, D), (D // 16) ** -0.5, 0.875, ((0, 8),))
    bias_table = noise(keys[9], (BUCKETS, HEADS), 1.0, 4.0, ((1, 4),))
    gain_ff = jnp.clip(1.0 + 0.18 * jax.random.normal(keys[10], (D,), jnp.float32), 0.099609375, 1.8984375).astype(jnp.bfloat16)
    w_gate = noise(keys[11], (D, FF), D ** -0.5, 0.21875, ((0, 8),))
    w_up = noise(keys[12], (D, FF), D ** -0.5, 0.21875, ((0, 8),))
    w_down = noise(keys[13], (FF, D), (FF // 4) ** -0.5, 0.25, ((0, 8),))
    return {"tokens": tokens, "cotangent": cotangent, "lengths": lengths, "dealing": dealing, "gain_attn": gain_attn, "w_query": w_query, "w_key": w_key, "w_value": w_value, "w_out": w_out, "bias_table": bias_table, "gain_ff": gain_ff, "w_gate": w_gate, "w_up": w_up, "w_down": w_down}


@jax.custom_vjp
def low(v):
    return lax.optimization_barrier(v.astype(jnp.bfloat16)).astype(jnp.float32)

@jax.custom_vjp
def low_back(v):
    return v

def low_keep(v):
    return (low(v), None)

def low_pass(kept, grad):
    return (grad,)

def back_keep(v):
    return (v, None)

def back_low(kept, grad):
    return (low(grad),)
low.defvjp(low_keep, low_pass)
low_back.defvjp(back_keep, back_low)
bucket_edges = (1, 2, 3, 4, 5, 6, 7, 8, 12, 16, 23, 32, 46, 64, 91)
epsilon = 1e-06
precise = lax.Precision.HIGHEST

def bucket_index(offset):
    distance = jnp.abs(offset)
    bucket_sum = jnp.where(offset > 0, BUCKETS // 2, 0).astype(jnp.int32)
    for border in bucket_edges:
        bucket_sum = bucket_sum + (distance >= border).astype(jnp.int32)
    return bucket_sum

def rms_norm(values, gain):
    return values * lax.rsqrt(lax.optimization_barrier(jnp.mean(values * values, axis=-1, keepdims=True)) + epsilon) * gain

def project(values, weight):
    return jnp.einsum('mtd,de->mte', values, weight, precision=precise, preferred_element_type=jnp.float32)

def to_groups(values):
    shaped = values.reshape(MICRO, N_FSDP, N_SP, N_FSDP, PIECE, values.shape[-1])
    return jnp.transpose(shaped, (0, 3, 2, 1, 4, 5)).reshape(MICRO, N_FSDP, GROUP, values.shape[-1])

def from_groups(values):
    shaped = values.reshape(MICRO, N_FSDP, N_SP, N_FSDP, PIECE, values.shape[-1])
    return jnp.transpose(shaped, (0, 3, 2, 1, 4, 5)).reshape(MICRO, TOKENS, values.shape[-1])

def group_attention(query_rows, key_rows, value_rows, seq_lengths, bias_rows):
    position = jnp.arange(GROUP, dtype=jnp.int32)
    bounds = jnp.cumsum(seq_lengths).astype(jnp.int32)
    segment = lax.optimization_barrier(jnp.sum((position[:, None] >= bounds[None, :]).astype(jnp.int32), axis=1))
    inside = segment[:, None] == segment[None, :]
    rel_bias = jnp.transpose(bias_rows[bucket_index(position[None, :] - position[:, None])], (2, 0, 1))
    scores = jnp.einsum('qhd,khd->hqk', query_rows, key_rows, precision=precise, preferred_element_type=jnp.float32)
    logits = jnp.where(inside[None], low_back(scores) + rel_bias, -1e+30)
    weights = low(jax.nn.softmax(logits, axis=-1))
    context = jnp.einsum('hqk,khd->qhd', weights, value_rows, precision=precise, preferred_element_type=jnp.float32)
    return low(low_back(context))

def forward(tokens, gain_attn, w_query, w_key, w_value, w_out, bias_table, gain_ff, w_gate, w_up, w_down, lengths, dealing):
    normed = low(rms_norm(tokens, gain_attn))
    queries = low(low_back(project(normed, w_query)))
    keys_all = low(low_back(project(normed, w_key)))
    values_all = low(low_back(project(normed, w_value)))
    slot_order = dealing[..., None]

    def slotted(arrays):
        return jnp.take_along_axis(to_groups(arrays), slot_order, axis=2).reshape(MICRO * N_FSDP, GROUP, HEADS, DH)
    single = jax.checkpoint(lambda members: group_attention(members[0], members[1], members[2], members[3], bias_table))
    context = lax.map(single, (slotted(queries), slotted(keys_all), slotted(values_all), lengths.reshape(MICRO * N_FSDP, SEQ_GRP)))
    inverse = jnp.argsort(dealing, axis=-1).astype(jnp.int32)
    context = jnp.take_along_axis(context.reshape(MICRO, N_FSDP, GROUP, D), inverse[..., None], axis=2)
    attended = low_back(project(from_groups(context), w_out))
    middle = tokens + attended
    normed_ff = low(rms_norm(middle, gain_ff))
    gate_proj = low_back(project(normed_ff, w_gate))
    up_proj = low_back(project(normed_ff, w_up))
    hidden = low(jax.nn.gelu(gate_proj, approximate=True) * up_proj)
    return middle + project(hidden, w_down)

def reference(tokens, cotangent, lengths, dealing, gain_attn, w_query, w_key, w_value, w_out, bias_table, gain_ff, w_gate, w_up, w_down):
    floats = tuple((member.astype(jnp.float32) for member in (tokens, gain_attn, w_query, w_key, w_value, w_out, bias_table, gain_ff, w_gate, w_up, w_down)))

    def layer_fn(*members):
        return forward(*members, lengths, dealing)
    result, pullback = jax.vjp(layer_fn, *floats)
    gradients = pullback(cotangent.astype(jnp.float32))
    return (result.astype(jnp.bfloat16), gradients[0].astype(jnp.bfloat16), gradients[1], gradients[2], gradients[3], gradients[4], gradients[5], gradients[6], gradients[7], gradients[8], gradients[9], gradients[10])
```

```python
import functools
import math

import jax
import jax.numpy as jnp
from jax import lax
from jax.experimental import pallas as pl
from jax.experimental.pallas import tpu as pltpu
from jax.sharding import PartitionSpec as P

bucket_edges = (1, 2, 3, 4, 5, 6, 7, 8, 12, 16, 23, 32, 46, 64, 91)
epsilon = 1e-06
longest = 1024
lanes = 128
block = 256
far = 768
reach = 1792
MESH = pl.DeviceIdType.MESH
f32 = jnp.float32
bf16 = jnp.bfloat16
vmem_limit = 60 * 2**20


def nn(left, right):
    return jnp.dot(left, right, preferred_element_type=f32)


def nt(left, right):
    return lax.dot_general(left, right, (((1,), (1,)), ((), ())), preferred_element_type=f32)


def tn(left, right):
    return lax.dot_general(left, right, (((0,), (0,)), ((), ())), preferred_element_type=f32)


def iota(shape, dim):
    return lax.broadcasted_iota(jnp.int32, shape, dim)


def one_hot(column, row):
    return jnp.where(column == row, 1.0, 0.0).astype(bf16)


def inverse_rms(values):
    return lax.rsqrt(jnp.mean(values * values, axis=-1, keepdims=True) + epsilon)


def bucket_index(offset):
    distance = jnp.abs(offset)
    bucket_sum = jnp.where(offset > 0, 16, 0).astype(jnp.int32)
    for border in bucket_edges:
        bucket_sum = bucket_sum + (distance >= border).astype(jnp.int32)
    return bucket_sum


def band_buckets():
    shape = (3 * lanes, lanes)
    return bucket_index(iota(shape, 0) - lanes - iota(shape, 1))


def whole_spec(shape, space=pltpu.VMEM):
    return pl.BlockSpec(shape, lambda *_: (0,) * len(shape), memory_space=space,
                        pipeline_mode=pl.Buffered(1))


def deal_kernel(fsdp_count, tok_ref, cot_ref, xa_ref, ca_ref, send, recv, pass_send, pass_recv, own):
    f = lax.axis_index("fsdp")
    s = lax.axis_index("sp")
    p, c = s // 2, s % 2
    mine = p * fsdp_count + f
    peers = 2 * fsdp_count
    barrier = pltpu.get_barrier_semaphore()

    def where(k):
        return {"fsdp": k % fsdp_count, "sp": (k // fsdp_count) * 2 + c}

    def greet(i, carry):
        k = lax.rem(mine + i, peers)
        pl.semaphore_signal(barrier, inc=1, device_id=where(k), device_id_type=MESH)
        return carry

    lax.fori_loop(1, peers, greet, 0)
    sibling = {"fsdp": f, "sp": 2 * p + 1 - c}
    pl.semaphore_signal(barrier, inc=1, device_id=sibling, device_id_type=MESH)
    pl.semaphore_wait(barrier, peers)

    def piece(which, src, dst, k):
        return pltpu.make_async_remote_copy(
            src_ref=src.at[k // fsdp_count, k % fsdp_count],
            dst_ref=dst.at[c, p, f],
            send_sem=send.at[which, k],
            recv_sem=recv.at[which, mine],
            device_id=where(k),
            device_id_type=MESH,
        )

    def arrived(which, src, dst, k):
        return pltpu.make_async_remote_copy(
            src_ref=src.at[k // fsdp_count, k % fsdp_count],
            dst_ref=dst.at[c, k // fsdp_count, k % fsdp_count],
            send_sem=send.at[which, k],
            recv_sem=recv.at[which, k],
            device_id=where(k),
            device_id_type=MESH,
        )

    def onward(which, dst, k, side):
        return pltpu.make_async_remote_copy(
            src_ref=dst.at[side, k // fsdp_count, k % fsdp_count],
            dst_ref=dst.at[side, k // fsdp_count, k % fsdp_count],
            send_sem=pass_send.at[which, k],
            recv_sem=pass_recv.at[which, k],
            device_id=sibling,
            device_id_type=MESH,
        )

    pairs = ((0, tok_ref, xa_ref), (1, cot_ref, ca_ref))
    for which, src, dst in pairs:

        def start(i, carry):
            piece(which, src, dst, lax.rem(mine + i, peers)).start()
            return carry

        lax.fori_loop(1, peers, start, 0)
    for which, src, dst in pairs:
        local = pltpu.make_async_copy(src.at[p, f], dst.at[c, p, f], own.at[which])
        local.start()
        local.wait()
        onward(which, dst, mine, c).start()

        def forward(i, carry):
            k = lax.rem(mine + peers - i, peers)
            arrived(which, src, dst, k).wait_recv()
            onward(which, dst, k, c).start()
            return carry

        lax.fori_loop(1, peers, forward, 0)
    for which, src, dst in pairs:

        def finish(k, carry):
            onward(which, dst, k, c).wait_send()
            onward(which, dst, k, 1 - c).wait_recv()
            return carry

        lax.fori_loop(0, peers, finish, 0)

        def sent(i, carry):
            piece(which, src, dst, lax.rem(mine + i, peers)).wait_send()
            return carry

        lax.fori_loop(1, peers, sent, 0)


def deal(tokens, cotangent, fsdp_count):
    micro, fsdp_count, piece, width = tokens.shape
    out = jax.ShapeDtypeStruct((2, 2, fsdp_count, piece, width), bf16)
    hbm = pl.BlockSpec(memory_space=pl.ANY)
    sem = pltpu.SemaphoreType.DMA((2, 2 * fsdp_count))
    return pl.pallas_call(
        functools.partial(deal_kernel, fsdp_count),
        out_shape=(out, out),
        in_specs=[hbm, hbm],
        out_specs=(hbm, hbm),
        scratch_shapes=[sem, sem, sem, sem, pltpu.SemaphoreType.DMA((2,))],
        compiler_params=pltpu.CompilerParams(collective_id=0, has_side_effects=True),
        name="deal",
    )(tokens, cotangent)


def home_kernel(fsdp_count, a_ref, b_ref, ra_ref, rb_ref, send, recv, own):
    f = lax.axis_index("fsdp")
    s = lax.axis_index("sp")
    p, c = s // 2, s % 2
    mine = p * fsdp_count + f
    peers = 2 * fsdp_count
    barrier = pltpu.get_barrier_semaphore()

    def where(k):
        return {"fsdp": k % fsdp_count, "sp": (k // fsdp_count) * 2 + c}

    def greet(i, carry):
        k = lax.rem(mine + i, peers)
        pl.semaphore_signal(barrier, inc=1, device_id=where(k), device_id_type=MESH)
        return carry

    lax.fori_loop(1, peers, greet, 0)
    pl.semaphore_wait(barrier, peers - 1)

    def piece(which, src, dst, k):
        return pltpu.make_async_remote_copy(
            src_ref=src.at[k // fsdp_count, k % fsdp_count],
            dst_ref=dst.at[p, f],
            send_sem=send.at[which, k],
            recv_sem=recv.at[which, mine],
            device_id=where(k),
            device_id_type=MESH,
        )

    def arrived(which, src, dst, k):
        return pltpu.make_async_remote_copy(
            src_ref=src.at[k // fsdp_count, k % fsdp_count],
            dst_ref=dst.at[k // fsdp_count, k % fsdp_count],
            send_sem=send.at[which, k],
            recv_sem=recv.at[which, k],
            device_id=where(k),
            device_id_type=MESH,
        )

    pairs = ((0, a_ref, ra_ref), (1, b_ref, rb_ref))
    for which, src, dst in pairs:

        def start(i, carry):
            piece(which, src, dst, lax.rem(mine + i, peers)).start()
            return carry

        lax.fori_loop(1, peers, start, 0)
        local = pltpu.make_async_copy(src.at[p, f], dst.at[p, f], own.at[which])
        local.start()
        local.wait()
    for which, src, dst in pairs:

        def finish(i, carry):
            k = lax.rem(mine + i, peers)
            arrived(which, src, dst, k).wait_recv()
            piece(which, src, dst, k).wait_send()
            return carry

        lax.fori_loop(1, peers, finish, 0)


def home(first, second):
    fsdp_count, piece, width = first.shape[1:]
    out = jax.ShapeDtypeStruct((2, fsdp_count, piece, width), bf16)
    hbm = pl.BlockSpec(memory_space=pl.ANY)
    sem = pltpu.SemaphoreType.DMA((2, 2 * fsdp_count))
    return pl.pallas_call(
        functools.partial(home_kernel, fsdp_count),
        out_shape=(out, out),
        in_specs=[hbm, hbm],
        out_specs=(hbm, hbm),
        scratch_shapes=[sem, sem, pltpu.SemaphoreType.DMA((2,))],
        compiler_params=pltpu.CompilerParams(collective_id=1, has_side_effects=True),
        name="home",
    )(first, second)


def build_diagonals(table_ref, band):
    left = jnp.broadcast_to(band[0:1, :], (lanes, lanes))
    right = jnp.broadcast_to(band[3 * lanes - 1 : 3 * lanes, :], (lanes, lanes))
    for half in range(2):
        cols = slice(half * lanes, (half + 1) * lanes)
        first = far - lanes + half * lanes
        for row in range(0, first, lanes):
            table_ref[row : row + lanes, cols] = left
        table_ref[first : first + 3 * lanes, cols] = band
        for row in range(first + 3 * lanes, reach, lanes):
            table_ref[row : row + lanes, cols] = right


def attend_kernel(
    bound_ref, idx_ref, x_ref, ct_ref, gain_ref, w_ref, band_ref,
    xs_ref, cs_ref, qkv_ref, pl_ref, ps_ref, ctx_ref, ctx32_ref, linv_ref,
    table, mask, km, vt, ctx_t, linv_t,
):
    rows_all, width = x_ref.shape
    pairs = pl.num_programs(0)
    part = pairs * lanes
    step = pl.program_id(0)
    short = rows_all - longest

    @pl.when(step == 0)
    def _():
        def tile(i, carry):
            rows = pl.ds(pl.multiple_of(i * block, block), block)
            chosen = one_hot(idx_ref[rows, :], iota((block, rows_all), 1))
            x = nn(chosen, x_ref[...])
            xs_ref[rows, :] = x.astype(bf16)
            normed = (x * inverse_rms(x) * gain_ref[...]).astype(bf16)
            for k in range(3):
                cols = slice(k * part, (k + 1) * part)
                qkv_ref[rows, cols] = nn(normed, w_ref[:, cols]).astype(bf16)
            cs_ref[rows, :] = nn(chosen, ct_ref[...]).astype(bf16)
            return carry

        lax.fori_loop(0, rows_all // block, tile, 0)
        bound = bound_ref[0]
        inside = (iota((short, short), 0) < bound) == (iota((short, short), 1) < bound)
        mask[...] = jnp.where(inside, 0.0, -1e30)

    def columns(kind):
        return pl.ds(pl.multiple_of(kind * part + step * lanes, lanes), lanes)

    keys = qkv_ref[:, columns(1)]
    vt[...] = jnp.transpose(qkv_ref[:, columns(2)].astype(f32)).astype(bf16)
    own = iota((rows_all, lanes), 1) < lanes // 2
    half = lanes // 2
    for h in range(2):
        build_diagonals(table, band_ref[h])
        km[...] = jnp.where(own == (h == 0), keys, jnp.zeros_like(keys))

        def strip(base, count, out_ref, masked, b, carry):
            here = pl.ds(pl.multiple_of(base + b * block, block), block)
            queries = qkv_ref[here, columns(0)]
            logits = nt(km[base : base + count, :], queries)
            first = pl.multiple_of(far - b * block, block)
            logits = logits + table[pl.ds(first, count), :]
            cols = pl.ds(pl.multiple_of(b * block, block), block)
            if masked:
                logits = logits + mask[:, cols]
            top = jnp.max(logits, axis=0, keepdims=True)
            weights = jnp.exp(logits - top)
            inv = 1.0 / jnp.sum(weights, axis=0, keepdims=True)
            low = weights.astype(bf16)
            spot = pl.ds(pl.multiple_of(h * count + b * block, block), block)
            out_ref[0, :, spot] = low
            part_rows = slice(h * half, (h + 1) * half)
            ctx_t[part_rows, here] = nn(vt[part_rows, base : base + count], low) * inv
            linv_t[part_rows, here] = jnp.broadcast_to(inv, (half, block))
            return carry

        lax.fori_loop(
            0, longest // block, functools.partial(strip, 0, longest, pl_ref, False), 0)
        lax.fori_loop(
            0, short // block, functools.partial(strip, longest, short, ps_ref, True), 0)
    context = jnp.transpose(ctx_t[...])
    ctx32_ref[...] = context
    ctx_ref[...] = context.astype(bf16)
    linv_ref[...] = jnp.transpose(linv_t[...])


def attend(bound, idx_col, arrived, cot_arrived, gain, w_qkv, band):
    rows, width = arrived.shape
    part = w_qkv.shape[1] // 3
    pairs = part // lanes
    short = rows - longest
    lane_block = pl.BlockSpec((rows, lanes), lambda i: (0, i))
    return pl.pallas_call(
        attend_kernel,
        grid=(pairs,),
        in_specs=[
            pl.BlockSpec(memory_space=pltpu.SMEM),
            whole_spec((rows, 1)),
            whole_spec((rows, width)),
            whole_spec((rows, width)),
            whole_spec((1, width)),
            whole_spec(w_qkv.shape),
            pl.BlockSpec((2, 3 * lanes, lanes), lambda i: (i, 0, 0)),
        ],
        out_specs=(
            whole_spec((rows, width)),
            whole_spec((rows, width)),
            whole_spec((rows, 3 * part)),
            pl.BlockSpec((1, longest, 2 * longest), lambda i: (i, 0, 0)),
            pl.BlockSpec((1, short, 2 * short), lambda i: (i, 0, 0)),
            lane_block, lane_block, lane_block,
        ),
        out_shape=(
            jax.ShapeDtypeStruct((rows, width), bf16),
            jax.ShapeDtypeStruct((rows, width), bf16),
            jax.ShapeDtypeStruct((rows, 3 * part), bf16),
            jax.ShapeDtypeStruct((pairs, longest, 2 * longest), bf16),
            jax.ShapeDtypeStruct((pairs, short, 2 * short), bf16),
            jax.ShapeDtypeStruct((rows, part), bf16),
            jax.ShapeDtypeStruct((rows, part), f32),
            jax.ShapeDtypeStruct((rows, part), f32),
        ),
        scratch_shapes=[
            pltpu.VMEM((reach, block), f32),
            pltpu.VMEM((short, short), f32),
            pltpu.VMEM((rows, lanes), bf16),
            pltpu.VMEM((lanes, rows), bf16),
            pltpu.VMEM((lanes, rows), f32),
            pltpu.VMEM((lanes, rows), f32),
        ],
        compiler_params=pltpu.CompilerParams(
            dimension_semantics=("arbitrary",), vmem_limit_bytes=vmem_limit),
        name="attend",
    )(bound, idx_col, arrived, cot_arrived, gain, w_qkv, band)


def feed_kernel(
    own_ref, sib_ref, xs_ref, cs_ref, wo_ref, gains_ref, wgu_ref, wd_ref,
    out_ref, ggu_ref, gd_ref, datt_ref, dctx_ref, go_own_ref, go_sib_ref, ggain_ref,
    mid, nff, hid, dgu, dn, dn_sib, send, recv,
):
    rows_all, width = xs_ref.shape
    ff = wd_ref.shape[0]
    part = width // 2
    lift = math.sqrt(2 / math.pi)
    tiles = rows_all // block
    s = lax.axis_index("sp")
    sibling = {"fsdp": lax.axis_index("fsdp"), "sp": (s // 2) * 2 + 1 - s % 2}
    gain = gains_ref[1:2, :]
    barrier = pltpu.get_barrier_semaphore()
    pl.semaphore_signal(barrier, inc=1, device_id=sibling, device_id_type=MESH)
    pl.semaphore_wait(barrier, 1)

    def exchange(i):
        rows = pl.ds(pl.multiple_of(i * block, block), block)
        return pltpu.make_async_remote_copy(
            src_ref=dn.at[rows, :], dst_ref=dn_sib.at[rows, :], send_sem=send.at[i],
            recv_sem=recv.at[i], device_id=sibling, device_id_type=MESH)

    def tile(i, carry):
        rows = pl.ds(pl.multiple_of(i * block, block), block)
        mixed = jnp.concatenate((own_ref[rows, :], sib_ref[rows, :]), axis=1)
        middle = xs_ref[rows, :].astype(f32) + nn(mixed, wo_ref[...])
        mid[rows, :] = middle
        normed = (middle * inverse_rms(middle) * gain).astype(bf16)
        nff[rows, :] = normed
        upstream = cs_ref[rows, :]
        gate = nn(normed, wgu_ref[:, :ff])
        up = nn(normed, wgu_ref[:, ff:])
        d_hidden = nt(upstream, wd_ref[...])
        square = gate * gate
        bent = jnp.tanh(lift * gate * (1.0 + 0.044715 * square))
        halved = 0.5 * (1.0 + bent)
        gelu = gate * halved
        slope = halved + 0.5 * gate * (1.0 - bent * bent) * (
            lift * (1.0 + 3 * 0.044715 * square))
        hidden = (gelu * up).astype(bf16)
        hid[rows, :] = hidden
        d_gate = (d_hidden * up * slope).astype(bf16)
        d_up = (d_hidden * gelu).astype(bf16)
        dgu[rows, :ff] = d_gate
        dgu[rows, ff:] = d_up
        dn[rows, :] = (nt(d_gate, wgu_ref[:, :ff]) + nt(d_up, wgu_ref[:, ff:])).astype(bf16)
        exchange(i).start()
        out_ref[rows, :] = (0.5 * middle + nn(hidden, wd_ref[...])).astype(bf16)
        return carry

    lax.fori_loop(0, tiles, tile, 0)

    def down(i, carry):
        cols = pl.ds(pl.multiple_of(i * block, block), block)
        gd_ref[cols, :] = tn(hid[:, cols], cs_ref[...]).astype(bf16)
        return carry

    lax.fori_loop(0, ff // block, down, 0)

    def settle(i, total):
        rows = pl.ds(pl.multiple_of(i * block, block), block)
        exchange(i).wait()
        mine = dn[rows, :].astype(f32)
        grad = mine + dn_sib[rows, :].astype(f32)
        middle = mid[rows, :]
        s = inverse_rms(middle)
        unit = middle * s
        scaled = gain * grad
        d_middle = cs_ref[rows, :].astype(f32) + s * (
            scaled - unit * jnp.mean(scaled * unit, axis=-1, keepdims=True))
        low = d_middle.astype(bf16)
        datt_ref[rows, :] = low
        dctx_ref[rows, :] = nt(low, wo_ref[0:part, :]).astype(bf16)
        return total + jnp.sum(mine * unit, axis=0, keepdims=True)

    ggain_ref[...] = lax.fori_loop(0, tiles, settle, jnp.zeros((1, width), f32))
    c = lax.axis_index("sp") % 2
    cols = pl.ds(pl.multiple_of(c * part, lanes), part)
    go_own_ref[...] = tn(own_ref[...], datt_ref[:, cols]).astype(bf16)
    go_sib_ref[...] = tn(sib_ref[...], datt_ref[:, cols]).astype(bf16)

    def gate_up(i, carry):
        cols = pl.ds(pl.multiple_of(i * block, block), block)
        ggu_ref[cols, :] = tn(nff[:, cols], dgu[...]).astype(bf16)
        return carry

    lax.fori_loop(0, width // block, gate_up, 0)


def feed(own, sib, xs, cs, w_out, gains, w_gu, w_down):
    rows, width = xs.shape
    ff = w_down.shape[0]
    part = width // 2
    vm = pl.BlockSpec(memory_space=pltpu.VMEM)
    return pl.pallas_call(
        feed_kernel,
        in_specs=[vm] * 8,
        out_specs=(vm,) * 8,
        out_shape=(
            jax.ShapeDtypeStruct((rows, width), bf16),
            jax.ShapeDtypeStruct((width, 2 * ff), bf16),
            jax.ShapeDtypeStruct((ff, width), bf16),
            jax.ShapeDtypeStruct((rows, width), bf16),
            jax.ShapeDtypeStruct((rows, part), bf16),
            jax.ShapeDtypeStruct((part, part), bf16),
            jax.ShapeDtypeStruct((part, part), bf16),
            jax.ShapeDtypeStruct((1, width), f32),
        ),
        scratch_shapes=[
            pltpu.VMEM((rows, width), f32),
            pltpu.VMEM((rows, width), bf16),
            pltpu.VMEM((rows, ff), bf16),
            pltpu.VMEM((rows, 2 * ff), bf16),
            pltpu.VMEM((rows, width), bf16),
            pltpu.VMEM((rows, width), bf16),
            pltpu.SemaphoreType.DMA((rows // block,)),
            pltpu.SemaphoreType.DMA((rows // block,)),
        ],
        compiler_params=pltpu.CompilerParams(
            vmem_limit_bytes=vmem_limit, collective_id=2, has_side_effects=True),
        name="feed",
    )(own, sib, xs, cs, w_out, gains, w_gu, w_down)


def back_kernel(
    xs_ref, gain_ref, w_ref, datt_ref, dctx_ref, qkv_ref, pl_ref, ps_ref, ctx32_ref, linv_ref,
    y_ref, gqkv_ref, ggain_ref, band_ref,
    normed, dqkv, table, dos, qs, ds_l, ds_s, va, kt, dq_t,
):
    rows_all, width = xs_ref.shape
    pairs = pl.num_programs(0)
    part = pairs * lanes
    step = pl.program_id(0)
    short = rows_all - longest
    half = lanes // 2
    gain_attn = gain_ref[0:1, :]

    def columns(kind):
        return pl.ds(pl.multiple_of(kind * part + step * lanes, lanes), lanes)

    lane = iota((rows_all, lanes), 1)
    queries = qkv_ref[:, columns(0)]
    keys = qkv_ref[:, columns(1)]
    values = qkv_ref[:, columns(2)]
    none = jnp.zeros_like(keys)
    kt[...] = jnp.transpose(keys.astype(f32)).astype(bf16)
    scaled = (dctx_ref[:, columns(0)].astype(f32) * linv_ref[...]).astype(bf16)
    against = scaled.astype(f32) * ctx32_ref[...]
    for h in range(2):
        mine = (lane < half) if h == 0 else (lane >= half)
        spare = half if h == 0 else 0
        delta = jnp.sum(jnp.where(mine, against, 0.0), axis=1, keepdims=True)
        high = delta.astype(bf16).astype(f32)
        rest = delta - high
        extra = jnp.where(lane == spare, -high, jnp.where(lane == spare + 1, -rest, 0.0))
        dos[h] = jnp.where(mine, scaled.astype(f32), extra).astype(bf16)
        qs[h] = jnp.where(mine, queries, none)
        ones = jnp.where((lane == spare) | (lane == spare + 1), 1.0, 0.0)
        va[...] = jnp.where(mine, values.astype(f32), ones).astype(bf16)
        table[...] = jnp.zeros_like(table)

        def strip(base, count, p_ref, ds_ref, b, carry):
            here = pl.ds(pl.multiple_of(base + b * block, block), block)
            spot = pl.ds(pl.multiple_of(h * count + b * block, block), block)
            d_weights = nt(va[base : base + count, :], dos[h, here, :])
            d_logits = p_ref[0, :, spot].astype(f32) * d_weights
            window = pl.ds(pl.multiple_of(far - b * block, block), count)
            table[window, :] = table[window, :] + d_logits
            low = d_logits.astype(bf16)
            ds_ref[:, spot] = low
            part_rows = slice(h * half, (h + 1) * half)
            dq_t[part_rows, here] = nn(kt[part_rows, base : base + count], low)
            return carry

        lax.fori_loop(
            0, longest // block, functools.partial(strip, 0, longest, pl_ref, ds_l), 0)
        lax.fori_loop(
            0, short // block, functools.partial(strip, longest, short, ps_ref, ds_s), 0)
        before = far - lanes
        after = far + 3 * lanes
        band = table[before : before + 3 * lanes, :lanes] + table[far : far + 3 * lanes, lanes:]
        left = jnp.sum(table[:before, :lanes] + table[:before, lanes:], axis=0, keepdims=True)
        left = left + jnp.sum(table[before:far, lanes:], axis=0, keepdims=True)
        right = jnp.sum(table[after:, :lanes] + table[after:, lanes:], axis=0, keepdims=True)
        right = right + jnp.sum(table[after - lanes : after, :lanes], axis=0, keepdims=True)
        row = iota((3 * lanes, lanes), 0)
        band = band + jnp.where(row == 0, left, 0.0) + jnp.where(row == 3 * lanes - 1, right, 0.0)
        band_ref[h] = band

    dqkv[:, columns(0)] = jnp.transpose(dq_t[...]).astype(bf16)
    own = iota((rows_all, lanes), 1) < half
    for base, count, p_ref, ds_ref in ((0, longest, pl_ref, ds_l), (longest, short, ps_ref, ds_s)):
        rows = slice(base, base + count)
        clean = [
            jnp.where(own[rows] == (h == 0), dos[h, rows, :].astype(f32), 0.0).astype(bf16)
            for h in range(2)
        ]
        dqkv[rows, columns(2)] = nn(p_ref[0], jnp.concatenate(clean, axis=0)).astype(bf16)
        both = jnp.concatenate((qs[0, rows, :], qs[1, rows, :]), axis=0)
        dqkv[rows, columns(1)] = nn(ds_ref[...], both).astype(bf16)

    @pl.when(step == pairs - 1)
    def _():
        def tile(i, total):
            rows = pl.ds(pl.multiple_of(i * block, block), block)
            x = xs_ref[rows, :].astype(f32)
            s = inverse_rms(x)
            unit = x * s
            grad = nt(dqkv[rows, :], w_ref[...])
            scaled = gain_attn * grad
            y = 0.5 * datt_ref[rows, :].astype(f32) + s * (
                scaled - unit * jnp.mean(scaled * unit, axis=-1, keepdims=True))
            y_ref[rows, :] = y.astype(bf16)
            normed[rows, :] = (unit * gain_attn).astype(bf16)
            return total + jnp.sum(grad * unit, axis=0, keepdims=True)

        zero = jnp.zeros((1, width), f32)
        ggain_ref[...] = lax.fori_loop(0, rows_all // block, tile, zero)

        def weight(i, carry):
            cols = pl.ds(pl.multiple_of(i * block, block), block)
            gqkv_ref[cols, :] = tn(normed[:, cols], dqkv[...]).astype(bf16)
            return carry

        lax.fori_loop(0, width // block, weight, 0)


def back(xs, gain, w_qkv, datt, dctx, qkv, p_long, p_short, ctx32, linv):
    rows, width = xs.shape
    part = w_qkv.shape[1] // 3
    pairs = part // lanes
    short = rows - longest
    lane_block = pl.BlockSpec((rows, lanes), lambda i: (0, i))
    return pl.pallas_call(
        back_kernel,
        grid=(pairs,),
        in_specs=[
            *(whole_spec(a.shape) for a in (xs, gain, w_qkv, datt, dctx, qkv)),
            pl.BlockSpec((1, longest, 2 * longest), lambda i: (i, 0, 0)),
            pl.BlockSpec((1, short, 2 * short), lambda i: (i, 0, 0)),
            lane_block, lane_block,
        ],
        out_specs=(
            whole_spec((rows, width)),
            whole_spec((width, 3 * part)),
            whole_spec((1, width)),
            pl.BlockSpec((2, 3 * lanes, lanes), lambda i: (i, 0, 0)),
        ),
        out_shape=(
            jax.ShapeDtypeStruct((rows, width), bf16),
            jax.ShapeDtypeStruct((width, 3 * part), bf16),
            jax.ShapeDtypeStruct((1, width), f32),
            jax.ShapeDtypeStruct((2 * pairs, 3 * lanes, lanes), f32),
        ),
        scratch_shapes=[
            pltpu.VMEM((rows, width), bf16),
            pltpu.VMEM((rows, 3 * part), bf16),
            pltpu.VMEM((reach, block), f32),
            pltpu.VMEM((2, rows, lanes), bf16),
            pltpu.VMEM((2, rows, lanes), bf16),
            pltpu.VMEM((longest, 2 * longest), bf16),
            pltpu.VMEM((short, 2 * short), bf16),
            pltpu.VMEM((rows, lanes), bf16),
            pltpu.VMEM((lanes, rows), bf16),
            pltpu.VMEM((lanes, rows), f32),
        ],
        compiler_params=pltpu.CompilerParams(
            dimension_semantics=("arbitrary",), vmem_limit_bytes=vmem_limit),
        name="back",
    )(xs, gain, w_qkv, datt, dctx, qkv, p_long, p_short, ctx32, linv)


def unslot_kernel(idx_ref, a_ref, b_ref, oa_ref, ob_ref):
    rows_all = a_ref.shape[0]

    def tile(i, carry):
        rows = pl.ds(pl.multiple_of(i * block, block), block)
        chosen = one_hot(iota((block, rows_all), 0) + i * block, idx_ref[...])
        oa_ref[rows, :] = nn(chosen, a_ref[...]).astype(bf16)
        ob_ref[rows, :] = nn(chosen, b_ref[...]).astype(bf16)
        return carry

    lax.fori_loop(0, rows_all // block, tile, 0)


def unslot(idx_row, first, second):
    vm = pl.BlockSpec(memory_space=pltpu.VMEM)
    out = jax.ShapeDtypeStruct(first.shape, bf16)
    return pl.pallas_call(
        unslot_kernel,
        in_specs=[vm] * 3,
        out_specs=(vm, vm),
        out_shape=(out, out),
        compiler_params=pltpu.CompilerParams(vmem_limit_bytes=vmem_limit),
        name="unslot",
    )(idx_row, first, second)


def shards(
    tokens, cotangent, lengths, dealing, gain_attn, w_query, w_key, w_value, w_out, bias_table,
    gain_ff, w_gate, w_up, w_down,
):
    fsdp_count = lax.axis_size("fsdp")
    sp_count = lax.axis_size("sp")
    micro_count, token_rows, width = tokens.shape
    piece = token_rows // fsdp_count
    group_rows = token_rows * sp_count
    local_heads = bias_table.shape[1]
    heads = local_heads * sp_count
    part = width // 2
    s = lax.axis_index("sp")
    p, c = s // 2, s % 2
    sibling = [(0, 1), (1, 0), (2, 3), (3, 2)]
    across = [(0, 2), (2, 0), (1, 3), (3, 1)]

    def swap(value):
        return lax.ppermute(value, "sp", sibling)

    shape = (micro_count, fsdp_count, piece, width)
    xa, ca = deal(tokens.reshape(shape), cotangent.reshape(shape), fsdp_count)
    xa = xa.reshape(group_rows, width)
    ca = ca.reshape(group_rows, width)

    order = lax.dynamic_index_in_dim(dealing[:, 0], p, 0, keepdims=False)
    length = lax.dynamic_index_in_dim(lengths[:, 0], p, 0, keepdims=False)
    first_long = length[0] == longest
    start = jnp.where(first_long, 0, jnp.where(length[1] == longest, length[0],
                                               length[0] + length[1]))
    bound = jnp.where(first_long, length[1], length[0]).reshape(1)
    short = group_rows - longest
    head_part = lax.dynamic_slice_in_dim(order, start, longest, 0)
    tail = jnp.where(jnp.arange(short) < start, order[:short], order[longest:])
    order = jnp.concatenate((head_part, tail))
    source = order // token_rows
    idx = (source % 2) * (group_rows // 2) + (source // 2) * token_rows + order % token_rows

    def half_cols(weight):
        return lax.dynamic_slice_in_dim(weight, c * part, part, 1)

    def half_ff(weight):
        split = weight.reshape(weight.shape[0], fsdp_count, 2, -1)
        return lax.dynamic_index_in_dim(split, c, 2, keepdims=False).reshape(weight.shape[0], -1)

    def gather(value, axis=0):
        return lax.all_gather(value, "fsdp", axis=axis, tiled=True)

    gains = gather(jnp.stack((gain_attn, gain_ff)), 1).astype(f32)
    table = lax.all_gather(bias_table, "sp", axis=1, tiled=True).astype(f32)
    table = lax.dynamic_slice_in_dim(table, c * (heads // 2), heads // 2, 1)
    w_qkv = gather(jnp.concatenate([half_cols(w) for w in (w_query, w_key, w_value)], axis=1))
    down_rows = w_down.shape[0] // 2
    wd_half = lax.dynamic_slice_in_dim(w_down, c * down_rows, down_rows, 0)
    model_rows = w_out.shape[0]
    rest = gather(jnp.concatenate(
        [half_ff(w_gate), half_ff(w_up), w_out, wd_half.reshape(model_rows, -1)], axis=1))
    ff_wide = w_gate.shape[1] // 2
    w_gu = rest[:, : 2 * ff_wide]
    wo = rest[:, 2 * ff_wide : 2 * ff_wide + width]
    wo = jnp.where(c == 0, wo, jnp.concatenate((wo[part:], wo[:part])))
    wd = rest[:, 2 * ff_wide + width :].reshape(-1, width)

    buckets = band_buckets()
    band = jnp.zeros((heads // 2, *buckets.shape), f32)
    for label in range(table.shape[0]):
        band = band + jnp.where(buckets[None] == label, table[label][:, None, None], 0.0)

    xs, cs, qkv, p_long, p_short, ctx, ctx32, linv = attend(
        bound, idx.reshape(-1, 1), xa, ca, gains[0:1], w_qkv, band)
    ctx_sib = swap(ctx)
    out_part, grad_gu, grad_d, datt, dctx, go_own, go_sib, grad_gain_ff = feed(
        ctx, ctx_sib, xs, cs, wo, gains, w_gu, wd)
    grad_o = jnp.where(c == 0, jnp.concatenate((go_own, go_sib)),
                       jnp.concatenate((go_sib, go_own)))
    y, grad_qkv, grad_gain_attn, grad_band = back(
        xs, gains[0:1], w_qkv, datt, dctx, qkv, p_long, p_short, ctx32, linv)
    grad_gain = jnp.concatenate((grad_gain_attn, grad_gain_ff))
    back_rows = unslot(idx.reshape(1, -1), out_part, y)
    mine = group_rows // 2

    def join(value):
        kept = lax.dynamic_slice_in_dim(value, c * mine, mine, 0)
        given = lax.dynamic_slice_in_dim(value, (1 - c) * mine, mine, 0)
        return (kept.astype(f32) + swap(given).astype(f32)).astype(bf16).reshape(shape)

    output, grad_tokens = home(join(back_rows[0]), join(back_rows[1]))

    def packed(values, unit):
        cut = [v.reshape(fsdp_count, v.shape[0] // fsdp_count, -1, unit) for v in values]
        cut = [jnp.swapaxes(v, 1, 2).reshape(fsdp_count, -1, unit) for v in cut]
        return jnp.concatenate(cut, axis=1)

    def scatter(values, unit):
        whole = packed(values, unit)
        share = lax.psum_scatter(whole, "fsdp", scatter_dimension=0, tiled=True)[0]
        out, at = [], 0
        for v in values:
            rows, count = v.shape[0] // fsdp_count, v.shape[1] // unit
            one = share[at : at + rows * count].reshape(count, rows, unit)
            out.append(jnp.swapaxes(one, 0, 1).reshape(rows, -1))
            at += rows * count
        return out

    shares = scatter((grad_gu, grad_d), 256) + scatter((grad_qkv, grad_o), 384)
    flat = jnp.concatenate([v.reshape(-1) for v in shares])
    flat = (flat.astype(f32) + lax.ppermute(flat, "sp", across).astype(f32)).astype(bf16)
    flat_sib = swap(flat)
    low = jnp.where(c == 0, flat, flat_sib).astype(f32)
    high = jnp.where(c == 0, flat_sib, flat).astype(f32)
    pieces = []
    at = 0
    for v in shares:
        pieces.append([x[at : at + v.size].reshape(v.shape) for x in (low, high)])
        at += v.size
    gu, gd, gqkv, go = pieces
    ff = gu[0].shape[1] // 2

    def ff_cols(which):
        sides = [x[:, which * ff : (which + 1) * ff].reshape(x.shape[0], fsdp_count, 1, -1)
                 for x in gu]
        return jnp.concatenate(sides, axis=2).reshape(gu[0].shape[0], -1)

    def proj(which):
        return jnp.concatenate([x[:, which * part : (which + 1) * part] for x in gqkv], axis=1)

    sums = jnp.stack([
        jnp.sum(jnp.where(buckets[None] == label, grad_band, 0.0), axis=(1, 2))
        for label in range(table.shape[0])
    ])
    spread = jnp.zeros((table.shape[0], heads), f32)
    spread = lax.dynamic_update_slice(spread, sums, (0, c * (heads // 2)))
    small = lax.psum(jnp.concatenate((grad_gain.reshape(-1), spread.reshape(-1))), ("fsdp", "sp"))
    own_gain = width // fsdp_count
    f = lax.axis_index("fsdp")
    gains_grad = lax.dynamic_slice_in_dim(small[: 2 * width].reshape(2, width), f * own_gain,
                                          own_gain, 1)
    bias_grad = lax.dynamic_slice_in_dim(small[2 * width :].reshape(-1, heads), s * local_heads,
                                         local_heads, 1)
    return (
        output.reshape(tokens.shape), grad_tokens.reshape(tokens.shape), gains_grad[0],
        proj(0), proj(1), proj(2), jnp.concatenate(go, axis=1), bias_grad, gains_grad[1],
        ff_cols(0), ff_cols(1), jnp.concatenate(gd, axis=0),
    )


def solution(mesh):
    return jax.shard_map(
        shards,
        mesh=mesh,
        in_specs=(
            P(None, ("fsdp", "sp"), None), P(None, ("fsdp", "sp"), None),
            P(None, "fsdp", None), P(None, "fsdp", None),
            P("fsdp"), P("fsdp", None), P("fsdp", None), P("fsdp", None), P("fsdp", None),
            P(None, "sp"), P("fsdp"), P("fsdp", None), P("fsdp", None), P("fsdp", None),
        ),
        out_specs=(
            P(None, ("fsdp", "sp"), None), P(None, ("fsdp", "sp"), None),
            P("fsdp"), P("fsdp", None), P("fsdp", None), P("fsdp", None), P("fsdp", None),
            P(None, "sp"), P("fsdp"), P("fsdp", None), P("fsdp", None), P("fsdp", None),
        ),
        check_vma=False,
    )
```

```python
import functools
import math

import jax
import jax.numpy as jnp
from jax import lax
from jax.experimental import pallas as pl
from jax.experimental.pallas import tpu as pltpu
from jax.sharding import PartitionSpec as P

bucket_edges = (1, 2, 3, 4, 5, 6, 7, 8, 12, 16, 23, 32, 46, 64, 91)
epsilon = 1e-06
longest = 1024
lanes = 128
block = 256
far = 768
reach = 1792
MESH = pl.DeviceIdType.MESH
f32 = jnp.float32
bf16 = jnp.bfloat16
vmem_limit = 60 * 2**20


def nn(left, right):
    return jnp.dot(left, right, preferred_element_type=f32)


def nt(left, right):
    return lax.dot_general(left, right, (((1,), (1,)), ((), ())), preferred_element_type=f32)


def tn(left, right):
    return lax.dot_general(left, right, (((0,), (0,)), ((), ())), preferred_element_type=f32)


def iota(shape, dim):
    return lax.broadcasted_iota(jnp.int32, shape, dim)


def one_hot(column, row):
    return jnp.where(column == row, 1.0, 0.0).astype(bf16)


def inverse_rms(values):
    return lax.rsqrt(jnp.mean(values * values, axis=-1, keepdims=True) + epsilon)


def bucket_index(offset):
    distance = jnp.abs(offset)
    bucket_sum = jnp.where(offset > 0, 16, 0).astype(jnp.int32)
    for border in bucket_edges:
        bucket_sum = bucket_sum + (distance >= border).astype(jnp.int32)
    return bucket_sum


def band_buckets():
    shape = (3 * lanes, lanes)
    return bucket_index(iota(shape, 0) - lanes - iota(shape, 1))


def whole_spec(shape, space=pltpu.VMEM):
    return pl.BlockSpec(shape, lambda *_: (0,) * len(shape), memory_space=space,
                        pipeline_mode=pl.Buffered(1))


def place():
    f = lax.axis_index("fsdp")
    s = lax.axis_index("sp")
    return f, s // 2, s % 2


def device(f, p, c):
    return {"fsdp": f, "sp": 2 * p + c}


def signal(barrier, where):
    pl.semaphore_signal(barrier, inc=1, device_id=where, device_id_type=MESH)


def greet_all(fsdp_count):
    f, p, c = place()
    barrier = pltpu.get_barrier_semaphore()
    peers = 2 * fsdp_count
    mine = p * fsdp_count + f

    def greet(i, carry):
        k = lax.rem(mine + i, peers)
        signal(barrier, device(k % fsdp_count, k // fsdp_count, c))
        return carry

    lax.fori_loop(1, peers, greet, 0)
    signal(barrier, device(f, p, 1 - c))
    pl.semaphore_wait(barrier, peers)


def push(src, dst, send, recv, where):
    return pltpu.make_async_remote_copy(
        src_ref=src, dst_ref=dst, send_sem=send, recv_sem=recv, device_id=where,
        device_id_type=MESH)


def looped(first, last, body):
    def step(i, carry):
        body(i)
        return carry

    lax.fori_loop(first, last, step, 0)


class Dealing:
    def __init__(self, fsdp_count, src, dst, send, recv, pass_send, pass_recv, own):
        self.f, self.p, self.c = place()
        self.count = fsdp_count
        self.peers = 2 * fsdp_count
        self.mine = self.p * fsdp_count + self.f
        self.src, self.dst, self.send, self.recv = src, dst, send, recv
        self.pass_send, self.pass_recv, self.own = pass_send, pass_recv, own

    def source(self, k):
        return self.src.at[k // self.count, k % self.count] if len(self.src.shape) == 4 else self.src

    def out(self, k):
        where = device(k % self.count, k // self.count, self.c)
        return push(self.source(k), self.dst.at[self.c, self.p, self.f], self.send.at[k],
                    self.recv.at[self.mine], where)

    def come(self, k):
        where = device(k % self.count, k // self.count, self.c)
        return push(self.source(k), self.dst.at[self.c, k // self.count, k % self.count],
                    self.send.at[k], self.recv.at[k], where)

    def onward(self, k, side):
        here = self.dst.at[side, k // self.count, k % self.count]
        return push(here, here, self.pass_send.at[k], self.pass_recv.at[k],
                    device(self.f, self.p, 1 - self.c))

    def local(self):
        return pltpu.make_async_copy(
            self.source(self.mine), self.dst.at[self.c, self.p, self.f], self.own)

    def start(self):
        looped(1, self.peers, lambda i: self.out(lax.rem(self.mine + i, self.peers)).start())
        self.local().start()

    def forward(self):
        self.local().wait()
        self.onward(self.mine, self.c).start()

        def one(i):
            k = lax.rem(self.mine + self.peers - i, self.peers)
            self.come(k).wait_recv()
            self.onward(k, self.c).start()

        looped(1, self.peers, one)

    def sent(self):
        looped(1, self.peers, lambda i: self.out(lax.rem(self.mine + i, self.peers)).wait_send())

    def finish(self):
        looped(0, self.peers, lambda k: self.onward(k, 1 - self.c).wait_recv())

    def passed(self):
        looped(0, self.peers, lambda k: self.onward(k, self.c).wait_send())


class Gathering:
    def __init__(self, fsdp_count, srcs, dsts, sends, recvs, own):
        self.f, self.y, self.c = place()
        self.count = fsdp_count
        self.planes = fsdp_count // 2
        self.z, self.x = self.f // 2, self.f % 2
        self.srcs, self.dsts, self.sends, self.recvs, self.own = srcs, dsts, sends, recvs, own
        self.x_side = device(self.z * 2 + 1 - self.x, self.y, self.c)
        self.y_side = device(self.f, 1 - self.y, self.c)

    def rows(self, dst, f, k):
        total = dst.shape[0] // self.count
        quarter = total // 4
        return dst.at[pl.ds(pl.multiple_of(f * total + k * quarter, 8), quarter)]

    def copies(self, link, f, k, where, fresh=False):
        out = []
        for n, (src, dst) in enumerate(zip(self.srcs, self.dsts)):
            there = self.rows(dst, f, k)
            quarter = src.shape[0] // 4
            here = src.at[pl.ds(pl.multiple_of(k * quarter, 8), quarter)] if fresh else there
            out.append(push(here, there, self.sends.at[n, link, f, k], self.recvs.at[n, f, k],
                            where))
        return out

    def go(self, *args, **kw):
        for copy in self.copies(*args, **kw):
            copy.start()

    def arrived(self, f, k):
        for copy in self.copies(0, f, k, self.x_side):
            copy.wait_recv()

    def plane(self, j):
        return lax.rem(self.z + j, self.planes)

    def z_out(self, j, k):
        out = []
        z = self.plane(j)
        where = device(2 * z + self.x, self.y, self.c)
        for n, (src, dst) in enumerate(zip(self.srcs, self.dsts)):
            quarter = src.shape[0] // 4
            out.append(push(src.at[pl.ds(pl.multiple_of(k * quarter, 8), quarter)],
                            self.rows(dst, self.f, k), self.sends.at[n, 0, 2 * z + self.x, k],
                            self.recvs.at[n, self.f, k], where))
        return out

    def local(self):
        return [
            pltpu.make_async_copy(
                src, dst.at[pl.ds(pl.multiple_of(self.f * src.shape[0], 8), src.shape[0])],
                self.own.at[n])
            for n, (src, dst) in enumerate(zip(self.srcs, self.dsts))
        ]

    def start_x(self):
        for copy in self.local():
            copy.start()
        for k in (2 * self.y, 2 * self.y + 1, 2 * (1 - self.y) + 1):
            self.go(1, self.f, k, self.x_side, fresh=True)

    def start_z(self):
        def one(j):
            for side in range(2):
                for copy in self.z_out(j, 2 * self.y + side):
                    copy.start()

        looped(1, self.planes, one)

    def start(self):
        self.start_z()
        self.start_x()

    def spread(self, j):
        f = 2 * self.plane(j) + self.x
        for side in range(2):
            k = 2 * self.y + side
            self.arrived(f, k)
            self.go(1, f, k, self.x_side)
            self.go(2, f, k, self.y_side)

    def turn_x(self, j):
        f = 2 * self.plane(j) + 1 - self.x
        self.arrived(f, 2 * self.y)
        self.go(2, f, 2 * self.y, self.y_side)

    def turn_y(self, j):
        f = 2 * self.plane(j) + self.x
        k = 2 * (1 - self.y) + 1
        self.arrived(f, k)
        self.go(1, f, k, self.x_side)

    def events(self):
        out = [functools.partial(self.spread, j) for j in range(1, self.planes)]
        out += [functools.partial(self.turn_x, 0)]
        for j in range(1, self.planes):
            out += [functools.partial(self.turn_x, j), functools.partial(self.turn_y, j)]
        return out

    def finish(self):
        x, y = self.x, self.y
        for copy in self.local():
            copy.wait()

        def one(j):
            other = 2 * self.plane(j) + 1 - x
            self.arrived(other, 2 * y + 1)
            self.arrived(other, 2 * (1 - y) + 1)
            self.arrived(other, 2 * (1 - y))

        looped(0, self.planes, one)

        def two(j):
            self.arrived(2 * self.plane(j) + x, 2 * (1 - y))

        looped(1, self.planes, two)

        for k in (2 * y, 2 * y + 1, 2 * (1 - y) + 1):
            for copy in self.copies(1, self.f, k, self.x_side, fresh=True):
                copy.wait_send()

        def three(j):
            f = 2 * self.plane(j) + x
            for side in range(2):
                k = 2 * y + side
                for copy in (*self.z_out(j, k), *self.copies(1, f, k, self.x_side),
                             *self.copies(2, f, k, self.y_side)):
                    copy.wait_send()
            for copy in self.copies(1, f, 2 * (1 - y) + 1, self.x_side):
                copy.wait_send()

        looped(1, self.planes, three)

        def four(j):
            for copy in self.copies(2, 2 * self.plane(j) + 1 - x, 2 * y, self.y_side):
                copy.wait_send()

        looped(0, self.planes, four)


def build_diagonals(table_ref, band):
    left = jnp.broadcast_to(band[0:1, :], (lanes, lanes))
    right = jnp.broadcast_to(band[3 * lanes - 1 : 3 * lanes, :], (lanes, lanes))
    for half in range(2):
        cols = slice(half * lanes, (half + 1) * lanes)
        first = far - lanes + half * lanes
        for row in range(0, first, lanes):
            table_ref[row : row + lanes, cols] = left
        table_ref[first : first + 3 * lanes, cols] = band
        for row in range(first + 3 * lanes, reach, lanes):
            table_ref[row : row + lanes, cols] = right


def attend_kernel(
    fsdp_count, gathers, bound_ref, idx_ref, small_ref, tok_ref, cot_ref, *refs,
):
    if gathers:
        wq_src, wo_src, wgu_src, wd_src, *refs = refs
    else:
        w_given, *refs = refs
    (xs_ref, cs_ref, qkv_ref, pl_ref, ps_ref, ctx_ref, ctx32_ref, linv_ref, gains_ref, w_ref,
     *refs) = refs
    if gathers:
        wo_ref, wgu_ref, wd_ref, *refs = refs
    (smalls, xa, ca, p_long, p_short, table, mask, band, km, vt, ctx_t, linv_t,
     deal_send, deal_recv, pass_send, pass_recv, own, ctx_send, ctx_recv, p_sem, *refs) = refs
    f, p, c = place()
    rows_all, width = xs_ref.shape
    part = width // 2
    pairs = part // lanes
    short = rows_all - longest
    half = lanes // 2
    sibling = device(f, p, 1 - c)

    greet_all(fsdp_count)
    deals = [
        Dealing(fsdp_count, src, dst, deal_send.at[n], deal_recv.at[n], pass_send.at[n],
                pass_recv.at[n], own.at[n])
        for n, (src, dst) in enumerate(((small_ref, smalls), (tok_ref, xa), (cot_ref, ca)))
    ]
    events = []
    deals[0].start()
    deals[1].start()
    if gathers:
        sends_q, recvs_q, own_q, sends_r, recvs_r, own_r = refs
        first = Gathering(fsdp_count, (wq_src,), (w_ref,), sends_q, recvs_q, own_q)
        rest = Gathering(fsdp_count, (wo_src, wgu_src, wd_src), (wo_ref, wgu_ref, wd_ref),
                         sends_r, recvs_r, own_r)
        first.start()
        rest.start_x()
    deals[0].forward()
    deals[0].finish()

    slice_width = width // fsdp_count

    def gain_of(k, total):
        row = iota((lanes, width), 0)
        spot = jnp.where((iota((lanes, width), 1) == k * slice_width + row) & (row < slice_width),
                         1.0, 0.0).astype(bf16)
        return total + nn(smalls[c, p, k].astype(bf16), spot)

    gains_ref[...] = lax.fori_loop(0, fsdp_count, gain_of, jnp.zeros((8, width), f32))

    wide = 4 * lanes
    place_of = iota((lanes, wide), 1)
    offset = jnp.where(place_of < wide // 2, -place_of, wide - place_of)
    chosen = jnp.where(bucket_index(offset) == iota((lanes, wide), 0), 1.0, 0.0).astype(bf16)
    for side in range(2):
        by_head = nn(smalls[side, c, f].astype(bf16), chosen)
        for h in range(pairs):
            line = jnp.broadcast_to(by_head[2 + h : 3 + h, :], (lanes, wide))
            for d in range(3):
                turned = pltpu.roll(line, d * lanes, 1, stride=1, stride_axis=0)
                band[side * pairs + h, d * lanes : (d + 1) * lanes, :] = turned[:, lanes : 2 * lanes]

    bound = bound_ref[0]
    inside = (iota((short, short), 0) < bound) == (iota((short, short), 1) < bound)
    mask[...] = jnp.where(inside, 0.0, -1e30)

    if gathers:
        for event in first.events()[: first.planes - 1]:
            event()
    deals[1].forward()
    if gathers:
        rest.start_z()
        for event in first.events()[first.planes - 1 :]:
            event()
        events = rest.events()
    else:
        given = pltpu.make_async_copy(w_given, w_ref, own.at[3])
        given.start()
        given.wait()
    deals[2].start()
    deals[1].finish()
    if gathers:
        first.finish()

    xa_rows = xa.shape[0] * xa.shape[1] * xa.shape[2] * xa.shape[3]

    def arrive(i):
        rows = pl.ds(pl.multiple_of(i * block, block), block)
        chosen = one_hot(idx_ref[rows, :], iota((block, xa_rows), 1))
        return rows, chosen

    def tile(i):
        rows, chosen = arrive(i)
        x = nn(chosen, xa[...].reshape(xa_rows, width))
        xs_ref[rows, :] = x.astype(bf16)
        normed = (x * inverse_rms(x) * gains_ref[0:1, :]).astype(bf16)
        for k in range(3):
            cols = slice(k * part, (k + 1) * part)
            qkv_ref[rows, cols] = nn(normed, w_ref[:, cols]).astype(bf16)

    looped(0, rows_all // block, tile)

    def poll(count):
        for _ in range(count):
            if events:
                events.pop(0)()

    own_lane = iota((rows_all, lanes), 1) < half
    for pair in range(pairs):
        cols = [slice(kind * part + pair * lanes, kind * part + (pair + 1) * lanes)
                for kind in range(3)]
        keys = qkv_ref[:, cols[1]]
        vt[...] = jnp.transpose(qkv_ref[:, cols[2]].astype(f32)).astype(bf16)
        for h in range(2):
            build_diagonals(table, band[2 * pair + h])
            km[...] = jnp.where(own_lane == (h == 0), keys, jnp.zeros_like(keys))

            def strip(base, count, out_ref, masked, b):
                here = pl.ds(pl.multiple_of(base + b * block, block), block)
                logits = nt(km[base : base + count, :], qkv_ref[here, cols[0]])
                top_row = pl.multiple_of(far - b * block, block)
                logits = logits + table[pl.ds(top_row, count), :]
                spot = pl.ds(pl.multiple_of(b * block, block), block)
                if masked:
                    logits = logits + mask[:, spot]
                top = jnp.max(logits, axis=0, keepdims=True)
                weights = jnp.exp(logits - top)
                inv = 1.0 / jnp.sum(weights, axis=0, keepdims=True)
                low = weights.astype(bf16)
                spot = pl.ds(pl.multiple_of(h * count + b * block, block), block)
                out_ref[pair % 2, :, spot] = low
                part_rows = slice(h * half, (h + 1) * half)
                ctx_t[part_rows, here] = nn(vt[part_rows, base : base + count], low) * inv
                linv_t[part_rows, here] = jnp.broadcast_to(inv, (half, block))

            if h == 0 and pair >= 2:
                for copy in p_copies(p_long, p_short, pl_ref, ps_ref, p_sem, pair - 2):
                    copy.wait()
            looped(0, longest // block, functools.partial(strip, 0, longest, p_long, False))
            poll(1)
            looped(0, short // block, functools.partial(strip, longest, short, p_short, True))
            poll(1)
        context = jnp.transpose(ctx_t[...])
        spot = c * pairs + pair
        ctx32_ref[:, pair * lanes : (pair + 1) * lanes] = context
        ctx_ref[spot] = context.astype(bf16)
        linv_ref[:, pair * lanes : (pair + 1) * lanes] = jnp.transpose(linv_t[...])
        push(ctx_ref.at[spot], ctx_ref.at[spot], ctx_send.at[pair], ctx_recv.at[pair],
             sibling).start()
        for copy in p_copies(p_long, p_short, pl_ref, ps_ref, p_sem, pair):
            copy.start()
        if pair == pairs - 2:
            deals[2].forward()
    poll(len(events))
    deals[2].finish()

    def cot_tile(i):
        rows, chosen = arrive(i)
        cs_ref[rows, :] = nn(chosen, ca[...].reshape(xa_rows, width)).astype(bf16)

    looped(0, rows_all // block, cot_tile)
    for pair in range(pairs):
        spot = c * pairs + pair
        there = (1 - c) * pairs + pair
        push(ctx_ref.at[spot], ctx_ref.at[spot], ctx_send.at[pair], ctx_recv.at[pair],
             sibling).wait_send()
        push(ctx_ref.at[there], ctx_ref.at[there], ctx_send.at[pair], ctx_recv.at[pair],
             sibling).wait_recv()
    for pair in range(max(0, pairs - 2), pairs):
        for copy in p_copies(p_long, p_short, pl_ref, ps_ref, p_sem, pair):
            copy.wait()
    for deal in deals:
        deal.sent()
        deal.passed()
    if gathers:
        rest.finish()


def p_copies(p_long, p_short, pl_ref, ps_ref, sem, pair):
    return [
        pltpu.make_async_copy(p_long.at[pair % 2], pl_ref.at[pair], sem.at[0, pair]),
        pltpu.make_async_copy(p_short.at[pair % 2], ps_ref.at[pair], sem.at[1, pair]),
    ]


def attend(fsdp_count, gathers, bound, idx_col, small, tokens, cotangent, *weights):
    rows = idx_col.shape[0]
    piece, width = tokens.shape[2:]
    part = width // 2
    pairs = part // lanes
    short = rows - longest
    vm = pl.BlockSpec(memory_space=pltpu.VMEM)
    hbm = pl.BlockSpec(memory_space=pl.ANY)
    dma = pltpu.SemaphoreType.DMA
    arrivals = pltpu.VMEM((2, 2, fsdp_count, piece, width), bf16)
    full = [jax.ShapeDtypeStruct((w.shape[0] * fsdp_count, w.shape[1]), bf16) for w in weights]
    out_shape = [
        jax.ShapeDtypeStruct((rows, width), bf16),
        jax.ShapeDtypeStruct((rows, width), bf16),
        jax.ShapeDtypeStruct((rows, 3 * part), bf16),
        jax.ShapeDtypeStruct((pairs, longest, 2 * longest), bf16),
        jax.ShapeDtypeStruct((pairs, short, 2 * short), bf16),
        jax.ShapeDtypeStruct((2 * pairs, rows, lanes), bf16),
        jax.ShapeDtypeStruct((rows, part), f32),
        jax.ShapeDtypeStruct((rows, part), f32),
        jax.ShapeDtypeStruct((8, width), f32),
        jax.ShapeDtypeStruct((width, 3 * part), bf16),
    ]
    out_specs = [vm, vm, vm, hbm, hbm, vm, vm, vm, vm, vm]
    scratch = [
        pltpu.VMEM((2, 2, fsdp_count, 8, lanes), f32),
        arrivals, arrivals,
        pltpu.VMEM((2, longest, 2 * longest), bf16),
        pltpu.VMEM((2, short, 2 * short), bf16),
        pltpu.VMEM((reach, block), f32),
        pltpu.VMEM((short, short), f32),
        pltpu.VMEM((2 * pairs, 3 * lanes, lanes), f32),
        pltpu.VMEM((rows, lanes), bf16),
        pltpu.VMEM((lanes, rows), bf16),
        pltpu.VMEM((lanes, rows), f32),
        pltpu.VMEM((lanes, rows), f32),
        dma((3, 2 * fsdp_count)), dma((3, 2 * fsdp_count)), dma((3, 2 * fsdp_count)),
        dma((3, 2 * fsdp_count)), dma((4,)), dma((pairs,)), dma((pairs,)), dma((2, pairs)),
    ]
    if gathers:
        out_shape += full[1:]
        out_specs += [hbm] * 3
        scratch += [
            dma((1, 3, fsdp_count, 4)), dma((1, fsdp_count, 4)), dma((1,)),
            dma((3, 3, fsdp_count, 4)), dma((3, fsdp_count, 4)), dma((3,)),
        ]
    return pl.pallas_call(
        functools.partial(attend_kernel, fsdp_count, gathers),
        in_specs=[pl.BlockSpec(memory_space=pltpu.SMEM), vm, vm, hbm, hbm] + [hbm] * len(weights),
        out_specs=tuple(out_specs),
        out_shape=tuple(out_shape),
        scratch_shapes=scratch,
        compiler_params=pltpu.CompilerParams(
            vmem_limit_bytes=vmem_limit, collective_id=0, has_side_effects=True),
        name="attend",
    )(bound, idx_col, small, tokens, cotangent, *weights)


def feed_kernel(
    ctx_ref, xs_ref, cs_ref, wo_ref, gains_ref, wgu_ref, wd_ref,
    out_ref, ggu_ref, gd_ref, datt_ref, dctx_ref, go_ref, ggain_ref,
    mid, nff, hid, dgu, dn, dn_sib, send, recv,
):
    rows_all, width = xs_ref.shape
    ff = wd_ref.shape[0]
    part = width // 2
    lift = math.sqrt(2 / math.pi)
    tiles = rows_all // block
    f, p, c = place()
    sibling = device(f, p, 1 - c)
    gain = gains_ref[1:2, :]
    half_cols = pl.ds(pl.multiple_of(c * part, lanes), part)
    barrier = pltpu.get_barrier_semaphore()
    signal(barrier, sibling)
    pl.semaphore_wait(barrier, 1)

    def exchange(i):
        rows = pl.ds(pl.multiple_of(i * block, block), block)
        return pltpu.make_async_remote_copy(
            src_ref=dn.at[rows, :], dst_ref=dn_sib.at[rows, :], send_sem=send.at[i],
            recv_sem=recv.at[i], device_id=sibling, device_id_type=MESH)

    def tile(i, carry):
        rows = pl.ds(pl.multiple_of(i * block, block), block)
        mixed = jnp.concatenate([ctx_ref[n, rows, :] for n in range(ctx_ref.shape[0])], axis=1)
        middle = xs_ref[rows, :].astype(f32) + nn(mixed, wo_ref[...])
        mid[rows, :] = middle
        normed = (middle * inverse_rms(middle) * gain).astype(bf16)
        nff[rows, :] = normed
        upstream = cs_ref[rows, :]
        gate = nn(normed, wgu_ref[:, :ff])
        up = nn(normed, wgu_ref[:, ff:])
        d_hidden = nt(upstream, wd_ref[...])
        square = gate * gate
        bent = jnp.tanh(lift * gate * (1.0 + 0.044715 * square))
        halved = 0.5 * (1.0 + bent)
        gelu = gate * halved
        slope = halved + 0.5 * gate * (1.0 - bent * bent) * (
            lift * (1.0 + 3 * 0.044715 * square))
        hidden = (gelu * up).astype(bf16)
        hid[rows, :] = hidden
        d_gate = (d_hidden * up * slope).astype(bf16)
        d_up = (d_hidden * gelu).astype(bf16)
        dgu[rows, :ff] = d_gate
        dgu[rows, ff:] = d_up
        dn[rows, :] = (nt(d_gate, wgu_ref[:, :ff]) + nt(d_up, wgu_ref[:, ff:])).astype(bf16)
        exchange(i).start()
        out_ref[rows, :] = (0.5 * middle + nn(hidden, wd_ref[...])).astype(bf16)
        return carry

    lax.fori_loop(0, tiles, tile, 0)

    def down(i, carry):
        cols = pl.ds(pl.multiple_of(i * block, block), block)
        gd_ref[cols, :] = tn(hid[:, cols], cs_ref[...]).astype(bf16)
        return carry

    lax.fori_loop(0, ff // block, down, 0)

    def settle(i, total):
        rows = pl.ds(pl.multiple_of(i * block, block), block)
        exchange(i).wait()
        mine = dn[rows, :].astype(f32)
        grad = mine + dn_sib[rows, :].astype(f32)
        middle = mid[rows, :]
        s = inverse_rms(middle)
        unit = middle * s
        scaled = gain * grad
        d_middle = cs_ref[rows, :].astype(f32) + s * (
            scaled - unit * jnp.mean(scaled * unit, axis=-1, keepdims=True))
        low = d_middle.astype(bf16)
        datt_ref[rows, :] = low
        dctx_ref[rows, :] = nt(low, wo_ref[half_cols, :]).astype(bf16)
        return total + jnp.sum(mine * unit, axis=0, keepdims=True)

    ggain_ref[...] = lax.fori_loop(0, tiles, settle, jnp.zeros((1, width), f32))
    for n in range(0, ctx_ref.shape[0], 2):
        mixed = jnp.concatenate((ctx_ref[n], ctx_ref[n + 1]), axis=1)
        go_ref[n * lanes : (n + 2) * lanes, :] = tn(mixed, datt_ref[:, half_cols]).astype(bf16)

    def gate_up(i, carry):
        cols = pl.ds(pl.multiple_of(i * block, block), block)
        ggu_ref[cols, :] = tn(nff[:, cols], dgu[...]).astype(bf16)
        return carry

    lax.fori_loop(0, width // block, gate_up, 0)


def feed(ctx, xs, cs, w_out, gains, w_gu, w_down):
    rows, width = xs.shape
    ff = w_down.shape[0]
    part = width // 2
    vm = pl.BlockSpec(memory_space=pltpu.VMEM)
    return pl.pallas_call(
        feed_kernel,
        in_specs=[vm] * 7,
        out_specs=(vm,) * 7,
        out_shape=(
            jax.ShapeDtypeStruct((rows, width), bf16),
            jax.ShapeDtypeStruct((width, 2 * ff), bf16),
            jax.ShapeDtypeStruct((ff, width), bf16),
            jax.ShapeDtypeStruct((rows, width), bf16),
            jax.ShapeDtypeStruct((rows, part), bf16),
            jax.ShapeDtypeStruct((width, part), bf16),
            jax.ShapeDtypeStruct((1, width), f32),
        ),
        scratch_shapes=[
            pltpu.VMEM((rows, width), f32),
            pltpu.VMEM((rows, width), bf16),
            pltpu.VMEM((rows, ff), bf16),
            pltpu.VMEM((rows, 2 * ff), bf16),
            pltpu.VMEM((rows, width), bf16),
            pltpu.VMEM((rows, width), bf16),
            pltpu.SemaphoreType.DMA((rows // block,)),
            pltpu.SemaphoreType.DMA((rows // block,)),
        ],
        compiler_params=pltpu.CompilerParams(
            vmem_limit_bytes=vmem_limit, collective_id=2, has_side_effects=True),
        name="feed",
    )(ctx, xs, cs, w_out, gains, w_gu, w_down)


def back_kernel(
    xs_ref, gain_ref, w_ref, datt_ref, dctx_ref, qkv_ref, pl_ref, ps_ref, ctx32_ref, linv_ref,
    y_ref, gqkv_ref, ggain_ref, band_ref,
    normed, dqkv, table, dos, qs, ds_l, ds_s, va, kt, dq_t,
):
    rows_all, width = xs_ref.shape
    pairs = pl.num_programs(0)
    part = pairs * lanes
    step = pl.program_id(0)
    short = rows_all - longest
    half = lanes // 2
    gain_attn = gain_ref[0:1, :]

    def columns(kind):
        return pl.ds(pl.multiple_of(kind * part + step * lanes, lanes), lanes)

    lane = iota((rows_all, lanes), 1)
    queries = qkv_ref[:, columns(0)]
    keys = qkv_ref[:, columns(1)]
    values = qkv_ref[:, columns(2)]
    none = jnp.zeros_like(keys)
    kt[...] = jnp.transpose(keys.astype(f32)).astype(bf16)
    scaled = (dctx_ref[:, columns(0)].astype(f32) * linv_ref[...]).astype(bf16)
    against = scaled.astype(f32) * ctx32_ref[...]
    for h in range(2):
        mine = (lane < half) if h == 0 else (lane >= half)
        spare = half if h == 0 else 0
        delta = jnp.sum(jnp.where(mine, against, 0.0), axis=1, keepdims=True)
        high = delta.astype(bf16).astype(f32)
        rest = delta - high
        extra = jnp.where(lane == spare, -high, jnp.where(lane == spare + 1, -rest, 0.0))
        dos[h] = jnp.where(mine, scaled.astype(f32), extra).astype(bf16)
        qs[h] = jnp.where(mine, queries, none)
        ones = jnp.where((lane == spare) | (lane == spare + 1), 1.0, 0.0)
        va[...] = jnp.where(mine, values.astype(f32), ones).astype(bf16)
        table[...] = jnp.zeros_like(table)

        def strip(base, count, p_ref, ds_ref, b, carry):
            here = pl.ds(pl.multiple_of(base + b * block, block), block)
            spot = pl.ds(pl.multiple_of(h * count + b * block, block), block)
            d_weights = nt(va[base : base + count, :], dos[h, here, :])
            d_logits = p_ref[0, :, spot].astype(f32) * d_weights
            window = pl.ds(pl.multiple_of(far - b * block, block), count)
            table[window, :] = table[window, :] + d_logits
            low = d_logits.astype(bf16)
            ds_ref[:, spot] = low
            part_rows = slice(h * half, (h + 1) * half)
            dq_t[part_rows, here] = nn(kt[part_rows, base : base + count], low)
            return carry

        lax.fori_loop(
            0, longest // block, functools.partial(strip, 0, longest, pl_ref, ds_l), 0)
        lax.fori_loop(
            0, short // block, functools.partial(strip, longest, short, ps_ref, ds_s), 0)
        before = far - lanes
        after = far + 3 * lanes
        band = table[before : before + 3 * lanes, :lanes] + table[far : far + 3 * lanes, lanes:]
        left = jnp.sum(table[:before, :lanes] + table[:before, lanes:], axis=0, keepdims=True)
        left = left + jnp.sum(table[before:far, lanes:], axis=0, keepdims=True)
        right = jnp.sum(table[after:, :lanes] + table[after:, lanes:], axis=0, keepdims=True)
        right = right + jnp.sum(table[after - lanes : after, :lanes], axis=0, keepdims=True)
        row = iota((3 * lanes, lanes), 0)
        band = band + jnp.where(row == 0, left, 0.0) + jnp.where(row == 3 * lanes - 1, right, 0.0)
        band_ref[h] = band

    dqkv[:, columns(0)] = jnp.transpose(dq_t[...]).astype(bf16)
    own = iota((rows_all, lanes), 1) < half
    for base, count, p_ref, ds_ref in ((0, longest, pl_ref, ds_l), (longest, short, ps_ref, ds_s)):
        rows = slice(base, base + count)
        clean = [
            jnp.where(own[rows] == (h == 0), dos[h, rows, :].astype(f32), 0.0).astype(bf16)
            for h in range(2)
        ]
        dqkv[rows, columns(2)] = nn(p_ref[0], jnp.concatenate(clean, axis=0)).astype(bf16)
        both = jnp.concatenate((qs[0, rows, :], qs[1, rows, :]), axis=0)
        dqkv[rows, columns(1)] = nn(ds_ref[...], both).astype(bf16)

    @pl.when(step == pairs - 1)
    def _():
        def tile(i, total):
            rows = pl.ds(pl.multiple_of(i * block, block), block)
            x = xs_ref[rows, :].astype(f32)
            s = inverse_rms(x)
            unit = x * s
            grad = nt(dqkv[rows, :], w_ref[...])
            scaled = gain_attn * grad
            y = 0.5 * datt_ref[rows, :].astype(f32) + s * (
                scaled - unit * jnp.mean(scaled * unit, axis=-1, keepdims=True))
            y_ref[rows, :] = y.astype(bf16)
            normed[rows, :] = (unit * gain_attn).astype(bf16)
            return total + jnp.sum(grad * unit, axis=0, keepdims=True)

        zero = jnp.zeros((1, width), f32)
        ggain_ref[...] = lax.fori_loop(0, rows_all // block, tile, zero)

        def weight(i, carry):
            cols = pl.ds(pl.multiple_of(i * block, block), block)
            gqkv_ref[cols, :] = tn(normed[:, cols], dqkv[...]).astype(bf16)
            return carry

        lax.fori_loop(0, width // block, weight, 0)


def back(xs, gain, w_qkv, datt, dctx, qkv, p_long, p_short, ctx32, linv):
    rows, width = xs.shape
    part = w_qkv.shape[1] // 3
    pairs = part // lanes
    short = rows - longest
    lane_block = pl.BlockSpec((rows, lanes), lambda i: (0, i))
    return pl.pallas_call(
        back_kernel,
        grid=(pairs,),
        in_specs=[
            *(whole_spec(a.shape) for a in (xs, gain, w_qkv, datt, dctx, qkv)),
            pl.BlockSpec((1, longest, 2 * longest), lambda i: (i, 0, 0)),
            pl.BlockSpec((1, short, 2 * short), lambda i: (i, 0, 0)),
            lane_block, lane_block,
        ],
        out_specs=(
            whole_spec((rows, width)),
            whole_spec((width, 3 * part)),
            whole_spec((1, width)),
            pl.BlockSpec((2, 3 * lanes, lanes), lambda i: (i, 0, 0)),
        ),
        out_shape=(
            jax.ShapeDtypeStruct((rows, width), bf16),
            jax.ShapeDtypeStruct((width, 3 * part), bf16),
            jax.ShapeDtypeStruct((1, width), f32),
            jax.ShapeDtypeStruct((2 * pairs, 3 * lanes, lanes), f32),
        ),
        scratch_shapes=[
            pltpu.VMEM((rows, width), bf16),
            pltpu.VMEM((rows, 3 * part), bf16),
            pltpu.VMEM((reach, block), f32),
            pltpu.VMEM((2, rows, lanes), bf16),
            pltpu.VMEM((2, rows, lanes), bf16),
            pltpu.VMEM((longest, 2 * longest), bf16),
            pltpu.VMEM((short, 2 * short), bf16),
            pltpu.VMEM((rows, lanes), bf16),
            pltpu.VMEM((lanes, rows), bf16),
            pltpu.VMEM((lanes, rows), f32),
        ],
        compiler_params=pltpu.CompilerParams(
            dimension_semantics=("arbitrary",), vmem_limit_bytes=vmem_limit),
        name="back",
    )(xs, gain, w_qkv, datt, dctx, qkv, p_long, p_short, ctx32, linv)


def home_kernel(fsdp_count, a_ref, b_ref, ra_ref, rb_ref, send, recv, own):
    f = lax.axis_index("fsdp")
    s = lax.axis_index("sp")
    p, c = s // 2, s % 2
    mine = p * fsdp_count + f
    peers = 2 * fsdp_count
    barrier = pltpu.get_barrier_semaphore()

    def where(k):
        return {"fsdp": k % fsdp_count, "sp": (k // fsdp_count) * 2 + c}

    def greet(i, carry):
        k = lax.rem(mine + i, peers)
        pl.semaphore_signal(barrier, inc=1, device_id=where(k), device_id_type=MESH)
        return carry

    lax.fori_loop(1, peers, greet, 0)
    pl.semaphore_wait(barrier, peers - 1)

    def piece(which, src, dst, k):
        return pltpu.make_async_remote_copy(
            src_ref=src.at[k // fsdp_count, k % fsdp_count],
            dst_ref=dst.at[p, f],
            send_sem=send.at[which, k],
            recv_sem=recv.at[which, mine],
            device_id=where(k),
            device_id_type=MESH,
        )

    def arrived(which, src, dst, k):
        return pltpu.make_async_remote_copy(
            src_ref=src.at[k // fsdp_count, k % fsdp_count],
            dst_ref=dst.at[k // fsdp_count, k % fsdp_count],
            send_sem=send.at[which, k],
            recv_sem=recv.at[which, k],
            device_id=where(k),
            device_id_type=MESH,
        )

    pairs = ((0, a_ref, ra_ref), (1, b_ref, rb_ref))
    for which, src, dst in pairs:

        def start(i, carry):
            piece(which, src, dst, lax.rem(mine + i, peers)).start()
            return carry

        lax.fori_loop(1, peers, start, 0)
        local = pltpu.make_async_copy(src.at[p, f], dst.at[p, f], own.at[which])
        local.start()
        local.wait()
    for which, src, dst in pairs:

        def finish(i, carry):
            k = lax.rem(mine + i, peers)
            arrived(which, src, dst, k).wait_recv()
            piece(which, src, dst, k).wait_send()
            return carry

        lax.fori_loop(1, peers, finish, 0)


def home(first, second):
    fsdp_count, piece, width = first.shape[1:]
    out = jax.ShapeDtypeStruct((2, fsdp_count, piece, width), bf16)
    hbm = pl.BlockSpec(memory_space=pl.ANY)
    sem = pltpu.SemaphoreType.DMA((2, 2 * fsdp_count))
    return pl.pallas_call(
        functools.partial(home_kernel, fsdp_count),
        out_shape=(out, out),
        in_specs=[hbm, hbm],
        out_specs=(hbm, hbm),
        scratch_shapes=[sem, sem, pltpu.SemaphoreType.DMA((2,))],
        compiler_params=pltpu.CompilerParams(collective_id=1, has_side_effects=True),
        name="home",
    )(first, second)


def unslot_kernel(idx_ref, a_ref, b_ref, oa_ref, ob_ref):
    rows_all = a_ref.shape[0]

    def tile(i):
        rows = pl.ds(pl.multiple_of(i * block, block), block)
        chosen = one_hot(iota((block, rows_all), 0) + i * block, idx_ref[...])
        oa_ref[rows, :] = nn(chosen, a_ref[...]).astype(bf16)
        ob_ref[rows, :] = nn(chosen, b_ref[...]).astype(bf16)

    looped(0, oa_ref.shape[0] // block, tile)


def unslot(rows, idx_row, first, second):
    vm = pl.BlockSpec(memory_space=pltpu.VMEM)
    out = jax.ShapeDtypeStruct((rows, first.shape[1]), bf16)
    return pl.pallas_call(
        unslot_kernel,
        in_specs=[vm] * 3,
        out_specs=(vm, vm),
        out_shape=(out, out),
        compiler_params=pltpu.CompilerParams(vmem_limit_bytes=vmem_limit),
        name="unslot",
    )(idx_row, first, second)


def shards(
    tokens, cotangent, lengths, dealing, gain_attn, w_query, w_key, w_value, w_out, bias_table,
    gain_ff, w_gate, w_up, w_down,
):
    fsdp_count = lax.axis_size("fsdp")
    sp_count = lax.axis_size("sp")
    micro_count, token_rows, width = tokens.shape
    piece = token_rows // fsdp_count
    group_rows = token_rows * sp_count
    local_heads = bias_table.shape[1]
    heads = local_heads * sp_count
    part = width // 2
    s = lax.axis_index("sp")
    p, c = s // 2, s % 2
    sibling = [(0, 1), (1, 0), (2, 3), (3, 2)]
    across = [(0, 2), (2, 0), (1, 3), (3, 1)]

    def swap(value):
        return lax.ppermute(value, "sp", sibling)

    full_piece = -(-piece // 8) * 8

    def pieces(value):
        value = value.reshape(micro_count, fsdp_count, piece, width)
        return jnp.pad(value, ((0, 0), (0, 0), (0, full_piece - piece), (0, 0)))

    order = lax.dynamic_index_in_dim(dealing[:, 0], p, 0, keepdims=False)
    length = lax.dynamic_index_in_dim(lengths[:, 0], p, 0, keepdims=False)
    first_long = length[0] == longest
    start = jnp.where(first_long, 0, jnp.where(length[1] == longest, length[0],
                                               length[0] + length[1]))
    bound = jnp.where(first_long, length[1], length[0]).reshape(1)
    short = group_rows - longest
    head_part = lax.dynamic_slice_in_dim(order, start, longest, 0)
    tail = jnp.where(jnp.arange(short) < start, order[:short], order[longest:])
    order = jnp.concatenate((head_part, tail))
    source, within = order // token_rows, order % token_rows
    idx = ((source % 2) * 2 + source // 2) * fsdp_count + within // piece
    idx = idx * full_piece + within % piece

    def half_cols(weight):
        return lax.dynamic_slice_in_dim(weight, c * part, part, 1)

    def half_ff(weight):
        split = weight.reshape(weight.shape[0], fsdp_count, 2, -1)
        return lax.dynamic_index_in_dim(split, c, 2, keepdims=False).reshape(weight.shape[0], -1)

    def gather(value, axis=0):
        return lax.all_gather(value, "fsdp", axis=axis, tiled=True)

    def line(value):
        return jnp.pad(value.astype(f32), ((0, 0), (0, lanes - value.shape[1])))

    small = jnp.concatenate([line(gain_attn[None]), line(gain_ff[None]), line(bias_table.T)])
    small = jnp.pad(small, ((0, 8 - small.shape[0]), (0, 0)))
    down_rows = w_down.shape[0] // 2
    weights = (
        jnp.concatenate([half_cols(w) for w in (w_query, w_key, w_value)], axis=1),
        w_out,
        jnp.concatenate([half_ff(w) for w in (w_gate, w_up)], axis=1),
        lax.dynamic_slice_in_dim(w_down, c * down_rows, down_rows, 0),
    )
    gathers = all(w.shape[0] % 32 == 0 for w in weights)
    if not gathers:
        weights = tuple(gather(w) for w in weights)
    args = (bound, idx.reshape(-1, 1), small, pieces(tokens), pieces(cotangent))
    xs, cs, qkv, p_long, p_short, ctx, ctx32, linv, gains, w_qkv, *late = attend(
        fsdp_count, gathers, *args, *(weights if gathers else weights[:1]))
    wo, w_gu, wd = late if gathers else weights[1:]
    buckets = band_buckets()
    out_part, grad_gu, grad_d, datt, dctx, grad_o, grad_gain_ff = feed(
        ctx, xs, cs, wo, gains, w_gu, wd)
    y, grad_qkv, grad_gain_attn, grad_band = back(
        xs, gains, w_qkv, datt, dctx, qkv, p_long, p_short, ctx32, linv)
    grad_gain = jnp.concatenate((grad_gain_attn, grad_gain_ff))
    back_rows = unslot(4 * fsdp_count * full_piece, idx.reshape(1, -1), out_part, y)
    mine = 2 * fsdp_count * full_piece
    shape = (2, fsdp_count, full_piece, width)

    def join(value):
        kept = lax.dynamic_slice_in_dim(value, c * mine, mine, 0)
        given = lax.dynamic_slice_in_dim(value, (1 - c) * mine, mine, 0)
        return (kept.astype(f32) + swap(given).astype(f32)).astype(bf16).reshape(shape)

    output, grad_tokens = (x[:, :, :piece] for x in home(join(back_rows[0]), join(back_rows[1])))

    def packed(values, unit):
        cut = [v.reshape(fsdp_count, v.shape[0] // fsdp_count, -1, unit) for v in values]
        cut = [jnp.swapaxes(v, 1, 2).reshape(fsdp_count, -1, unit) for v in cut]
        return jnp.concatenate(cut, axis=1)

    def scatter(values, unit):
        whole = packed(values, unit)
        share = lax.psum_scatter(whole, "fsdp", scatter_dimension=0, tiled=True)[0]
        out, at = [], 0
        for v in values:
            rows, count = v.shape[0] // fsdp_count, v.shape[1] // unit
            one = share[at : at + rows * count].reshape(count, rows, unit)
            out.append(jnp.swapaxes(one, 0, 1).reshape(rows, -1))
            at += rows * count
        return out

    shares = scatter((grad_gu, grad_d), 256) + scatter((grad_qkv, grad_o), 384)
    flat = jnp.concatenate([v.reshape(-1) for v in shares])
    flat = (flat.astype(f32) + lax.ppermute(flat, "sp", across).astype(f32)).astype(bf16)
    flat_sib = swap(flat)
    low = jnp.where(c == 0, flat, flat_sib).astype(f32)
    high = jnp.where(c == 0, flat_sib, flat).astype(f32)
    pieces = []
    at = 0
    for v in shares:
        pieces.append([x[at : at + v.size].reshape(v.shape) for x in (low, high)])
        at += v.size
    gu, gd, gqkv, go = pieces
    ff = gu[0].shape[1] // 2

    def ff_cols(which):
        sides = [x[:, which * ff : (which + 1) * ff].reshape(x.shape[0], fsdp_count, 1, -1)
                 for x in gu]
        return jnp.concatenate(sides, axis=2).reshape(gu[0].shape[0], -1)

    def proj(which):
        return jnp.concatenate([x[:, which * part : (which + 1) * part] for x in gqkv], axis=1)

    sums = jnp.stack([
        jnp.sum(jnp.where(buckets[None] == label, grad_band, 0.0), axis=(1, 2))
        for label in range(bias_table.shape[0])
    ])
    spread = jnp.zeros((bias_table.shape[0], heads), f32)
    spread = lax.dynamic_update_slice(spread, sums, (0, c * (heads // 2)))
    small = lax.psum(jnp.concatenate((grad_gain.reshape(-1), spread.reshape(-1))), ("fsdp", "sp"))
    own_gain = width // fsdp_count
    f = lax.axis_index("fsdp")
    gains_grad = lax.dynamic_slice_in_dim(small[: 2 * width].reshape(2, width), f * own_gain,
                                          own_gain, 1)
    bias_grad = lax.dynamic_slice_in_dim(small[2 * width :].reshape(-1, heads), s * local_heads,
                                         local_heads, 1)
    return (
        output.reshape(tokens.shape), grad_tokens.reshape(tokens.shape), gains_grad[0],
        proj(0), proj(1), proj(2), jnp.concatenate(go, axis=1), bias_grad, gains_grad[1],
        ff_cols(0), ff_cols(1), jnp.concatenate(gd, axis=0),
    )


def solution(mesh):
    return jax.shard_map(
        shards,
        mesh=mesh,
        in_specs=(
            P(None, ("fsdp", "sp"), None), P(None, ("fsdp", "sp"), None),
            P(None, "fsdp", None), P(None, "fsdp", None),
            P("fsdp"), P("fsdp", None), P("fsdp", None), P("fsdp", None), P("fsdp", None),
            P(None, "sp"), P("fsdp"), P("fsdp", None), P("fsdp", None), P("fsdp", None),
        ),
        out_specs=(
            P(None, ("fsdp", "sp"), None), P(None, ("fsdp", "sp"), None),
            P("fsdp"), P("fsdp", None), P("fsdp", None), P("fsdp", None), P("fsdp", None),
            P(None, "sp"), P("fsdp"), P("fsdp", None), P("fsdp", None), P("fsdp", None),
        ),
        check_vma=False,
    )
```

```python
import functools
import math

import jax
import jax.numpy as jnp
from jax import lax
from jax.experimental import pallas as pl
from jax.experimental.pallas import tpu as pltpu
from jax.sharding import PartitionSpec as P

bucket_edges = (1, 2, 3, 4, 5, 6, 7, 8, 12, 16, 23, 32, 46, 64, 91)
epsilon = 1e-06
longest = 1024
lanes = 128
block = 256
far = 768
reach = 1792
MESH = pl.DeviceIdType.MESH
f32 = jnp.float32
bf16 = jnp.bfloat16
vmem_limit = 62 * 2**20


def nn(left, right):
    return jnp.dot(left, right, preferred_element_type=f32)


def nt(left, right):
    return lax.dot_general(left, right, (((1,), (1,)), ((), ())), preferred_element_type=f32)


def tn(left, right):
    return lax.dot_general(left, right, (((0,), (0,)), ((), ())), preferred_element_type=f32)


def iota(shape, dim):
    return lax.broadcasted_iota(jnp.int32, shape, dim)


def one_hot(column, row):
    return jnp.where(column == row, 1.0, 0.0).astype(bf16)


def inverse_rms(values):
    return lax.rsqrt(jnp.mean(values * values, axis=-1, keepdims=True) + epsilon)


def bucket_index(offset):
    distance = jnp.abs(offset)
    bucket_sum = jnp.where(offset > 0, 16, 0).astype(jnp.int32)
    for border in bucket_edges:
        bucket_sum = bucket_sum + (distance >= border).astype(jnp.int32)
    return bucket_sum


def band_buckets():
    shape = (3 * lanes, lanes)
    return bucket_index(iota(shape, 0) - lanes - iota(shape, 1))


def whole_spec(shape, space=pltpu.VMEM):
    return pl.BlockSpec(shape, lambda *_: (0,) * len(shape), memory_space=space,
                        pipeline_mode=pl.Buffered(1))


def place():
    f = lax.axis_index("fsdp")
    s = lax.axis_index("sp")
    return f, s // 2, s % 2


def device(f, p, c):
    return {"fsdp": f, "sp": 2 * p + c}


def signal(barrier, where):
    pl.semaphore_signal(barrier, inc=1, device_id=where, device_id_type=MESH)


def greet_all(fsdp_count):
    f, p, c = place()
    barrier = pltpu.get_barrier_semaphore()
    peers = 2 * fsdp_count
    mine = p * fsdp_count + f

    def greet(i, carry):
        k = lax.rem(mine + i, peers)
        signal(barrier, device(k % fsdp_count, k // fsdp_count, c))
        return carry

    lax.fori_loop(1, peers, greet, 0)
    signal(barrier, device(f, p, 1 - c))
    pl.semaphore_wait(barrier, peers)


def push(src, dst, send, recv, where):
    return pltpu.make_async_remote_copy(
        src_ref=src, dst_ref=dst, send_sem=send, recv_sem=recv, device_id=where,
        device_id_type=MESH)


def looped(first, last, body):
    def step(i, carry):
        body(i)
        return carry

    lax.fori_loop(first, last, step, 0)


class Dealing:
    def __init__(self, fsdp_count, src, dst, send, recv, pass_send, pass_recv, own):
        self.f, self.p, self.c = place()
        self.count = fsdp_count
        self.peers = 2 * fsdp_count
        self.mine = self.p * fsdp_count + self.f
        self.src, self.dst, self.send, self.recv = src, dst, send, recv
        self.pass_send, self.pass_recv, self.own = pass_send, pass_recv, own

    def source(self, k):
        return self.src.at[k // self.count, k % self.count] if len(self.src.shape) == 4 else self.src

    def out(self, k):
        where = device(k % self.count, k // self.count, self.c)
        return push(self.source(k), self.dst.at[self.c, self.p, self.f], self.send.at[k],
                    self.recv.at[self.mine], where)

    def come(self, k):
        where = device(k % self.count, k // self.count, self.c)
        return push(self.source(k), self.dst.at[self.c, k // self.count, k % self.count],
                    self.send.at[k], self.recv.at[k], where)

    def onward(self, k, side):
        here = self.dst.at[side, k // self.count, k % self.count]
        return push(here, here, self.pass_send.at[k], self.pass_recv.at[k],
                    device(self.f, self.p, 1 - self.c))

    def local(self):
        return pltpu.make_async_copy(
            self.source(self.mine), self.dst.at[self.c, self.p, self.f], self.own)

    def start(self):
        looped(1, self.peers, lambda i: self.out(lax.rem(self.mine + i, self.peers)).start())
        self.local().start()

    def forward(self):
        self.local().wait()
        self.onward(self.mine, self.c).start()

        def one(i):
            k = lax.rem(self.mine + self.peers - i, self.peers)
            self.come(k).wait_recv()
            self.onward(k, self.c).start()

        looped(1, self.peers, one)

    def sent(self):
        looped(1, self.peers, lambda i: self.out(lax.rem(self.mine + i, self.peers)).wait_send())

    def finish(self):
        looped(0, self.peers, lambda k: self.onward(k, 1 - self.c).wait_recv())

    def passed(self):
        looped(0, self.peers, lambda k: self.onward(k, self.c).wait_send())


class Gathering:
    def __init__(self, fsdp_count, srcs, dsts, sends, recvs, own):
        self.f, self.y, self.c = place()
        self.count = fsdp_count
        self.planes = fsdp_count // 2
        self.z, self.x = self.f // 2, self.f % 2
        self.srcs, self.dsts, self.sends, self.recvs, self.own = srcs, dsts, sends, recvs, own
        self.x_side = device(self.z * 2 + 1 - self.x, self.y, self.c)
        self.y_side = device(self.f, 1 - self.y, self.c)

    def rows(self, dst, f, k):
        total = dst.shape[0] // self.count
        quarter = total // 4
        return dst.at[pl.ds(pl.multiple_of(f * total + k * quarter, 8), quarter)]

    def copies(self, link, f, k, where, fresh=False):
        out = []
        for n, (src, dst) in enumerate(zip(self.srcs, self.dsts)):
            there = self.rows(dst, f, k)
            quarter = src.shape[0] // 4
            here = src.at[pl.ds(pl.multiple_of(k * quarter, 8), quarter)] if fresh else there
            out.append(push(here, there, self.sends.at[n, link, f, k], self.recvs.at[n, f, k],
                            where))
        return out

    def go(self, *args, **kw):
        for copy in self.copies(*args, **kw):
            copy.start()

    def arrived(self, f, k):
        for copy in self.copies(0, f, k, self.x_side):
            copy.wait_recv()

    def plane(self, j):
        return lax.rem(self.z + j, self.planes)

    def z_out(self, j, k):
        out = []
        z = self.plane(j)
        where = device(2 * z + self.x, self.y, self.c)
        for n, (src, dst) in enumerate(zip(self.srcs, self.dsts)):
            quarter = src.shape[0] // 4
            out.append(push(src.at[pl.ds(pl.multiple_of(k * quarter, 8), quarter)],
                            self.rows(dst, self.f, k), self.sends.at[n, 0, 2 * z + self.x, k],
                            self.recvs.at[n, self.f, k], where))
        return out

    def local(self):
        return [
            pltpu.make_async_copy(
                src, dst.at[pl.ds(pl.multiple_of(self.f * src.shape[0], 8), src.shape[0])],
                self.own.at[n])
            for n, (src, dst) in enumerate(zip(self.srcs, self.dsts))
        ]

    def start_x(self):
        for copy in self.local():
            copy.start()
        for k in (2 * self.y, 2 * self.y + 1, 2 * (1 - self.y) + 1):
            self.go(1, self.f, k, self.x_side, fresh=True)

    def start_z(self):
        def one(j):
            for side in range(2):
                for copy in self.z_out(j, 2 * self.y + side):
                    copy.start()

        looped(1, self.planes, one)

    def start(self):
        self.start_z()
        self.start_x()

    def spread(self, j):
        f = 2 * self.plane(j) + self.x
        for side in range(2):
            k = 2 * self.y + side
            self.arrived(f, k)
            self.go(1, f, k, self.x_side)
            self.go(2, f, k, self.y_side)

    def turn_x(self, j):
        f = 2 * self.plane(j) + 1 - self.x
        self.arrived(f, 2 * self.y)
        self.go(2, f, 2 * self.y, self.y_side)

    def turn_y(self, j):
        f = 2 * self.plane(j) + self.x
        k = 2 * (1 - self.y) + 1
        self.arrived(f, k)
        self.go(1, f, k, self.x_side)

    def events(self):
        out = [functools.partial(self.spread, j) for j in range(1, self.planes)]
        out += [functools.partial(self.turn_x, 0)]
        for j in range(1, self.planes):
            out += [functools.partial(self.turn_x, j), functools.partial(self.turn_y, j)]
        return out

    def finish(self):
        x, y = self.x, self.y
        for copy in self.local():
            copy.wait()

        def one(j):
            other = 2 * self.plane(j) + 1 - x
            self.arrived(other, 2 * y + 1)
            self.arrived(other, 2 * (1 - y) + 1)
            self.arrived(other, 2 * (1 - y))

        looped(0, self.planes, one)

        def two(j):
            self.arrived(2 * self.plane(j) + x, 2 * (1 - y))

        looped(1, self.planes, two)

        for k in (2 * y, 2 * y + 1, 2 * (1 - y) + 1):
            for copy in self.copies(1, self.f, k, self.x_side, fresh=True):
                copy.wait_send()

        def three(j):
            f = 2 * self.plane(j) + x
            for side in range(2):
                k = 2 * y + side
                for copy in (*self.z_out(j, k), *self.copies(1, f, k, self.x_side),
                             *self.copies(2, f, k, self.y_side)):
                    copy.wait_send()
            for copy in self.copies(1, f, 2 * (1 - y) + 1, self.x_side):
                copy.wait_send()

        looped(1, self.planes, three)

        def four(j):
            for copy in self.copies(2, 2 * self.plane(j) + 1 - x, 2 * y, self.y_side):
                copy.wait_send()

        looped(0, self.planes, four)


def build_diagonals(table_ref, band):
    left = jnp.broadcast_to(band[0:1, :], (lanes, lanes))
    right = jnp.broadcast_to(band[3 * lanes - 1 : 3 * lanes, :], (lanes, lanes))
    for half in range(2):
        cols = slice(half * lanes, (half + 1) * lanes)
        first = far - lanes + half * lanes
        for row in range(0, first, lanes):
            table_ref[row : row + lanes, cols] = left
        table_ref[first : first + 3 * lanes, cols] = band
        for row in range(first + 3 * lanes, reach, lanes):
            table_ref[row : row + lanes, cols] = right


def attend_kernel(
    fsdp_count, gathers, bound_ref, idx_ref, small_ref, tok_ref, cot_ref, *refs,
):
    if gathers:
        wq_src, wo_src, wgu_src, wd_src, *refs = refs
    else:
        w_given, *refs = refs
    (xs_ref, cs_ref, qkv_ref, pl_ref, ps_ref, ctx_ref, ctx32_ref, linv_ref, gains_ref, w_ref,
     *refs) = refs
    if gathers:
        wo_ref, wgu_ref, wd_ref, *refs = refs
    (smalls, xa, ca, p_long, p_short, table, mask, band, km, vt, ctx_t, linv_t,
     deal_send, deal_recv, pass_send, pass_recv, own, ctx_send, ctx_recv, p_sem, *refs) = refs
    f, p, c = place()
    rows_all, width = xs_ref.shape
    part = width // 2
    pairs = part // lanes
    short = rows_all - longest
    half = lanes // 2
    sibling = device(f, p, 1 - c)

    greet_all(fsdp_count)
    deals = [
        Dealing(fsdp_count, src, dst, deal_send.at[n], deal_recv.at[n], pass_send.at[n],
                pass_recv.at[n], own.at[n])
        for n, (src, dst) in enumerate(((small_ref, smalls), (tok_ref, xa), (cot_ref, ca)))
    ]
    events = []
    deals[0].start()
    deals[1].start()
    if gathers:
        sends_q, recvs_q, own_q, sends_r, recvs_r, own_r = refs
        first = Gathering(fsdp_count, (wq_src,), (w_ref,), sends_q, recvs_q, own_q)
        rest = Gathering(fsdp_count, (wo_src, wgu_src, wd_src), (wo_ref, wgu_ref, wd_ref),
                         sends_r, recvs_r, own_r)
        first.start()
        rest.start_x()
    deals[0].forward()
    deals[0].finish()

    slice_width = width // fsdp_count

    def gain_of(k, total):
        row = iota((lanes, width), 0)
        spot = jnp.where((iota((lanes, width), 1) == k * slice_width + row) & (row < slice_width),
                         1.0, 0.0).astype(bf16)
        return total + nn(smalls[c, p, k].astype(bf16), spot)

    gains_ref[...] = lax.fori_loop(0, fsdp_count, gain_of, jnp.zeros((8, width), f32))

    wide = 4 * lanes
    place_of = iota((lanes, wide), 1)
    offset = jnp.where(place_of < wide // 2, -place_of, wide - place_of)
    chosen = jnp.where(bucket_index(offset) == iota((lanes, wide), 0), 1.0, 0.0).astype(bf16)
    for side in range(2):
        by_head = nn(smalls[side, c, f].astype(bf16), chosen)
        for h in range(pairs):
            line = jnp.broadcast_to(by_head[2 + h : 3 + h, :], (lanes, wide))
            for d in range(3):
                turned = pltpu.roll(line, d * lanes, 1, stride=1, stride_axis=0)
                band[side * pairs + h, d * lanes : (d + 1) * lanes, :] = turned[:, lanes : 2 * lanes]

    bound = bound_ref[0]
    inside = (iota((short, short), 0) < bound) == (iota((short, short), 1) < bound)
    mask[...] = jnp.where(inside, 0.0, -1e30)

    if gathers:
        for event in first.events()[: first.planes - 1]:
            event()
    deals[1].forward()
    if gathers:
        rest.start_z()
        for event in first.events()[first.planes - 1 :]:
            event()
        events = rest.events()
    else:
        given = pltpu.make_async_copy(w_given, w_ref, own.at[3])
        given.start()
        given.wait()
    deals[2].start()
    deals[1].finish()
    if gathers:
        first.finish()

    xa_rows = xa.shape[0] * xa.shape[1] * xa.shape[2] * xa.shape[3]

    def arrive(i):
        rows = pl.ds(pl.multiple_of(i * block, block), block)
        chosen = one_hot(idx_ref[rows, :], iota((block, xa_rows), 1))
        return rows, chosen

    def tile(i):
        rows, chosen = arrive(i)
        x = nn(chosen, xa[...].reshape(xa_rows, width))
        xs_ref[rows, :] = x.astype(bf16)
        normed = (x * inverse_rms(x) * gains_ref[0:1, :]).astype(bf16)
        for k in range(3):
            cols = slice(k * part, (k + 1) * part)
            qkv_ref[rows, cols] = nn(normed, w_ref[:, cols]).astype(bf16)

    looped(0, rows_all // block, tile)

    def poll(count):
        for _ in range(count):
            if events:
                events.pop(0)()

    own_lane = iota((rows_all, lanes), 1) < half
    for pair in range(pairs):
        cols = [slice(kind * part + pair * lanes, kind * part + (pair + 1) * lanes)
                for kind in range(3)]
        keys = qkv_ref[:, cols[1]]
        vt[...] = jnp.transpose(qkv_ref[:, cols[2]].astype(f32)).astype(bf16)
        for h in range(2):
            build_diagonals(table, band[2 * pair + h])
            km[...] = jnp.where(own_lane == (h == 0), keys, jnp.zeros_like(keys))

            def strip(base, count, out_ref, masked, b):
                here = pl.ds(pl.multiple_of(base + b * block, block), block)
                logits = nt(km[base : base + count, :], qkv_ref[here, cols[0]])
                top_row = pl.multiple_of(far - b * block, block)
                logits = logits + table[pl.ds(top_row, count), :]
                spot = pl.ds(pl.multiple_of(b * block, block), block)
                if masked:
                    logits = logits + mask[:, spot]
                top = jnp.max(logits, axis=0, keepdims=True)
                weights = jnp.exp(logits - top)
                inv = 1.0 / jnp.sum(weights, axis=0, keepdims=True)
                low = weights.astype(bf16)
                spot = pl.ds(pl.multiple_of(h * count + b * block, block), block)
                out_ref[pair % 2, :, spot] = low
                part_rows = slice(h * half, (h + 1) * half)
                ctx_t[part_rows, here] = nn(vt[part_rows, base : base + count], low) * inv
                linv_t[part_rows, here] = jnp.broadcast_to(inv, (half, block))

            if h == 0 and pair >= 2:
                for copy in p_copies(p_long, p_short, pl_ref, ps_ref, p_sem, pair - 2):
                    copy.wait()
            looped(0, longest // block, functools.partial(strip, 0, longest, p_long, False))
            poll(1)
            looped(0, short // block, functools.partial(strip, longest, short, p_short, True))
            poll(1)
        context = jnp.transpose(ctx_t[...])
        spot = c * pairs + pair
        ctx32_ref[:, pair * lanes : (pair + 1) * lanes] = context
        ctx_ref[spot] = context.astype(bf16)
        linv_ref[:, pair * lanes : (pair + 1) * lanes] = jnp.transpose(linv_t[...])
        push(ctx_ref.at[spot], ctx_ref.at[spot], ctx_send.at[pair], ctx_recv.at[pair],
             sibling).start()
        for copy in p_copies(p_long, p_short, pl_ref, ps_ref, p_sem, pair):
            copy.start()
        if pair == pairs - 2:
            deals[2].forward()
    poll(len(events))
    deals[2].finish()

    def cot_tile(i):
        rows, chosen = arrive(i)
        cs_ref[rows, :] = nn(chosen, ca[...].reshape(xa_rows, width)).astype(bf16)

    looped(0, rows_all // block, cot_tile)
    for pair in range(pairs):
        spot = c * pairs + pair
        there = (1 - c) * pairs + pair
        push(ctx_ref.at[spot], ctx_ref.at[spot], ctx_send.at[pair], ctx_recv.at[pair],
             sibling).wait_send()
        push(ctx_ref.at[there], ctx_ref.at[there], ctx_send.at[pair], ctx_recv.at[pair],
             sibling).wait_recv()
    for pair in range(max(0, pairs - 2), pairs):
        for copy in p_copies(p_long, p_short, pl_ref, ps_ref, p_sem, pair):
            copy.wait()
    for deal in deals:
        deal.sent()
        deal.passed()
    if gathers:
        rest.finish()


def p_copies(p_long, p_short, pl_ref, ps_ref, sem, pair):
    return [
        pltpu.make_async_copy(p_long.at[pair % 2], pl_ref.at[pair], sem.at[0, pair]),
        pltpu.make_async_copy(p_short.at[pair % 2], ps_ref.at[pair], sem.at[1, pair]),
    ]


def attend(fsdp_count, gathers, bound, idx_col, small, tokens, cotangent, *weights):
    rows = idx_col.shape[0]
    piece, width = tokens.shape[2:]
    part = width // 2
    pairs = part // lanes
    short = rows - longest
    vm = pl.BlockSpec(memory_space=pltpu.VMEM)
    hbm = pl.BlockSpec(memory_space=pl.ANY)
    dma = pltpu.SemaphoreType.DMA
    arrivals = pltpu.VMEM((2, 2, fsdp_count, piece, width), bf16)
    full = [jax.ShapeDtypeStruct((w.shape[0] * fsdp_count, w.shape[1]), bf16) for w in weights]
    out_shape = [
        jax.ShapeDtypeStruct((rows, width), bf16),
        jax.ShapeDtypeStruct((rows, width), bf16),
        jax.ShapeDtypeStruct((rows, 3 * part), bf16),
        jax.ShapeDtypeStruct((pairs, longest, 2 * longest), bf16),
        jax.ShapeDtypeStruct((pairs, short, 2 * short), bf16),
        jax.ShapeDtypeStruct((2 * pairs, rows, lanes), bf16),
        jax.ShapeDtypeStruct((rows, part), f32),
        jax.ShapeDtypeStruct((rows, part), f32),
        jax.ShapeDtypeStruct((8, width), f32),
        jax.ShapeDtypeStruct((width, 3 * part), bf16),
    ]
    out_specs = [vm, vm, vm, hbm, hbm, vm, vm, vm, vm, vm]
    scratch = [
        pltpu.VMEM((2, 2, fsdp_count, 8, lanes), f32),
        arrivals, arrivals,
        pltpu.VMEM((2, longest, 2 * longest), bf16),
        pltpu.VMEM((2, short, 2 * short), bf16),
        pltpu.VMEM((reach, block), f32),
        pltpu.VMEM((short, short), f32),
        pltpu.VMEM((2 * pairs, 3 * lanes, lanes), f32),
        pltpu.VMEM((rows, lanes), bf16),
        pltpu.VMEM((lanes, rows), bf16),
        pltpu.VMEM((lanes, rows), f32),
        pltpu.VMEM((lanes, rows), f32),
        dma((3, 2 * fsdp_count)), dma((3, 2 * fsdp_count)), dma((3, 2 * fsdp_count)),
        dma((3, 2 * fsdp_count)), dma((4,)), dma((pairs,)), dma((pairs,)), dma((2, pairs)),
    ]
    if gathers:
        out_shape += full[1:]
        out_specs += [hbm] * 3
        scratch += [
            dma((1, 3, fsdp_count, 4)), dma((1, fsdp_count, 4)), dma((1,)),
            dma((3, 3, fsdp_count, 4)), dma((3, fsdp_count, 4)), dma((3,)),
        ]
    return pl.pallas_call(
        functools.partial(attend_kernel, fsdp_count, gathers),
        in_specs=[pl.BlockSpec(memory_space=pltpu.SMEM), vm, vm, hbm, hbm] + [hbm] * len(weights),
        out_specs=tuple(out_specs),
        out_shape=tuple(out_shape),
        scratch_shapes=scratch,
        compiler_params=pltpu.CompilerParams(
            vmem_limit_bytes=vmem_limit, collective_id=0, has_side_effects=True),
        name="attend",
    )(bound, idx_col, small, tokens, cotangent, *weights)


def feed_kernel(
    ctx_ref, ctx32_ref, linv_ref, xs_ref, cs_ref, wo_ref, gains_ref, wgu_ref, wd_ref,
    out_ref, ggu_ref, gd_ref, datt_ref, dos_ref, go_ref, ggain_ref,
    mid, nff, hid, dgu, dn, dn_sib, send, recv,
):
    rows_all, width = xs_ref.shape
    ff = wd_ref.shape[0]
    part = width // 2
    lift = math.sqrt(2 / math.pi)
    tiles = rows_all // block
    f, p, c = place()
    sibling = device(f, p, 1 - c)
    gain = gains_ref[1:2, :]
    half_cols = pl.ds(pl.multiple_of(c * part, lanes), part)
    barrier = pltpu.get_barrier_semaphore()
    signal(barrier, sibling)
    pl.semaphore_wait(barrier, 1)

    def exchange(i):
        rows = pl.ds(pl.multiple_of(i * block, block), block)
        return pltpu.make_async_remote_copy(
            src_ref=dn.at[rows, :], dst_ref=dn_sib.at[rows, :], send_sem=send.at[i],
            recv_sem=recv.at[i], device_id=sibling, device_id_type=MESH)

    def tile(i, carry):
        rows = pl.ds(pl.multiple_of(i * block, block), block)
        mixed = jnp.concatenate([ctx_ref[n, rows, :] for n in range(ctx_ref.shape[0])], axis=1)
        middle = xs_ref[rows, :].astype(f32) + nn(mixed, wo_ref[...])
        mid[rows, :] = middle
        normed = (middle * inverse_rms(middle) * gain).astype(bf16)
        nff[rows, :] = normed
        upstream = cs_ref[rows, :]
        gate = nn(normed, wgu_ref[:, :ff])
        up = nn(normed, wgu_ref[:, ff:])
        d_hidden = nt(upstream, wd_ref[...])
        square = gate * gate
        bent = jnp.tanh(lift * gate * (1.0 + 0.044715 * square))
        halved = 0.5 * (1.0 + bent)
        gelu = gate * halved
        slope = halved + 0.5 * gate * (1.0 - bent * bent) * (
            lift * (1.0 + 3 * 0.044715 * square))
        hidden = (gelu * up).astype(bf16)
        hid[rows, :] = hidden
        d_gate = (d_hidden * up * slope).astype(bf16)
        d_up = (d_hidden * gelu).astype(bf16)
        dgu[rows, :ff] = d_gate
        dgu[rows, ff:] = d_up
        dn[rows, :] = (nt(d_gate, wgu_ref[:, :ff]) + nt(d_up, wgu_ref[:, ff:])).astype(bf16)
        exchange(i).start()
        out_ref[rows, :] = (0.5 * middle + nn(hidden, wd_ref[...])).astype(bf16)
        return carry

    lax.fori_loop(0, tiles, tile, 0)

    def down(i, carry):
        cols = pl.ds(pl.multiple_of(i * block, block), block)
        gd_ref[cols, :] = tn(hid[:, cols], cs_ref[...]).astype(bf16)
        return carry

    lax.fori_loop(0, ff // block, down, 0)

    def settle(i, total):
        rows = pl.ds(pl.multiple_of(i * block, block), block)
        exchange(i).wait()
        mine = dn[rows, :].astype(f32)
        grad = mine + dn_sib[rows, :].astype(f32)
        middle = mid[rows, :]
        s = inverse_rms(middle)
        unit = middle * s
        scaled = gain * grad
        d_middle = cs_ref[rows, :].astype(f32) + s * (
            scaled - unit * jnp.mean(scaled * unit, axis=-1, keepdims=True))
        low = d_middle.astype(bf16)
        datt_ref[rows, :] = low
        d_context = nt(low, wo_ref[half_cols, :]).astype(bf16).astype(f32)
        scaled = (d_context * linv_ref[rows, :]).astype(bf16).astype(f32)
        against = scaled * ctx32_ref[rows, :]
        lane = iota((block, lanes), 1)
        for n in range(dos_ref.shape[0]):
            cols = slice((n // 2) * lanes, (n // 2 + 1) * lanes)
            mine_lanes = (lane < lanes // 2) == (n % 2 == 0)
            spare = lanes // 2 if n % 2 == 0 else 0
            delta = jnp.sum(jnp.where(mine_lanes, against[:, cols], 0.0), axis=1, keepdims=True)
            high = delta.astype(bf16).astype(f32)
            extra = jnp.where(lane == spare, -high,
                              jnp.where(lane == spare + 1, high - delta, 0.0))
            dos_ref[n, rows, :] = jnp.where(mine_lanes, scaled[:, cols], extra).astype(bf16)
        return total + jnp.sum(mine * unit, axis=0, keepdims=True)

    ggain_ref[...] = lax.fori_loop(0, tiles, settle, jnp.zeros((1, width), f32))
    for n in range(0, ctx_ref.shape[0], 2):
        mixed = jnp.concatenate((ctx_ref[n], ctx_ref[n + 1]), axis=1)
        go_ref[n * lanes : (n + 2) * lanes, :] = tn(mixed, datt_ref[:, half_cols]).astype(bf16)

    def gate_up(i, carry):
        cols = pl.ds(pl.multiple_of(i * block, block), block)
        ggu_ref[cols, :] = tn(nff[:, cols], dgu[...]).astype(bf16)
        return carry

    lax.fori_loop(0, width // block, gate_up, 0)


def feed(ctx, ctx32, linv, xs, cs, w_out, gains, w_gu, w_down):
    rows, width = xs.shape
    ff = w_down.shape[0]
    part = width // 2
    vm = pl.BlockSpec(memory_space=pltpu.VMEM)
    return pl.pallas_call(
        feed_kernel,
        in_specs=[vm] * 9,
        out_specs=(vm,) * 7,
        out_shape=(
            jax.ShapeDtypeStruct((rows, width), bf16),
            jax.ShapeDtypeStruct((width, 2 * ff), bf16),
            jax.ShapeDtypeStruct((ff, width), bf16),
            jax.ShapeDtypeStruct((rows, width), bf16),
            jax.ShapeDtypeStruct((ctx.shape[0], rows, lanes), bf16),
            jax.ShapeDtypeStruct((width, part), bf16),
            jax.ShapeDtypeStruct((1, width), f32),
        ),
        scratch_shapes=[
            pltpu.VMEM((rows, width), f32),
            pltpu.VMEM((rows, width), bf16),
            pltpu.VMEM((rows, ff), bf16),
            pltpu.VMEM((rows, 2 * ff), bf16),
            pltpu.VMEM((rows, width), bf16),
            pltpu.VMEM((rows, width), bf16),
            pltpu.SemaphoreType.DMA((rows // block,)),
            pltpu.SemaphoreType.DMA((rows // block,)),
        ],
        compiler_params=pltpu.CompilerParams(
            vmem_limit_bytes=vmem_limit, collective_id=2, has_side_effects=True),
        name="feed",
    )(ctx, ctx32, linv, xs, cs, w_out, gains, w_gu, w_down)


class Scattering:
    def __init__(self, fsdp_count, grads, in_y, in_x, turned, in_z, final, send, recv):
        self.f, self.y, self.c = place()
        self.count = fsdp_count
        self.planes = fsdp_count // 2
        self.z, self.x = self.f // 2, self.f % 2
        self.grads, self.in_y, self.in_x = grads, in_y, in_x
        self.turned, self.in_z, self.final = turned, in_z, final
        self.send, self.recv = send, recv
        self.x_side = device(self.z * 2 + 1 - self.x, self.y, self.c)
        self.y_side = device(self.f, 1 - self.y, self.c)
        self.sibling = device(self.f, self.y, 1 - self.c)

    def part(self, n, f, k):
        return self.grads[n].at[f * 4 + k]

    def plane(self, j):
        return lax.rem(self.z + j, self.planes)

    def order(self):
        return [*range(1, self.planes), 0]

    def move(self, n, kind, i, j, src, dst, where):
        return push(src, dst, self.send.at[n, kind, i, j], self.recv.at[n, kind, i, j], where)

    def along_y(self, n, z, x):
        return self.move(n, 0, z, x, self.part(n, 2 * z + x, 2 * (1 - self.y)),
                         self.in_y[n].at[z, x], self.y_side)

    def along_x(self, n, z, y):
        return self.move(n, 1, z, y, self.part(n, 2 * z + 1 - self.x, 2 * y + 1),
                         self.in_x[n].at[z, y], self.x_side)

    def turn(self, n, z, side):
        if side == 0:
            return self.move(n, 2, z, 0, self.in_y[n].at[z, 1 - self.x],
                             self.turned[n].at[z, 0], self.x_side)
        return self.move(n, 2, z, 1, self.in_x[n].at[z, 1 - self.y], self.turned[n].at[z, 1],
                         self.y_side)

    def summed(self, n, z, side):
        return (self.in_y[n].at[z, self.x], self.in_x[n].at[z, self.y])[side]

    def out_z(self, n, z, side):
        return push(self.summed(n, z, side), self.in_z[n].at[self.z, side],
                    self.send.at[n, 3, z, side], self.recv.at[n, 3, self.z, side],
                    device(2 * z + self.x, self.y, self.c))

    def come_z(self, n, z, side):
        return push(self.summed(n, z, side), self.in_z[n].at[z, side],
                    self.send.at[n, 3, z, side], self.recv.at[n, 3, z, side],
                    device(2 * z + self.x, self.y, self.c))

    def last_y(self, n, side, mine):
        y = self.y if mine else 1 - self.y
        here = self.final[n].at[self.c, 2 * y + side]
        return self.move(n, 4, 0, side, here, here, self.y_side)

    def last_core(self, n, mine):
        here = self.final[n].at[self.c if mine else 1 - self.c]
        return self.move(n, 5, 0, 0, here, here, self.sibling)

    def each(self, body):
        for n in range(len(self.grads)):
            body(n)

    def start(self):
        for j in self.order():
            z = self.plane(j)
            for n in range(len(self.grads)):
                for k in range(2):
                    self.along_y(n, z, k).start()
                    self.along_x(n, z, k).start()

    def fold(self, j):
        z = self.plane(j)
        for n in range(len(self.grads)):
            for k in range(2):
                self.along_y(n, z, k).wait_recv()
                add_to(self.in_y[n].at[z, k], self.part(n, 2 * z + k, 2 * self.y))
            self.turn(n, z, 0).start()
            for k in range(2):
                self.along_x(n, z, k).wait_recv()
                add_to(self.in_x[n].at[z, k], self.part(n, 2 * z + self.x, 2 * k + 1))
            self.turn(n, z, 1).start()

    def plane_sum(self, j):
        z = self.plane(j)
        for n in range(len(self.grads)):
            for side in range(2):
                self.turn(n, z, side).wait_recv()
                add_to(self.summed(n, z, side), self.turned[n].at[z, side])
                if j:
                    self.out_z(n, z, side).start()

    def total(self):
        for n in range(len(self.grads)):
            for side in range(2):
                value = self.summed(n, self.z, side)[...].astype(f32)
                for j in range(1, self.planes):
                    z = self.plane(j)
                    self.come_z(n, z, side).wait_recv()
                    value = value + self.in_z[n][z, side].astype(f32)
                self.final[n][self.c, 2 * self.y + side] = value.astype(bf16)
                self.last_y(n, side, True).start()

    def share(self):
        for n in range(len(self.grads)):
            for side in range(2):
                self.last_y(n, side, False).wait_recv()
            self.last_core(n, True).start()

    def finish(self):
        for n in range(len(self.grads)):
            self.last_core(n, False).wait_recv()
            self.last_core(n, True).wait_send()
            for side in range(2):
                self.last_y(n, side, True).wait_send()
            for j in range(self.planes):
                z = self.plane(j)
                for k in range(2):
                    self.along_y(n, z, k).wait_send()
                    self.along_x(n, z, k).wait_send()
                    self.turn(n, z, k).wait_send()
                    if j:
                        self.out_z(n, z, k).wait_send()

    def events(self):
        order = self.order()
        out = [functools.partial(self.fold, order[0])]
        for before, j in zip(order, order[1:]):
            out += [functools.partial(self.fold, j), functools.partial(self.plane_sum, before)]
        return out + [functools.partial(self.plane_sum, order[-1]), self.total, self.share]


def add_to(here, other):
    here[...] = (here[...].astype(f32) + other[...].astype(f32)).astype(bf16)


class Homing:
    def __init__(self, fsdp_count, src, dst, send, recv, own):
        self.f, self.p, self.c = place()
        self.count = fsdp_count
        self.src, self.dst, self.send, self.recv, self.own = src, dst, send, recv, own

    def out(self, q, g):
        return push(self.src.at[q, g], self.dst.at[self.p, self.f], self.send.at[q, g],
                    self.recv.at[self.p, self.f], device(g, q, self.c))

    def come(self, q, g):
        return push(self.src.at[q, g], self.dst.at[q, g], self.send.at[q, g],
                    self.recv.at[q, g], device(g, q, self.c))

    def local(self):
        return pltpu.make_async_copy(self.src.at[self.p, self.f], self.dst.at[self.p, self.f],
                                     self.own)

    def start(self, q):
        for i in range(1, self.count):
            self.out(q, lax.rem(self.f + i, self.count)).start()

    def start_other(self):
        self.out(1 - self.p, self.f).start()
        self.local().start()

    def finish(self):
        self.local().wait()
        self.come(1 - self.p, self.f).wait_recv()
        self.out(1 - self.p, self.f).wait_send()
        for q in range(2):

            def one(i, q=q):
                g = lax.rem(self.f + i, self.count)
                self.come(q, g).wait_recv()
                self.out(q, g).wait_send()

            looped(1, self.count, one)


def back_kernel(
    fsdp_count, scatters, idx_ref, xs_ref, gains_ref, ggain_ref, w_ref, dos_ref, qkv_ref, datt_ref,
    out_ref, pl_ref, ps_ref, *refs,
):
    if scatters:
        grads = refs[:3]
        refs = refs[3:]
    output_ref, tokens_ref, small_ref, *refs = refs
    if scatters:
        outs, refs = refs[:7], refs[7:]
        gqkv_refs, refs = refs[:3], refs[3:]
    else:
        gqkv_refs, refs = refs[:3], refs[3:]
    (ybuf, normed, dqkv, table, qs, ds_l, ds_s, p_l, p_s, acc, va, kt, dq_t, given, taken,
     smalls, load, p_sem, pass_send, pass_recv, home_send, home_recv, own,
     small_send, small_recv, small_pass, small_back, *refs) = refs
    f, p, c = place()
    sibling = device(f, p, 1 - c)
    rows_all, width = xs_ref.shape
    part = width // 2
    pairs = part // lanes
    short = rows_all - longest
    half = lanes // 2
    gain_attn = gains_ref[0:1, :]
    tile_rows = taken.shape[2] * taken.shape[3]

    loading = pltpu.make_async_copy(out_ref, ybuf, load)
    loading.start()

    def p_copies(head):
        pair, h = head // 2, head % 2
        return [
            pltpu.make_async_copy(pl_ref.at[pair, :, h * longest : (h + 1) * longest],
                                  p_l.at[h], p_sem.at[0, h]),
            pltpu.make_async_copy(ps_ref.at[pair, :, h * short : (h + 1) * short],
                                  p_s.at[h], p_sem.at[1, h]),
        ]

    for head in range(2):
        for copy in p_copies(head):
            copy.start()
    greet_all(fsdp_count)
    sets = []
    if scatters:
        for group in range(1 + pairs):
            arrays = grads if group == 0 else (gqkv_refs[group - 1],)
            count = len(arrays)
            bufs = [refs[k * count : (k + 1) * count] for k in range(5)]
            send, recv = refs[5 * count : 5 * count + 2]
            refs = refs[5 * count + 2 :]
            sets.append(Scattering(fsdp_count, arrays, *bufs, send, recv))
        sets[0].start()
    events = sets[0].events() if scatters else []

    def poll(count):
        for _ in range(count):
            if events:
                events.pop(0)()

    def unslot(side, q):
        first = (side * 2 + q) * tile_rows
        chosen = one_hot(iota((tile_rows, rows_all), 0) + first, idx_ref[...])
        return nn(chosen, ybuf[...])

    def pass_over(which, q):
        return push(given.at[q], taken.at[which, q], pass_send.at[which, q],
                    pass_recv.at[which, q], sibling)

    homes = [
        Homing(fsdp_count, taken.at[n], dst, home_send.at[n], home_recv.at[n], own.at[n])
        for n, dst in enumerate((output_ref, tokens_ref))
    ]

    def give(which):
        for q in range(2):
            given[q] = unslot(1 - c, q).astype(bf16).reshape(given.shape[1:])
            pass_over(which, q).start()

    def keep(which):
        for q in range(2):
            pass_over(which, q).wait_recv()
            value = unslot(c, q) + taken[which, q].reshape(tile_rows, width).astype(f32)
            taken[which, q] = value.astype(bf16).reshape(taken.shape[2:])
            homes[which].start(q)
        homes[which].start_other()
        for q in range(2):
            pass_over(which, q).wait_send()

    loading.wait()
    give(0)

    def norm_tile(i):
        rows = pl.ds(pl.multiple_of(i * block, block), block)
        x = xs_ref[rows, :].astype(f32)
        normed[rows, :] = (x * inverse_rms(x) * gain_attn).astype(bf16)

    looped(0, rows_all // block, norm_tile)
    keep(0)

    lane = iota((rows_all, lanes), 1)
    buckets = band_buckets()
    small_ref_rows = iota((lanes // 4, lanes), 1)
    bias = jnp.zeros((lanes // 4, lanes), f32)
    for pair in range(pairs):
        cols = [slice(kind * part + pair * lanes, kind * part + (pair + 1) * lanes)
                for kind in range(3)]
        queries = qkv_ref[:, cols[0]]
        keys = qkv_ref[:, cols[1]]
        values = qkv_ref[:, cols[2]]
        kt[...] = jnp.transpose(keys.astype(f32)).astype(bf16)
        for h in range(2):
            head = 2 * pair + h
            own_lanes = (lane < half) == (h == 0)
            spare = half if h == 0 else 0
            qs[...] = jnp.where(own_lanes, queries, jnp.zeros_like(queries))
            ones = jnp.where((lane == spare) | (lane == spare + 1), 1.0, 0.0)
            va[...] = jnp.where(own_lanes, values.astype(f32), ones).astype(bf16)
            table[...] = jnp.zeros_like(table)
            for copy in p_copies(head):
                copy.wait()

            def strip(base, count, p_buf, ds_buf, b):
                here = pl.ds(pl.multiple_of(base + b * block, block), block)
                spot = pl.ds(pl.multiple_of(b * block, block), block)
                d_weights = nt(va[base : base + count, :], dos_ref[head, here, :])
                d_logits = p_buf[h, :, spot].astype(f32) * d_weights
                window = pl.ds(pl.multiple_of(far - b * block, block), count)
                table[window, :] = table[window, :] + d_logits
                low = d_logits.astype(bf16)
                ds_buf[:, spot] = low
                part_rows = slice(h * half, (h + 1) * half)
                dq_t[part_rows, here] = nn(kt[part_rows, base : base + count], low)

            looped(0, longest // block, functools.partial(strip, 0, longest, p_l, ds_l))
            poll(1)
            looped(0, short // block, functools.partial(strip, longest, short, p_s, ds_s))
            for base, count, p_buf, ds_buf in ((0, longest, p_l, ds_l), (longest, short, p_s, ds_s)):
                rows = slice(base, base + count)
                clean = jnp.where(own_lanes[rows], dos_ref[head, rows, :].astype(f32), 0.0)
                d_value = nn(p_buf[h], clean.astype(bf16))
                d_key = nn(ds_buf[...], qs[rows, :])
                if h == 0:
                    acc[0, rows, :] = d_value
                    acc[1, rows, :] = d_key
                else:
                    dqkv[rows, cols[2]] = (acc[0, rows, :] + d_value).astype(bf16)
                    dqkv[rows, cols[1]] = (acc[1, rows, :] + d_key).astype(bf16)
            if head + 2 < 2 * pairs:
                for copy in p_copies(head + 2):
                    copy.start()
            before = far - lanes
            after = far + 3 * lanes
            band = table[before : before + 3 * lanes, :lanes] + table[far : far + 3 * lanes, lanes:]
            left = jnp.sum(table[:before, :lanes] + table[:before, lanes:], axis=0, keepdims=True)
            left = left + jnp.sum(table[before:far, lanes:], axis=0, keepdims=True)
            right = jnp.sum(table[after:, :lanes] + table[after:, lanes:], axis=0, keepdims=True)
            right = right + jnp.sum(table[after - lanes : after, :lanes], axis=0, keepdims=True)
            for label in range(lanes // 4):
                line = jnp.sum(jnp.where(buckets == label, band, 0.0), axis=0, keepdims=True)
                if label == 15:
                    line = line + left
                if label == 31:
                    line = line + right
                table[label : label + 1, :lanes] = line
            sums = jnp.sum(table[: lanes // 4, :lanes], axis=1, keepdims=True)
            bias = bias + jnp.where(small_ref_rows == c * 2 * pairs + head, sums, 0.0)
            poll(1)
        dqkv[:, cols[0]] = jnp.transpose(dq_t[...]).astype(bf16)
        for kind in range(3):
            grad = tn(normed[...], dqkv[:, cols[kind]])
            grad = grad.reshape(*gqkv_refs[pair].shape[:-1], lanes)
            gqkv_refs[pair][..., kind * lanes : (kind + 1) * lanes] = grad.astype(bf16)
        if pair == pairs - 1:
            reload = pltpu.make_async_copy(datt_ref, normed, load)
            reload.start()
        if scatters:
            sets[1 + pair].start()
            events += sets[1 + pair].events()

    def tile(i, total):
        rows = slice(i * block, (i + 1) * block)
        x = xs_ref[rows, :].astype(f32)
        s = inverse_rms(x)
        unit = x * s
        grad = nt(dqkv[rows, :], w_ref[...])
        scaled = gain_attn * grad
        y = 0.5 * normed[rows, :].astype(f32) + s * (
            scaled - unit * jnp.mean(scaled * unit, axis=-1, keepdims=True))
        ybuf[rows, :] = y.astype(bf16)
        return total + jnp.sum(grad * unit, axis=0, keepdims=True)

    grad_gain = jnp.zeros((1, width), f32)
    reload.wait()
    for i in range(rows_all // block):
        grad_gain = tile(i, grad_gain)
    give(1)
    quarter = lanes // 4
    small_ref[0:quarter, :] = bias
    small_ref[quarter:, :] = jnp.zeros((small_ref.shape[0] - quarter, lanes), f32)
    for j in range(width // lanes):
        cols = slice(j * lanes, (j + 1) * lanes)
        small_ref[quarter + j : quarter + j + 1, :] = grad_gain[:, cols]
        row = quarter + 8 + j
        small_ref[row : row + 1, :] = ggain_ref[:, cols]
    dealt = Dealing(fsdp_count, small_ref, smalls, small_send, small_recv, small_pass, small_back,
                    own.at[2])
    dealt.start()
    keep(1)
    poll(len(events))
    dealt.forward()
    dealt.finish()
    dealt.sent()
    dealt.passed()

    def gather_small(k, total):
        return total + smalls[k // (2 * fsdp_count), (k // fsdp_count) % 2, k % fsdp_count]

    small_ref[...] = lax.fori_loop(0, 4 * fsdp_count, gather_small,
                                   jnp.zeros(small_ref.shape, f32))
    for group in sets:
        group.finish()
    if scatters:
        gate, up, down, out_w, query, key, value = outs
        gu, dn, wo = sets[0].final
        ff = gu.shape[3] // 2
        cut = ff // fsdp_count
        for k in range(4):
            for side in range(2):
                rows = gu.shape[2]
                rows = slice(k * rows, (k + 1) * rows)
                for g in range(fsdp_count):
                    there = slice((2 * g + side) * cut, (2 * g + side + 1) * cut)
                    gate[rows, there] = gu[side, k, :, g * cut : (g + 1) * cut].astype(f32)
                    up[rows, there] = gu[side, k, :, ff + g * cut : ff + (g + 1) * cut].astype(f32)
                many = dn.shape[2]
                first = (side * 4 + k) * many
                down[first : first + many, :] = dn[side, k].astype(f32)
                out_w[rows, side * part : (side + 1) * part] = wo[side, k].astype(f32)
                for pair in range(pairs):
                    [one] = sets[1 + pair].final
                    there = slice(side * part + pair * lanes, side * part + (pair + 1) * lanes)
                    for kind, ref in enumerate((query, key, value)):
                        ref[rows, there] = one[side, k, :, kind * lanes : (kind + 1) * lanes].astype(
                            f32)
    for home in homes:
        home.finish()


def back(fsdp_count, piece, scatters, idx_row, xs, gains, ggain, w_qkv, datt, dos, qkv, out,
         p_long, p_short, grads):
    rows, width = xs.shape
    part = width // 2
    pairs = part // lanes
    short = rows - longest
    vm = pl.BlockSpec(memory_space=pltpu.VMEM)
    hbm = pl.BlockSpec(memory_space=pl.ANY)
    dma = pltpu.SemaphoreType.DMA
    shape = (2, fsdp_count, piece, width)
    own_rows = width // fsdp_count
    out_shape = [
        jax.ShapeDtypeStruct(shape, bf16), jax.ShapeDtypeStruct(shape, bf16),
        jax.ShapeDtypeStruct((48, lanes), f32),
    ]
    out_specs = [hbm, hbm, vm]
    if scatters:
        ff = grads[0].shape[1]
        out_shape += [jax.ShapeDtypeStruct((own_rows, ff), f32)] * 2
        out_shape += [jax.ShapeDtypeStruct((2 * grads[1].shape[0] // fsdp_count, width), f32)]
        out_shape += [jax.ShapeDtypeStruct((own_rows, width), f32)] * 4
        out_specs += [vm] * 7
    gqkv = [jax.ShapeDtypeStruct((width, 3 * lanes), bf16)] * pairs
    scratch = []
    if scatters:
        grads = tuple(g.reshape(4 * fsdp_count, -1, g.shape[1]) for g in grads)
        scratch = [pltpu.VMEM((4 * fsdp_count, own_rows // 4, 3 * lanes), bf16)] * pairs
    if not scatters:
        out_shape += gqkv
        out_specs += [vm] * pairs
    scratch += [
        pltpu.VMEM((rows, width), bf16),
        pltpu.VMEM((rows, width), bf16),
        pltpu.VMEM((rows, 3 * part), bf16),
        pltpu.VMEM((reach, block), f32),
        pltpu.VMEM((rows, lanes), bf16),
        pltpu.VMEM((longest, longest), bf16),
        pltpu.VMEM((short, short), bf16),
        pltpu.VMEM((2, longest, longest), bf16),
        pltpu.VMEM((2, short, short), bf16),
        pltpu.VMEM((2, rows, lanes), f32),
        pltpu.VMEM((rows, lanes), bf16),
        pltpu.VMEM((lanes, rows), bf16),
        pltpu.VMEM((lanes, rows), f32),
        pltpu.VMEM(shape, bf16),
        pltpu.VMEM((2, *shape), bf16),
        pltpu.VMEM((2, 2, fsdp_count, 48, lanes), f32),
        dma, dma((2, 2)), dma((2, 2)), dma((2, 2)),
        dma((2, 2, fsdp_count)), dma((2, 2, fsdp_count)), dma((3,)),
        *[dma((2 * fsdp_count,))] * 4,
    ]
    if scatters:
        planes = fsdp_count // 2
        for quarters in ([g.shape[1:] for g in grads], *[[(own_rows // 4, 3 * lanes)]] * pairs):
            for lead in ((planes, 2), (planes, 2), (planes, 2), (planes, 2), (2, 4)):
                scratch += [pltpu.VMEM((*lead, *q), bf16) for q in quarters]
            scratch += [dma((len(quarters), 6, planes, 2))] * 2
    return pl.pallas_call(
        functools.partial(back_kernel, fsdp_count, scatters),
        in_specs=[vm] * 7 + [hbm] * 4 + [vm] * (len(grads) if scatters else 0),
        out_specs=tuple(out_specs),
        out_shape=tuple(out_shape),
        scratch_shapes=scratch,
        compiler_params=pltpu.CompilerParams(
            vmem_limit_bytes=vmem_limit, collective_id=1, has_side_effects=True),
        name="back",
    )(idx_row, xs, gains, ggain, w_qkv, dos, qkv, datt, out, p_long, p_short,
      *(grads if scatters else ()))


def shards(
    tokens, cotangent, lengths, dealing, gain_attn, w_query, w_key, w_value, w_out, bias_table,
    gain_ff, w_gate, w_up, w_down,
):
    fsdp_count = lax.axis_size("fsdp")
    sp_count = lax.axis_size("sp")
    micro_count, token_rows, width = tokens.shape
    piece = token_rows // fsdp_count
    group_rows = token_rows * sp_count
    local_heads = bias_table.shape[1]
    heads = local_heads * sp_count
    part = width // 2
    s = lax.axis_index("sp")
    p, c = s // 2, s % 2
    full_piece = -(-piece // 8) * 8

    def pieces(value):
        value = value.reshape(micro_count, fsdp_count, piece, width)
        return jnp.pad(value, ((0, 0), (0, 0), (0, full_piece - piece), (0, 0)))

    order = lax.dynamic_index_in_dim(dealing[:, 0], p, 0, keepdims=False)
    length = lax.dynamic_index_in_dim(lengths[:, 0], p, 0, keepdims=False)
    first_long = length[0] == longest
    start = jnp.where(first_long, 0, jnp.where(length[1] == longest, length[0],
                                               length[0] + length[1]))
    bound = jnp.where(first_long, length[1], length[0]).reshape(1)
    short = group_rows - longest
    head_part = lax.dynamic_slice_in_dim(order, start, longest, 0)
    tail = jnp.where(jnp.arange(short) < start, order[:short], order[longest:])
    order = jnp.concatenate((head_part, tail))
    source, within = order // token_rows, order % token_rows
    idx = ((source % 2) * 2 + source // 2) * fsdp_count + within // piece
    idx = idx * full_piece + within % piece

    def half_cols(weight):
        return lax.dynamic_slice_in_dim(weight, c * part, part, 1)

    def half_ff(weight):
        split = weight.reshape(weight.shape[0], fsdp_count, 2, -1)
        return lax.dynamic_index_in_dim(split, c, 2, keepdims=False).reshape(weight.shape[0], -1)

    def gather(value, axis=0):
        return lax.all_gather(value, "fsdp", axis=axis, tiled=True)

    def line(value):
        return jnp.pad(value.astype(f32), ((0, 0), (0, lanes - value.shape[1])))

    small = jnp.concatenate([line(gain_attn[None]), line(gain_ff[None]), line(bias_table.T)])
    small = jnp.pad(small, ((0, 8 - small.shape[0]), (0, 0)))
    down_rows = w_down.shape[0] // 2
    weights = (
        jnp.concatenate([half_cols(w) for w in (w_query, w_key, w_value)], axis=1),
        w_out,
        jnp.concatenate([half_ff(w) for w in (w_gate, w_up)], axis=1),
        lax.dynamic_slice_in_dim(w_down, c * down_rows, down_rows, 0),
    )
    gathers = all(w.shape[0] % 32 == 0 for w in weights)
    if not gathers:
        weights = tuple(gather(w) for w in weights)
    args = (bound, idx.reshape(-1, 1), small, pieces(tokens), pieces(cotangent))
    xs, cs, qkv, p_long, p_short, ctx, ctx32, linv, gains, w_qkv, *late = attend(
        fsdp_count, gathers, *args, *(weights if gathers else weights[:1]))
    wo, w_gu, wd = late if gathers else weights[1:]
    buckets = band_buckets()
    out_part, grad_gu, grad_d, datt, dos, grad_o, grad_gain_ff = feed(
        ctx, ctx32, linv, xs, cs, wo, gains, w_gu, wd)
    output, grad_tokens, small, *grads = back(
        fsdp_count, full_piece, gathers, idx.reshape(1, -1), xs, gains, grad_gain_ff, w_qkv, datt,
        dos, qkv, out_part, p_long, p_short, (grad_gu, grad_d, grad_o))
    output, grad_tokens = (x[:, :, :piece].reshape(tokens.shape) for x in (output, grad_tokens))
    own_gain = width // fsdp_count
    f = lax.axis_index("fsdp")
    labels = bias_table.shape[0]
    bias_grad = lax.dynamic_slice_in_dim(small[:labels], s * local_heads, local_heads, 1)
    gain_grads = [
        lax.dynamic_slice_in_dim(
            small[first : first + width // lanes].reshape(-1), f * own_gain, own_gain, 0)
        for first in (labels, labels + 8)
    ]
    if not gathers:
        grads = scatter_rows(fsdp_count, c, (grad_gu, grad_d, grad_o, *grads))
    grad_gate, grad_up, grad_down, grad_out, grad_query, grad_key, grad_value = grads
    return (
        output, grad_tokens, gain_grads[0], grad_query, grad_key, grad_value, grad_out, bias_grad,
        gain_grads[1], grad_gate, grad_up, grad_down,
    )


def scatter_rows(fsdp_count, c, partial_grads):
    sibling = [(0, 1), (1, 0), (2, 3), (3, 2)]
    across = [(0, 2), (2, 0), (1, 3), (3, 1)]
    shares = [lax.psum_scatter(v, "fsdp", scatter_dimension=0, tiled=True) for v in partial_grads]
    shares = [v.astype(f32) + lax.ppermute(v, "sp", across).astype(f32) for v in shares]
    shares = [v.astype(bf16) for v in shares]
    others = [lax.ppermute(v, "sp", sibling) for v in shares]
    sides = [
        (jnp.where(c == 0, v, w).astype(f32), jnp.where(c == 0, w, v).astype(f32))
        for v, w in zip(shares, others)
    ]
    gu, down, out, *qkv = sides
    rows = gu[0].shape[0]
    ff = gu[0].shape[1] // 2

    def ff_cols(which):
        cut = [x[:, which * ff : (which + 1) * ff].reshape(rows, fsdp_count, 1, -1) for x in gu]
        return jnp.concatenate(cut, axis=2).reshape(rows, -1)

    def proj(kind):
        return jnp.concatenate(
            [pair[side][:, kind * lanes : (kind + 1) * lanes] for side in range(2) for pair in qkv],
            axis=1)

    return (ff_cols(0), ff_cols(1), jnp.concatenate(down), jnp.concatenate(out, axis=1),
            proj(0), proj(1), proj(2))


def solution(mesh):
    return jax.shard_map(
        shards,
        mesh=mesh,
        in_specs=(
            P(None, ("fsdp", "sp"), None), P(None, ("fsdp", "sp"), None),
            P(None, "fsdp", None), P(None, "fsdp", None),
            P("fsdp"), P("fsdp", None), P("fsdp", None), P("fsdp", None), P("fsdp", None),
            P(None, "sp"), P("fsdp"), P("fsdp", None), P("fsdp", None), P("fsdp", None),
        ),
        out_specs=(
            P(None, ("fsdp", "sp"), None), P(None, ("fsdp", "sp"), None),
            P("fsdp"), P("fsdp", None), P("fsdp", None), P("fsdp", None), P("fsdp", None),
            P(None, "sp"), P("fsdp"), P("fsdp", None), P("fsdp", None), P("fsdp", None),
        ),
        check_vma=False,
    )
```

```python
import functools
import math

import jax
import jax.numpy as jnp
from jax import lax
from jax.experimental import pallas as pl
from jax.experimental.pallas import tpu as pltpu
from jax.sharding import PartitionSpec as P

bucket_edges = (1, 2, 3, 4, 5, 6, 7, 8, 12, 16, 23, 32, 46, 64, 91)
epsilon = 1e-06
longest = 1024
lanes = 128
block = 256
far = 768
reach = 1792
MESH = pl.DeviceIdType.MESH
f32 = jnp.float32
bf16 = jnp.bfloat16
vmem_limit = 62 * 2**20


def nn(left, right):
    return jnp.dot(left, right, preferred_element_type=f32)


def nt(left, right):
    return lax.dot_general(left, right, (((1,), (1,)), ((), ())), preferred_element_type=f32)


def tn(left, right):
    return lax.dot_general(left, right, (((0,), (0,)), ((), ())), preferred_element_type=f32)


def iota(shape, dim):
    return lax.broadcasted_iota(jnp.int32, shape, dim)


def one_hot(column, row):
    return jnp.where(column == row, 1.0, 0.0).astype(bf16)


def inverse_rms(values):
    return lax.rsqrt(jnp.mean(values * values, axis=-1, keepdims=True) + epsilon)


def bucket_index(offset):
    distance = jnp.abs(offset)
    bucket_sum = jnp.where(offset > 0, 16, 0).astype(jnp.int32)
    for border in bucket_edges:
        bucket_sum = bucket_sum + (distance >= border).astype(jnp.int32)
    return bucket_sum


def band_buckets():
    shape = (3 * lanes, lanes)
    return bucket_index(iota(shape, 0) - lanes - iota(shape, 1))


def whole_spec(shape, space=pltpu.VMEM):
    return pl.BlockSpec(shape, lambda *_: (0,) * len(shape), memory_space=space,
                        pipeline_mode=pl.Buffered(1))


def place():
    f = lax.axis_index("fsdp")
    s = lax.axis_index("sp")
    return f, s // 2, s % 2


def device(f, p, c):
    return {"fsdp": f, "sp": 2 * p + c}


def signal(barrier, where):
    pl.semaphore_signal(barrier, inc=1, device_id=where, device_id_type=MESH)


def greet_all(fsdp_count):
    f, p, c = place()
    barrier = pltpu.get_barrier_semaphore()
    peers = 2 * fsdp_count
    mine = p * fsdp_count + f

    def greet(i, carry):
        k = lax.rem(mine + i, peers)
        signal(barrier, device(k % fsdp_count, k // fsdp_count, c))
        return carry

    lax.fori_loop(1, peers, greet, 0)
    signal(barrier, device(f, p, 1 - c))
    pl.semaphore_wait(barrier, peers)


def push(src, dst, send, recv, where):
    return pltpu.make_async_remote_copy(
        src_ref=src, dst_ref=dst, send_sem=send, recv_sem=recv, device_id=where,
        device_id_type=MESH)


def looped(first, last, body):
    def step(i, carry):
        body(i)
        return carry

    lax.fori_loop(first, last, step, 0)


class Dealing:
    def __init__(self, fsdp_count, src, dst, send, recv, pass_send, pass_recv, own):
        self.f, self.p, self.c = place()
        self.count = fsdp_count
        self.peers = 2 * fsdp_count
        self.mine = self.p * fsdp_count + self.f
        self.src, self.dst, self.send, self.recv = src, dst, send, recv
        self.pass_send, self.pass_recv, self.own = pass_send, pass_recv, own

    def source(self, k):
        return self.src.at[k // self.count, k % self.count] if len(self.src.shape) == 4 else self.src

    def out(self, k):
        where = device(k % self.count, k // self.count, self.c)
        return push(self.source(k), self.dst.at[self.c, self.p, self.f], self.send.at[k],
                    self.recv.at[self.mine], where)

    def come(self, k):
        where = device(k % self.count, k // self.count, self.c)
        return push(self.source(k), self.dst.at[self.c, k // self.count, k % self.count],
                    self.send.at[k], self.recv.at[k], where)

    def onward(self, k, side):
        here = self.dst.at[side, k // self.count, k % self.count]
        return push(here, here, self.pass_send.at[k], self.pass_recv.at[k],
                    device(self.f, self.p, 1 - self.c))

    def local(self):
        return pltpu.make_async_copy(
            self.source(self.mine), self.dst.at[self.c, self.p, self.f], self.own)

    def start(self):
        looped(1, self.peers, lambda i: self.out(lax.rem(self.mine + i, self.peers)).start())
        self.local().start()

    def forward(self):
        self.local().wait()
        self.onward(self.mine, self.c).start()

        def one(i):
            k = lax.rem(self.mine + self.peers - i, self.peers)
            self.come(k).wait_recv()
            self.onward(k, self.c).start()

        looped(1, self.peers, one)

    def sent(self):
        looped(1, self.peers, lambda i: self.out(lax.rem(self.mine + i, self.peers)).wait_send())

    def finish(self):
        looped(0, self.peers, lambda k: self.onward(k, 1 - self.c).wait_recv())

    def passed(self):
        looped(0, self.peers, lambda k: self.onward(k, self.c).wait_send())


class Gathering:
    def __init__(self, fsdp_count, srcs, dsts, sends, recvs, own):
        self.f, self.y, self.c = place()
        self.count = fsdp_count
        self.planes = fsdp_count // 2
        self.z, self.x = self.f // 2, self.f % 2
        self.srcs, self.dsts, self.sends, self.recvs, self.own = srcs, dsts, sends, recvs, own
        self.x_side = device(self.z * 2 + 1 - self.x, self.y, self.c)
        self.y_side = device(self.f, 1 - self.y, self.c)

    def rows(self, dst, f, k):
        total = dst.shape[0] // self.count
        quarter = total // 4
        return dst.at[pl.ds(pl.multiple_of(f * total + k * quarter, 8), quarter)]

    def copies(self, link, f, k, where, fresh=False):
        out = []
        for n, (src, dst) in enumerate(zip(self.srcs, self.dsts)):
            there = self.rows(dst, f, k)
            quarter = src.shape[0] // 4
            here = src.at[pl.ds(pl.multiple_of(k * quarter, 8), quarter)] if fresh else there
            out.append(push(here, there, self.sends.at[n, link, f, k], self.recvs.at[n, f, k],
                            where))
        return out

    def go(self, *args, **kw):
        for copy in self.copies(*args, **kw):
            copy.start()

    def arrived(self, f, k):
        for copy in self.copies(0, f, k, self.x_side):
            copy.wait_recv()

    def plane(self, j):
        return lax.rem(self.z + j, self.planes)

    def hop(self, z, k, up, fresh=False):
        to = self.z + 1 if up else self.z - 1
        where = device(2 * to + self.x, self.y, self.c)
        return self.copies(0 if up else 3, 2 * z + self.x, k, where, fresh)

    def hops(self, z, up, action, fresh=False):
        @pl.when(self.z + 1 < self.planes if up else self.z > 0)
        def _():
            for side in range(2):
                for copy in self.hop(z, 2 * self.y + side, up, fresh):
                    action(copy)

    def at(self, d, body):
        pl.when(self.z >= d)(lambda: body(self.z - d, True))
        pl.when(self.z + d < self.planes)(lambda: body(self.z + d, False))

    def local(self):
        return [
            pltpu.make_async_copy(
                src, dst.at[pl.ds(pl.multiple_of(self.f * src.shape[0], 8), src.shape[0])],
                self.own.at[n])
            for n, (src, dst) in enumerate(zip(self.srcs, self.dsts))
        ]

    def start_x(self):
        for copy in self.local():
            copy.start()
        for k in (2 * self.y, 2 * self.y + 1, 2 * (1 - self.y) + 1):
            self.go(1, self.f, k, self.x_side, fresh=True)

    def start_z(self):
        for up in (True, False):
            self.hops(self.z, up, lambda copy: copy.start(), fresh=True)

    def spread(self, d):
        def one(z, up):
            f = 2 * z + self.x
            for side in range(2):
                self.arrived(f, 2 * self.y + side)
            self.hops(z, up, lambda copy: copy.start())
            for side in range(2):
                k = 2 * self.y + side
                self.go(1, f, k, self.x_side)
                self.go(2, f, k, self.y_side)

        self.at(d, one)

    def turn(self, d):
        def one(z, up):
            f = 2 * z + 1 - self.x
            self.arrived(f, 2 * self.y)
            self.go(2, f, 2 * self.y, self.y_side)
            if d:
                f = 2 * z + self.x
                k = 2 * (1 - self.y) + 1
                self.arrived(f, k)
                self.go(1, f, k, self.x_side)

        if d:
            self.at(d, one)
        else:
            one(self.z, True)

    def finish(self):
        x, y = self.x, self.y
        for copy in self.local():
            copy.wait()

        def one(j):
            other = 2 * self.plane(j) + 1 - x
            self.arrived(other, 2 * y + 1)
            self.arrived(other, 2 * (1 - y) + 1)
            self.arrived(other, 2 * (1 - y))

        looped(0, self.planes, one)

        def two(j):
            self.arrived(2 * self.plane(j) + x, 2 * (1 - y))

        looped(1, self.planes, two)

        for k in (2 * y, 2 * y + 1, 2 * (1 - y) + 1):
            for copy in self.copies(1, self.f, k, self.x_side, fresh=True):
                copy.wait_send()

        def three(j):
            f = 2 * self.plane(j) + x
            for side in range(2):
                k = 2 * y + side
                for copy in (*self.copies(1, f, k, self.x_side),
                             *self.copies(2, f, k, self.y_side)):
                    copy.wait_send()
            for copy in self.copies(1, f, 2 * (1 - y) + 1, self.x_side):
                copy.wait_send()

        looped(1, self.planes, three)

        def four(j):
            for copy in self.copies(2, 2 * self.plane(j) + 1 - x, 2 * y, self.y_side):
                copy.wait_send()

        looped(0, self.planes, four)
        for up in (True, False):
            self.hops(self.z, up, lambda copy: copy.wait_send(), fresh=True)
        for d in range(1, self.planes):
            self.at(d, lambda z, up: self.hops(z, up, lambda copy: copy.wait_send()))


def build_diagonals(table_ref, band):
    left = jnp.broadcast_to(band[0:1, :], (lanes, lanes))
    right = jnp.broadcast_to(band[3 * lanes - 1 : 3 * lanes, :], (lanes, lanes))
    for half in range(2):
        cols = slice(half * lanes, (half + 1) * lanes)
        first = far - lanes + half * lanes
        for row in range(0, first, lanes):
            table_ref[row : row + lanes, cols] = left
        table_ref[first : first + 3 * lanes, cols] = band
        for row in range(first + 3 * lanes, reach, lanes):
            table_ref[row : row + lanes, cols] = right


def attend_kernel(
    fsdp_count, gathers, bound_ref, idx_ref, small_ref, tok_ref, cot_ref, *refs,
):
    if gathers:
        wq_src, wo_src, wgu_src, wd_src, *refs = refs
    else:
        w_given, *refs = refs
    (xs_ref, cs_ref, qkv_ref, pl_ref, ps_ref, ctx_ref, ctx32_ref, linv_ref, gains_ref, w_ref,
     *refs) = refs
    if gathers:
        wo_ref, wgu_ref, wd_ref, *refs = refs
    (smalls, xa, ca, p_long, p_short, table, mask, band, km, vt, ctx_t, linv_t,
     deal_send, deal_recv, pass_send, pass_recv, own, ctx_send, ctx_recv, p_sem, *refs) = refs
    f, p, c = place()
    rows_all, width = xs_ref.shape
    part = width // 2
    pairs = part // lanes
    short = rows_all - longest
    half = lanes // 2
    sibling = device(f, p, 1 - c)

    greet_all(fsdp_count)
    deals = [
        Dealing(fsdp_count, src, dst, deal_send.at[n], deal_recv.at[n], pass_send.at[n],
                pass_recv.at[n], own.at[n])
        for n, (src, dst) in enumerate(((small_ref, smalls), (tok_ref, xa), (cot_ref, ca)))
    ]
    events = []
    deals[0].start()
    if gathers:
        sends_q, recvs_q, own_q, sends_r, recvs_r, own_r = refs
        first = Gathering(fsdp_count, (wq_src,), (w_ref,), sends_q, recvs_q, own_q)
        rest = Gathering(fsdp_count, (wo_src, wgu_src, wd_src), (wo_ref, wgu_ref, wd_ref),
                         sends_r, recvs_r, own_r)
        first.start_z()
        rest.start_z()
        first.start_x()
    deals[1].start()
    if gathers:
        rest.start_x()
        order = [(first.spread, 1), (rest.spread, 1), (first.turn, 0), (first.spread, 2),
                 (first.turn, 1), (rest.spread, 2), (first.spread, 3), (first.turn, 2)]
        for step, d in order:
            step(d)
    deals[0].forward()
    deals[0].finish()

    slice_width = width // fsdp_count

    def gain_of(k, total):
        row = iota((lanes, width), 0)
        spot = jnp.where((iota((lanes, width), 1) == k * slice_width + row) & (row < slice_width),
                         1.0, 0.0).astype(bf16)
        return total + nn(smalls[c, p, k].astype(bf16), spot)

    gains_ref[...] = lax.fori_loop(0, fsdp_count, gain_of, jnp.zeros((8, width), f32))

    wide = 4 * lanes
    place_of = iota((lanes, wide), 1)
    offset = jnp.where(place_of < wide // 2, -place_of, wide - place_of)
    chosen = jnp.where(bucket_index(offset) == iota((lanes, wide), 0), 1.0, 0.0).astype(bf16)
    for side in range(2):
        by_head = nn(smalls[side, c, f].astype(bf16), chosen)
        for h in range(pairs):
            line = jnp.broadcast_to(by_head[2 + h : 3 + h, :], (lanes, wide))
            for d in range(3):
                turned = pltpu.roll(line, d * lanes, 1, stride=1, stride_axis=0)
                band[side * pairs + h, d * lanes : (d + 1) * lanes, :] = turned[:, lanes : 2 * lanes]

    bound = bound_ref[0]
    inside = (iota((short, short), 0) < bound) == (iota((short, short), 1) < bound)
    mask[...] = jnp.where(inside, 0.0, -1e30)

    if gathers:
        first.turn(3)
    deals[1].forward()
    if gathers:
        rest.spread(3)
        events = [functools.partial(rest.turn, d) for d in range(4)]
    else:
        given = pltpu.make_async_copy(w_given, w_ref, own.at[3])
        given.start()
        given.wait()
    deals[2].start()
    deals[1].finish()
    if gathers:
        first.finish()

    xa_rows = xa.shape[0] * xa.shape[1] * xa.shape[2] * xa.shape[3]

    def arrive(i):
        rows = pl.ds(pl.multiple_of(i * block, block), block)
        chosen = one_hot(idx_ref[rows, :], iota((block, xa_rows), 1))
        return rows, chosen

    def tile(i):
        rows, chosen = arrive(i)
        x = nn(chosen, xa[...].reshape(xa_rows, width))
        xs_ref[rows, :] = x.astype(bf16)
        normed = (x * inverse_rms(x) * gains_ref[0:1, :]).astype(bf16)
        for k in range(3):
            cols = slice(k * part, (k + 1) * part)
            qkv_ref[rows, cols] = nn(normed, w_ref[:, cols]).astype(bf16)

    looped(0, rows_all // block, tile)

    def poll(count):
        for _ in range(count):
            if events:
                events.pop(0)()

    own_lane = iota((rows_all, lanes), 1) < half
    for pair in range(pairs):
        cols = [slice(kind * part + pair * lanes, kind * part + (pair + 1) * lanes)
                for kind in range(3)]
        keys = qkv_ref[:, cols[1]]
        vt[...] = jnp.transpose(qkv_ref[:, cols[2]].astype(f32)).astype(bf16)
        for h in range(2):
            build_diagonals(table, band[2 * pair + h])
            km[...] = jnp.where(own_lane == (h == 0), keys, jnp.zeros_like(keys))

            def strip(base, count, out_ref, masked, b):
                here = pl.ds(pl.multiple_of(base + b * block, block), block)
                logits = nt(km[base : base + count, :], qkv_ref[here, cols[0]])
                top_row = pl.multiple_of(far - b * block, block)
                logits = logits + table[pl.ds(top_row, count), :]
                spot = pl.ds(pl.multiple_of(b * block, block), block)
                if masked:
                    logits = logits + mask[:, spot]
                top = jnp.max(logits, axis=0, keepdims=True)
                weights = jnp.exp(logits - top)
                inv = 1.0 / jnp.sum(weights, axis=0, keepdims=True)
                low = weights.astype(bf16)
                spot = pl.ds(pl.multiple_of(h * count + b * block, block), block)
                out_ref[pair % 2, :, spot] = low
                part_rows = slice(h * half, (h + 1) * half)
                ctx_t[part_rows, here] = nn(vt[part_rows, base : base + count], low) * inv
                linv_t[part_rows, here] = jnp.broadcast_to(inv, (half, block))

            if h == 0 and pair >= 2:
                for copy in p_copies(p_long, p_short, pl_ref, ps_ref, p_sem, pair - 2):
                    copy.wait()
            looped(0, longest // block, functools.partial(strip, 0, longest, p_long, False))
            poll(1)
            looped(0, short // block, functools.partial(strip, longest, short, p_short, True))
            poll(1)
        context = jnp.transpose(ctx_t[...])
        spot = c * pairs + pair
        ctx32_ref[:, pair * lanes : (pair + 1) * lanes] = context
        ctx_ref[spot] = context.astype(bf16)
        linv_ref[:, pair * lanes : (pair + 1) * lanes] = jnp.transpose(linv_t[...])
        push(ctx_ref.at[spot], ctx_ref.at[spot], ctx_send.at[pair], ctx_recv.at[pair],
             sibling).start()
        for copy in p_copies(p_long, p_short, pl_ref, ps_ref, p_sem, pair):
            copy.start()
        if pair == pairs - 2:
            deals[2].forward()
    poll(len(events))
    deals[2].finish()

    def cot_tile(i):
        rows, chosen = arrive(i)
        cs_ref[rows, :] = nn(chosen, ca[...].reshape(xa_rows, width)).astype(bf16)

    looped(0, rows_all // block, cot_tile)
    for pair in range(pairs):
        spot = c * pairs + pair
        there = (1 - c) * pairs + pair
        push(ctx_ref.at[spot], ctx_ref.at[spot], ctx_send.at[pair], ctx_recv.at[pair],
             sibling).wait_send()
        push(ctx_ref.at[there], ctx_ref.at[there], ctx_send.at[pair], ctx_recv.at[pair],
             sibling).wait_recv()
    for pair in range(max(0, pairs - 2), pairs):
        for copy in p_copies(p_long, p_short, pl_ref, ps_ref, p_sem, pair):
            copy.wait()
    for deal in deals:
        deal.sent()
        deal.passed()
    if gathers:
        rest.finish()


def p_copies(p_long, p_short, pl_ref, ps_ref, sem, pair):
    return [
        pltpu.make_async_copy(p_long.at[pair % 2], pl_ref.at[pair], sem.at[0, pair]),
        pltpu.make_async_copy(p_short.at[pair % 2], ps_ref.at[pair], sem.at[1, pair]),
    ]


def attend(fsdp_count, gathers, bound, idx_col, small, tokens, cotangent, *weights):
    rows = idx_col.shape[0]
    piece, width = tokens.shape[2:]
    part = width // 2
    pairs = part // lanes
    short = rows - longest
    vm = pl.BlockSpec(memory_space=pltpu.VMEM)
    hbm = pl.BlockSpec(memory_space=pl.ANY)
    dma = pltpu.SemaphoreType.DMA
    arrivals = pltpu.VMEM((2, 2, fsdp_count, piece, width), bf16)
    full = [jax.ShapeDtypeStruct((w.shape[0] * fsdp_count, w.shape[1]), bf16) for w in weights]
    out_shape = [
        jax.ShapeDtypeStruct((rows, width), bf16),
        jax.ShapeDtypeStruct((rows, width), bf16),
        jax.ShapeDtypeStruct((rows, 3 * part), bf16),
        jax.ShapeDtypeStruct((pairs, longest, 2 * longest), bf16),
        jax.ShapeDtypeStruct((pairs, short, 2 * short), bf16),
        jax.ShapeDtypeStruct((2 * pairs, rows, lanes), bf16),
        jax.ShapeDtypeStruct((rows, part), f32),
        jax.ShapeDtypeStruct((rows, part), f32),
        jax.ShapeDtypeStruct((8, width), f32),
        jax.ShapeDtypeStruct((width, 3 * part), bf16),
    ]
    out_specs = [vm, vm, vm, hbm, hbm, vm, vm, vm, vm, vm]
    scratch = [
        pltpu.VMEM((2, 2, fsdp_count, 8, lanes), f32),
        arrivals, arrivals,
        pltpu.VMEM((2, longest, 2 * longest), bf16),
        pltpu.VMEM((2, short, 2 * short), bf16),
        pltpu.VMEM((reach, block), f32),
        pltpu.VMEM((short, short), f32),
        pltpu.VMEM((2 * pairs, 3 * lanes, lanes), f32),
        pltpu.VMEM((rows, lanes), bf16),
        pltpu.VMEM((lanes, rows), bf16),
        pltpu.VMEM((lanes, rows), f32),
        pltpu.VMEM((lanes, rows), f32),
        dma((3, 2 * fsdp_count)), dma((3, 2 * fsdp_count)), dma((3, 2 * fsdp_count)),
        dma((3, 2 * fsdp_count)), dma((4,)), dma((pairs,)), dma((pairs,)), dma((2, pairs)),
    ]
    if gathers:
        out_shape += full[1:]
        out_specs += [hbm] * 3
        scratch += [
            dma((1, 4, fsdp_count, 4)), dma((1, fsdp_count, 4)), dma((1,)),
            dma((3, 4, fsdp_count, 4)), dma((3, fsdp_count, 4)), dma((3,)),
        ]
    return pl.pallas_call(
        functools.partial(attend_kernel, fsdp_count, gathers),
        in_specs=[pl.BlockSpec(memory_space=pltpu.SMEM), vm, vm, hbm, hbm] + [hbm] * len(weights),
        out_specs=tuple(out_specs),
        out_shape=tuple(out_shape),
        scratch_shapes=scratch,
        compiler_params=pltpu.CompilerParams(
            vmem_limit_bytes=vmem_limit, collective_id=0, has_side_effects=True),
        name="attend",
    )(bound, idx_col, small, tokens, cotangent, *weights)


class Homing:
    def __init__(self, fsdp_count, src, dst, send, recv, own):
        self.f, self.p, self.c = place()
        self.count = fsdp_count
        self.src, self.dst, self.send, self.recv, self.own = src, dst, send, recv, own

    def out(self, q, g):
        return push(self.src.at[q, g], self.dst.at[self.p, self.f], self.send.at[q, g],
                    self.recv.at[self.p, self.f], device(g, q, self.c))

    def come(self, q, g):
        return push(self.src.at[q, g], self.dst.at[q, g], self.send.at[q, g],
                    self.recv.at[q, g], device(g, q, self.c))

    def local(self):
        return pltpu.make_async_copy(self.src.at[self.p, self.f], self.dst.at[self.p, self.f],
                                     self.own)

    def start(self, q):
        for i in range(1, self.count):
            self.out(q, lax.rem(self.f + i, self.count)).start()

    def start_other(self):
        self.out(1 - self.p, self.f).start()
        self.local().start()

    def finish(self):
        self.local().wait()
        self.come(1 - self.p, self.f).wait_recv()
        self.out(1 - self.p, self.f).wait_send()
        for q in range(2):

            def one(i, q=q):
                g = lax.rem(self.f + i, self.count)
                self.come(q, g).wait_recv()
                self.out(q, g).wait_send()

            looped(1, self.count, one)


class Returning:
    def __init__(self, idx_ref, rows_ref, given, taken, pass_send, pass_recv, home):
        self.f, self.p, self.c = place()
        self.idx_ref, self.rows_ref, self.given, self.taken = idx_ref, rows_ref, given, taken
        self.pass_send, self.pass_recv, self.home = pass_send, pass_recv, home
        self.count = taken.shape[1] * taken.shape[2]

    def unslot(self, side, q):
        chosen = one_hot(
            iota((self.count, self.rows_ref.shape[0]), 0) + (side * 2 + q) * self.count,
            self.idx_ref[...])
        return nn(chosen, self.rows_ref[...])

    def pass_over(self, q):
        return push(self.given.at[q], self.taken.at[q], self.pass_send.at[q],
                    self.pass_recv.at[q], device(self.f, self.p, 1 - self.c))

    def give(self):
        for q in range(2):
            self.given[q] = self.unslot(1 - self.c, q).astype(bf16).reshape(self.given.shape[1:])
            self.pass_over(q).start()

    def keep(self):
        for q in range(2):
            self.pass_over(q).wait_recv()
            other = self.taken[q].reshape(self.count, self.rows_ref.shape[1]).astype(f32)
            value = self.unslot(self.c, q) + other
            self.taken[q] = value.astype(bf16).reshape(self.taken.shape[1:])
            self.home.start(q)
        self.home.start_other()

    def finish(self):
        for q in range(2):
            self.pass_over(q).wait_send()
        self.home.finish()


def feed_kernel(
    fsdp_count, idx_ref, ctx_ref, ctx32_ref, linv_ref, xs_ref, cs_ref, wo_ref, gains_ref, wgu_ref,
    wd_ref, output_ref, ggu_ref, gd_ref, datt_ref, dos_ref, go_ref, ggain_ref,
    out, mid, nff, hid, dgu, dn, dn_sib, given, taken, send, recv, pass_send, pass_recv,
    home_send, home_recv, own,
):
    rows_all, width = xs_ref.shape
    ff = wd_ref.shape[0]
    part = width // 2
    lift = math.sqrt(2 / math.pi)
    tiles = rows_all // block
    f, p, c = place()
    sibling = device(f, p, 1 - c)
    gain = gains_ref[1:2, :]
    half_cols = pl.ds(pl.multiple_of(c * part, lanes), part)
    home = Homing(fsdp_count, taken, output_ref, home_send, home_recv, own)
    rows_home = Returning(idx_ref, out, given, taken, pass_send, pass_recv, home)
    greet_all(fsdp_count)

    def exchange(i):
        rows = pl.ds(pl.multiple_of(i * block, block), block)
        return pltpu.make_async_remote_copy(
            src_ref=dn.at[rows, :], dst_ref=dn_sib.at[rows, :], send_sem=send.at[i],
            recv_sem=recv.at[i], device_id=sibling, device_id_type=MESH)

    def forward(i):
        rows = pl.ds(pl.multiple_of(i * block, block), block)
        mixed = jnp.concatenate([ctx_ref[n, rows, :] for n in range(ctx_ref.shape[0])], axis=1)
        middle = xs_ref[rows, :].astype(f32) + nn(mixed, wo_ref[...])
        mid[rows, :] = middle
        normed = (middle * inverse_rms(middle) * gain).astype(bf16)
        nff[rows, :] = normed
        gate = nn(normed, wgu_ref[:, :ff])
        up = nn(normed, wgu_ref[:, ff:])
        square = gate * gate
        bent = jnp.tanh(lift * gate * (1.0 + 0.044715 * square))
        halved = 0.5 * (1.0 + bent)
        gelu = gate * halved
        slope = halved + 0.5 * gate * (1.0 - bent * bent) * (
            lift * (1.0 + 3 * 0.044715 * square))
        hidden = (gelu * up).astype(bf16)
        hid[rows, :] = hidden
        dgu[rows, :ff] = (up * slope).astype(bf16)
        dgu[rows, ff:] = gelu.astype(bf16)
        out[rows, :] = (0.5 * middle + nn(hidden, wd_ref[...])).astype(bf16)

    def backward(i):
        rows = pl.ds(pl.multiple_of(i * block, block), block)
        d_hidden = nt(cs_ref[rows, :], wd_ref[...])
        d_gate = (d_hidden * dgu[rows, :ff].astype(f32)).astype(bf16)
        d_up = (d_hidden * dgu[rows, ff:].astype(f32)).astype(bf16)
        dgu[rows, :ff] = d_gate
        dgu[rows, ff:] = d_up
        dn[rows, :] = (nt(d_gate, wgu_ref[:, :ff]) + nt(d_up, wgu_ref[:, ff:])).astype(bf16)
        exchange(i).start()

    looped(0, tiles, forward)
    rows_home.give()
    looped(0, 1, backward)
    rows_home.keep()
    looped(1, tiles, backward)

    def down(i, carry):
        cols = pl.ds(pl.multiple_of(i * block, block), block)
        gd_ref[cols, :] = tn(hid[:, cols], cs_ref[...]).astype(bf16)
        return carry

    lax.fori_loop(0, ff // block, down, 0)

    def settle(i, total):
        rows = pl.ds(pl.multiple_of(i * block, block), block)
        exchange(i).wait()
        mine = dn[rows, :].astype(f32)
        grad = mine + dn_sib[rows, :].astype(f32)
        middle = mid[rows, :]
        s = inverse_rms(middle)
        unit = middle * s
        scaled = gain * grad
        d_middle = cs_ref[rows, :].astype(f32) + s * (
            scaled - unit * jnp.mean(scaled * unit, axis=-1, keepdims=True))
        low = d_middle.astype(bf16)
        datt_ref[rows, :] = low
        d_context = nt(low, wo_ref[half_cols, :]).astype(bf16).astype(f32)
        scaled = (d_context * linv_ref[rows, :]).astype(bf16).astype(f32)
        against = scaled * ctx32_ref[rows, :]
        lane = iota((block, lanes), 1)
        for n in range(dos_ref.shape[0]):
            cols = slice((n // 2) * lanes, (n // 2 + 1) * lanes)
            mine_lanes = (lane < lanes // 2) == (n % 2 == 0)
            spare = lanes // 2 if n % 2 == 0 else 0
            delta = jnp.sum(jnp.where(mine_lanes, against[:, cols], 0.0), axis=1, keepdims=True)
            high = delta.astype(bf16).astype(f32)
            extra = jnp.where(lane == spare, -high,
                              jnp.where(lane == spare + 1, high - delta, 0.0))
            dos_ref[n, rows, :] = jnp.where(mine_lanes, scaled[:, cols], extra).astype(bf16)
        return total + jnp.sum(mine * unit, axis=0, keepdims=True)

    ggain_ref[...] = lax.fori_loop(0, tiles, settle, jnp.zeros((1, width), f32))
    for n in range(0, ctx_ref.shape[0], 2):
        mixed = jnp.concatenate((ctx_ref[n], ctx_ref[n + 1]), axis=1)
        go_ref[n * lanes : (n + 2) * lanes, :] = tn(mixed, datt_ref[:, half_cols]).astype(bf16)

    def gate_up(i, carry):
        cols = pl.ds(pl.multiple_of(i * block, block), block)
        ggu_ref[cols, :] = tn(nff[:, cols], dgu[...]).astype(bf16)
        return carry

    lax.fori_loop(0, width // block, gate_up, 0)
    rows_home.finish()


def feed(fsdp_count, piece, idx_row, ctx, ctx32, linv, xs, cs, w_out, gains, w_gu, w_down):
    rows, width = xs.shape
    ff = w_down.shape[0]
    part = width // 2
    shape = (2, fsdp_count, piece, width)
    dma = pltpu.SemaphoreType.DMA
    vm = pl.BlockSpec(memory_space=pltpu.VMEM)
    return pl.pallas_call(
        functools.partial(feed_kernel, fsdp_count),
        in_specs=[vm] * 10,
        out_specs=(pl.BlockSpec(memory_space=pl.ANY), *(vm,) * 6),
        out_shape=(
            jax.ShapeDtypeStruct(shape, bf16),
            jax.ShapeDtypeStruct((width, 2 * ff), bf16),
            jax.ShapeDtypeStruct((ff, width), bf16),
            jax.ShapeDtypeStruct((rows, width), bf16),
            jax.ShapeDtypeStruct((ctx.shape[0], rows, lanes), bf16),
            jax.ShapeDtypeStruct((width, part), bf16),
            jax.ShapeDtypeStruct((1, width), f32),
        ),
        scratch_shapes=[
            pltpu.VMEM((rows, width), bf16),
            pltpu.VMEM((rows, width), f32),
            pltpu.VMEM((rows, width), bf16),
            pltpu.VMEM((rows, ff), bf16),
            pltpu.VMEM((rows, 2 * ff), bf16),
            pltpu.VMEM((rows, width), bf16),
            pltpu.VMEM((rows, width), bf16),
            pltpu.VMEM(shape, bf16),
            pltpu.VMEM(shape, bf16),
            dma((rows // block,)), dma((rows // block,)), dma((2,)), dma((2,)),
            dma((2, fsdp_count)), dma((2, fsdp_count)), dma,
        ],
        compiler_params=pltpu.CompilerParams(
            vmem_limit_bytes=vmem_limit, collective_id=2, has_side_effects=True),
        name="feed",
    )(idx_row, ctx, ctx32, linv, xs, cs, w_out, gains, w_gu, w_down)


class Scattering:
    def __init__(self, fsdp_count, grads, in_y, in_x, turned, in_z, final, send, recv):
        self.f, self.y, self.c = place()
        self.count = fsdp_count
        self.planes = fsdp_count // 2
        self.z, self.x = self.f // 2, self.f % 2
        self.grads, self.in_y, self.in_x = grads, in_y, in_x
        self.turned, self.in_z, self.final = turned, in_z, final
        self.send, self.recv = send, recv
        self.x_side = device(self.z * 2 + 1 - self.x, self.y, self.c)
        self.y_side = device(self.f, 1 - self.y, self.c)
        self.sibling = device(self.f, self.y, 1 - self.c)

    def part(self, n, f, k):
        return self.grads[n].at[f * 4 + k]

    def plane(self, j):
        return lax.rem(self.z + j, self.planes)

    def order(self):
        return [*range(1, self.planes), 0]

    def move(self, n, kind, i, j, src, dst, where):
        return push(src, dst, self.send.at[n, kind, i, j], self.recv.at[n, kind, i, j], where)

    def along_y(self, n, z, x):
        return self.move(n, 0, z, x, self.part(n, 2 * z + x, 2 * (1 - self.y)),
                         self.in_y[n].at[z, x], self.y_side)

    def along_x(self, n, z, y):
        return self.move(n, 1, z, y, self.part(n, 2 * z + 1 - self.x, 2 * y + 1),
                         self.in_x[n].at[z, y], self.x_side)

    def turn(self, n, z, side):
        if side == 0:
            return self.move(n, 2, z, 0, self.in_y[n].at[z, 1 - self.x],
                             self.turned[n].at[z, 0], self.x_side)
        return self.move(n, 2, z, 1, self.in_x[n].at[z, 1 - self.y], self.turned[n].at[z, 1],
                         self.y_side)

    def summed(self, n, z, side):
        return (self.in_y[n].at[z, self.x], self.in_x[n].at[z, self.y])[side]

    def out_z(self, n, z, side):
        return push(self.summed(n, z, side), self.in_z[n].at[self.z, side],
                    self.send.at[n, 3, z, side], self.recv.at[n, 3, self.z, side],
                    device(2 * z + self.x, self.y, self.c))

    def come_z(self, n, z, side):
        return push(self.summed(n, z, side), self.in_z[n].at[z, side],
                    self.send.at[n, 3, z, side], self.recv.at[n, 3, z, side],
                    device(2 * z + self.x, self.y, self.c))

    def last_y(self, n, side, mine):
        y = self.y if mine else 1 - self.y
        here = self.final[n].at[self.c, 2 * y + side]
        return self.move(n, 4, 0, side, here, here, self.y_side)

    def last_core(self, n, mine):
        here = self.final[n].at[self.c if mine else 1 - self.c]
        return self.move(n, 5, 0, 0, here, here, self.sibling)

    def each(self, body):
        for n in range(len(self.grads)):
            body(n)

    def start(self, j):
        z = self.plane(j)
        for n in range(len(self.grads)):
            for k in range(2):
                self.along_y(n, z, k).start()
                self.along_x(n, z, k).start()

    def fold(self, j):
        z = self.plane(j)
        for n in range(len(self.grads)):
            for k in range(2):
                self.along_y(n, z, k).wait_recv()
                add_to(self.in_y[n].at[z, k], self.part(n, 2 * z + k, 2 * self.y))
            self.turn(n, z, 0).start()
            for k in range(2):
                self.along_x(n, z, k).wait_recv()
                add_to(self.in_x[n].at[z, k], self.part(n, 2 * z + self.x, 2 * k + 1))
            self.turn(n, z, 1).start()

    def plane_sum(self, j):
        z = self.plane(j)
        for n in range(len(self.grads)):
            for side in range(2):
                self.turn(n, z, side).wait_recv()
                add_to(self.summed(n, z, side), self.turned[n].at[z, side])
                if j:
                    self.out_z(n, z, side).start()

    def total(self):
        for n in range(len(self.grads)):
            for side in range(2):
                value = self.summed(n, self.z, side)[...].astype(f32)
                for j in range(1, self.planes):
                    z = self.plane(j)
                    self.come_z(n, z, side).wait_recv()
                    value = value + self.in_z[n][z, side].astype(f32)
                self.final[n][self.c, 2 * self.y + side] = value.astype(bf16)
                self.last_y(n, side, True).start()

    def share(self):
        for n in range(len(self.grads)):
            for side in range(2):
                self.last_y(n, side, False).wait_recv()
            self.last_core(n, True).start()

    def finish(self):
        for n in range(len(self.grads)):
            self.last_core(n, False).wait_recv()
            self.last_core(n, True).wait_send()
            for side in range(2):
                self.last_y(n, side, True).wait_send()
            for j in range(self.planes):
                z = self.plane(j)
                for k in range(2):
                    self.along_y(n, z, k).wait_send()
                    self.along_x(n, z, k).wait_send()
                    self.turn(n, z, k).wait_send()
                    if j:
                        self.out_z(n, z, k).wait_send()

    def steps(self, together):
        order = self.order()
        if together:
            return [
                lambda: [self.start(j) for j in order],
                lambda: [self.fold(j) for j in order],
                lambda: [self.plane_sum(j) for j in order],
                self.total, self.share,
            ]
        ahead = 2
        out = [lambda: [self.start(j) for j in order[:ahead]]]

        def fold(n):
            self.fold(order[n])
            if n + ahead < len(order):
                self.start(order[n + ahead])

        for n in range(len(order)):
            out.append(functools.partial(fold, n))
            if n:
                out.append(functools.partial(self.plane_sum, order[n - 1]))
        return out + [functools.partial(self.plane_sum, order[-1]), self.total, self.share]


def add_to(here, other):
    here[...] = (here[...].astype(f32) + other[...].astype(f32)).astype(bf16)


def back_kernel(
    fsdp_count, scatters, idx_ref, xs_ref, gains_ref, ggain_ref, w_ref, dos_ref, qkv_ref, datt_ref,
    pl_ref, ps_ref, *refs,
):
    if scatters:
        grads = refs[:3]
        refs = refs[3:]
    tokens_ref, small_ref, *refs = refs
    if scatters:
        outs, refs = refs[:7], refs[7:]
        gqkv_refs, refs = refs[:3], refs[3:]
    else:
        gqkv_refs, refs = refs[:3], refs[3:]
    (ybuf, normed, dqkv, table, qs, ds_l, ds_s, p_l, p_s, acc, va, kt, dq_t, given, taken,
     smalls, load, p_sem, pass_send, pass_recv, home_send, home_recv, own,
     small_send, small_recv, small_pass, small_back, *refs) = refs
    f, p, c = place()
    sibling = device(f, p, 1 - c)
    rows_all, width = xs_ref.shape
    part = width // 2
    pairs = part // lanes
    short = rows_all - longest
    half = lanes // 2
    gain_attn = gains_ref[0:1, :]

    def p_copies(head):
        pair, h = head // 2, head % 2
        return [
            pltpu.make_async_copy(pl_ref.at[pair, :, h * longest : (h + 1) * longest],
                                  p_l.at[h], p_sem.at[0, h]),
            pltpu.make_async_copy(ps_ref.at[pair, :, h * short : (h + 1) * short],
                                  p_s.at[h], p_sem.at[1, h]),
        ]

    for head in range(2):
        for copy in p_copies(head):
            copy.start()
    greet_all(fsdp_count)
    sets = []
    if scatters:
        for group in range(1 + pairs):
            arrays = grads if group == 0 else (gqkv_refs[group - 1],)
            count = len(arrays)
            bufs = [refs[k * count : (k + 1) * count] for k in range(5)]
            send, recv = refs[5 * count : 5 * count + 2]
            refs = refs[5 * count + 2 :]
            sets.append(Scattering(fsdp_count, arrays, *bufs, send, recv))
    steps = [group.steps(n > 0) for n, group in enumerate(sets)]

    def poll(*which):
        for n in which:
            if scatters and steps[n]:
                steps[n].pop(0)()

    places = {0: (0,), 3: (0,), 4: (0,), 7: (0,), 8: (0,), 11: (0,), 12: (0,), 13: (1,), 14: (0,),
              15: (1,), 16: (0,), 17: (2,)}
    poll(0)

    home = Homing(fsdp_count, taken, tokens_ref, home_send, home_recv, own.at[0])
    rows_home = Returning(idx_ref, ybuf, given, taken, pass_send, pass_recv, home)

    def norm_tile(i):
        rows = pl.ds(pl.multiple_of(i * block, block), block)
        x = xs_ref[rows, :].astype(f32)
        normed[rows, :] = (x * inverse_rms(x) * gain_attn).astype(bf16)

    looped(0, rows_all // block, norm_tile)

    lane = iota((rows_all, lanes), 1)
    buckets = band_buckets()
    small_ref_rows = iota((lanes // 4, lanes), 1)
    bias = jnp.zeros((lanes // 4, lanes), f32)
    for pair in range(pairs):
        cols = [slice(kind * part + pair * lanes, kind * part + (pair + 1) * lanes)
                for kind in range(3)]
        queries = qkv_ref[:, cols[0]]
        keys = qkv_ref[:, cols[1]]
        values = qkv_ref[:, cols[2]]
        kt[...] = jnp.transpose(keys.astype(f32)).astype(bf16)
        for h in range(2):
            head = 2 * pair + h
            own_lanes = (lane < half) == (h == 0)
            spare = half if h == 0 else 0
            qs[...] = jnp.where(own_lanes, queries, jnp.zeros_like(queries))
            ones = jnp.where((lane == spare) | (lane == spare + 1), 1.0, 0.0)
            va[...] = jnp.where(own_lanes, values.astype(f32), ones).astype(bf16)
            table[...] = jnp.zeros_like(table)
            for copy in p_copies(head):
                copy.wait()

            def strip(base, count, p_buf, ds_buf, b):
                here = pl.ds(pl.multiple_of(base + b * block, block), block)
                spot = pl.ds(pl.multiple_of(b * block, block), block)
                d_weights = nt(va[base : base + count, :], dos_ref[head, here, :])
                d_logits = p_buf[h, :, spot].astype(f32) * d_weights
                window = pl.ds(pl.multiple_of(far - b * block, block), count)
                table[window, :] = table[window, :] + d_logits
                low = d_logits.astype(bf16)
                ds_buf[:, spot] = low
                part_rows = slice(h * half, (h + 1) * half)
                dq_t[part_rows, here] = nn(kt[part_rows, base : base + count], low)

            looped(0, longest // block, functools.partial(strip, 0, longest, p_l, ds_l))
            poll(*places.get(3 * head, ()))
            looped(0, short // block, functools.partial(strip, longest, short, p_s, ds_s))
            poll(*places.get(3 * head + 1, ()))
            for base, count, p_buf, ds_buf in ((0, longest, p_l, ds_l), (longest, short, p_s, ds_s)):
                rows = slice(base, base + count)
                clean = jnp.where(own_lanes[rows], dos_ref[head, rows, :].astype(f32), 0.0)
                d_value = nn(p_buf[h], clean.astype(bf16))
                d_key = nn(ds_buf[...], qs[rows, :])
                if h == 0:
                    acc[0, rows, :] = d_value
                    acc[1, rows, :] = d_key
                else:
                    dqkv[rows, cols[2]] = (acc[0, rows, :] + d_value).astype(bf16)
                    dqkv[rows, cols[1]] = (acc[1, rows, :] + d_key).astype(bf16)
            if head + 2 < 2 * pairs:
                for copy in p_copies(head + 2):
                    copy.start()
            before = far - lanes
            after = far + 3 * lanes
            band = table[before : before + 3 * lanes, :lanes] + table[far : far + 3 * lanes, lanes:]
            left = jnp.sum(table[:before, :lanes] + table[:before, lanes:], axis=0, keepdims=True)
            left = left + jnp.sum(table[before:far, lanes:], axis=0, keepdims=True)
            right = jnp.sum(table[after:, :lanes] + table[after:, lanes:], axis=0, keepdims=True)
            right = right + jnp.sum(table[after - lanes : after, :lanes], axis=0, keepdims=True)
            for label in range(lanes // 4):
                line = jnp.sum(jnp.where(buckets == label, band, 0.0), axis=0, keepdims=True)
                if label == 15:
                    line = line + left
                if label == 31:
                    line = line + right
                table[label : label + 1, :lanes] = line
            sums = jnp.sum(table[: lanes // 4, :lanes], axis=1, keepdims=True)
            bias = bias + jnp.where(small_ref_rows == c * 2 * pairs + head, sums, 0.0)
            poll(*places.get(3 * head + 2, ()))
        dqkv[:, cols[0]] = jnp.transpose(dq_t[...]).astype(bf16)
        for kind in range(3):
            grad = tn(normed[...], dqkv[:, cols[kind]])
            grad = grad.reshape(*gqkv_refs[pair].shape[:-1], lanes)
            gqkv_refs[pair][..., kind * lanes : (kind + 1) * lanes] = grad.astype(bf16)
        if pair == pairs - 1:
            reload = pltpu.make_async_copy(datt_ref, normed, load)
            reload.start()
        poll(1 + pair)

    def tile(i, total):
        rows = slice(i * block, (i + 1) * block)
        x = xs_ref[rows, :].astype(f32)
        s = inverse_rms(x)
        unit = x * s
        grad = nt(dqkv[rows, :], w_ref[...])
        scaled = gain_attn * grad
        y = 0.5 * normed[rows, :].astype(f32) + s * (
            scaled - unit * jnp.mean(scaled * unit, axis=-1, keepdims=True))
        ybuf[rows, :] = y.astype(bf16)
        return total + jnp.sum(grad * unit, axis=0, keepdims=True)

    grad_gain = jnp.zeros((1, width), f32)
    reload.wait()
    for i in range(rows_all // block):
        grad_gain = tile(i, grad_gain)
    poll(2, 1, 0)
    rows_home.give()
    quarter = lanes // 4
    small_ref[0:quarter, :] = bias
    small_ref[quarter:, :] = jnp.zeros((small_ref.shape[0] - quarter, lanes), f32)
    for j in range(width // lanes):
        cols = slice(j * lanes, (j + 1) * lanes)
        small_ref[quarter + j : quarter + j + 1, :] = grad_gain[:, cols]
        row = quarter + 8 + j
        small_ref[row : row + 1, :] = ggain_ref[:, cols]
    dealt = Dealing(fsdp_count, small_ref, smalls, small_send, small_recv, small_pass, small_back,
                    own.at[1])
    dealt.start()
    poll(3, 2, 1)
    rows_home.keep()
    poll(3, 2, 3, 3)
    dealt.forward()
    dealt.finish()
    dealt.sent()
    dealt.passed()

    def gather_small(k, total):
        return total + smalls[k // (2 * fsdp_count), (k // fsdp_count) % 2, k % fsdp_count]

    small_ref[...] = lax.fori_loop(0, 4 * fsdp_count, gather_small,
                                   jnp.zeros(small_ref.shape, f32))
    for group in sets:
        group.finish()
    if scatters:
        gate, up, down, out_w, query, key, value = outs
        gu, dn, wo = sets[0].final
        ff = gu.shape[3] // 2
        cut = ff // fsdp_count
        for k in range(4):
            for side in range(2):
                rows = gu.shape[2]
                rows = slice(k * rows, (k + 1) * rows)
                for g in range(fsdp_count):
                    there = slice((2 * g + side) * cut, (2 * g + side + 1) * cut)
                    gate[rows, there] = gu[side, k, :, g * cut : (g + 1) * cut].astype(f32)
                    up[rows, there] = gu[side, k, :, ff + g * cut : ff + (g + 1) * cut].astype(f32)
                many = dn.shape[2]
                first = (side * 4 + k) * many
                down[first : first + many, :] = dn[side, k].astype(f32)
                out_w[rows, side * part : (side + 1) * part] = wo[side, k].astype(f32)
                for pair in range(pairs):
                    [one] = sets[1 + pair].final
                    there = slice(side * part + pair * lanes, side * part + (pair + 1) * lanes)
                    for kind, ref in enumerate((query, key, value)):
                        ref[rows, there] = one[side, k, :, kind * lanes : (kind + 1) * lanes].astype(
                            f32)
    rows_home.finish()


def back(fsdp_count, piece, scatters, idx_row, xs, gains, ggain, w_qkv, datt, dos, qkv,
         p_long, p_short, grads):
    rows, width = xs.shape
    part = width // 2
    pairs = part // lanes
    short = rows - longest
    vm = pl.BlockSpec(memory_space=pltpu.VMEM)
    hbm = pl.BlockSpec(memory_space=pl.ANY)
    dma = pltpu.SemaphoreType.DMA
    shape = (2, fsdp_count, piece, width)
    own_rows = width // fsdp_count
    out_shape = [
        jax.ShapeDtypeStruct(shape, bf16), jax.ShapeDtypeStruct((48, lanes), f32),
    ]
    out_specs = [hbm, vm]
    if scatters:
        ff = grads[0].shape[1]
        out_shape += [jax.ShapeDtypeStruct((own_rows, ff), f32)] * 2
        out_shape += [jax.ShapeDtypeStruct((2 * grads[1].shape[0] // fsdp_count, width), f32)]
        out_shape += [jax.ShapeDtypeStruct((own_rows, width), f32)] * 4
        out_specs += [vm] * 7
    gqkv = [jax.ShapeDtypeStruct((width, 3 * lanes), bf16)] * pairs
    scratch = []
    if scatters:
        grads = tuple(g.reshape(4 * fsdp_count, -1, g.shape[1]) for g in grads)
        scratch = [pltpu.VMEM((4 * fsdp_count, own_rows // 4, 3 * lanes), bf16)] * pairs
    if not scatters:
        out_shape += gqkv
        out_specs += [vm] * pairs
    scratch += [
        pltpu.VMEM((rows, width), bf16),
        pltpu.VMEM((rows, width), bf16),
        pltpu.VMEM((rows, 3 * part), bf16),
        pltpu.VMEM((reach, block), f32),
        pltpu.VMEM((rows, lanes), bf16),
        pltpu.VMEM((longest, longest), bf16),
        pltpu.VMEM((short, short), bf16),
        pltpu.VMEM((2, longest, longest), bf16),
        pltpu.VMEM((2, short, short), bf16),
        pltpu.VMEM((2, rows, lanes), f32),
        pltpu.VMEM((rows, lanes), bf16),
        pltpu.VMEM((lanes, rows), bf16),
        pltpu.VMEM((lanes, rows), f32),
        pltpu.VMEM(shape, bf16),
        pltpu.VMEM(shape, bf16),
        pltpu.VMEM((2, 2, fsdp_count, 48, lanes), f32),
        dma, dma((2, 2)), dma((2,)), dma((2,)),
        dma((2, fsdp_count)), dma((2, fsdp_count)), dma((2,)),
        *[dma((2 * fsdp_count,))] * 4,
    ]
    if scatters:
        planes = fsdp_count // 2
        for quarters in ([g.shape[1:] for g in grads], *[[(own_rows // 4, 3 * lanes)]] * pairs):
            for lead in ((planes, 2), (planes, 2), (planes, 2), (planes, 2), (2, 4)):
                scratch += [pltpu.VMEM((*lead, *q), bf16) for q in quarters]
            scratch += [dma((len(quarters), 6, planes, 2))] * 2
    return pl.pallas_call(
        functools.partial(back_kernel, fsdp_count, scatters),
        in_specs=[vm] * 7 + [hbm] * 3 + [vm] * (len(grads) if scatters else 0),
        out_specs=tuple(out_specs),
        out_shape=tuple(out_shape),
        scratch_shapes=scratch,
        compiler_params=pltpu.CompilerParams(
            vmem_limit_bytes=vmem_limit, collective_id=1, has_side_effects=True),
        name="back",
    )(idx_row, xs, gains, ggain, w_qkv, dos, qkv, datt, p_long, p_short,
      *(grads if scatters else ()))


def shards(
    tokens, cotangent, lengths, dealing, gain_attn, w_query, w_key, w_value, w_out, bias_table,
    gain_ff, w_gate, w_up, w_down,
):
    fsdp_count = lax.axis_size("fsdp")
    sp_count = lax.axis_size("sp")
    micro_count, token_rows, width = tokens.shape
    piece = token_rows // fsdp_count
    group_rows = token_rows * sp_count
    local_heads = bias_table.shape[1]
    heads = local_heads * sp_count
    part = width // 2
    s = lax.axis_index("sp")
    p, c = s // 2, s % 2
    full_piece = -(-piece // 8) * 8

    def pieces(value):
        value = value.reshape(micro_count, fsdp_count, piece, width)
        return jnp.pad(value, ((0, 0), (0, 0), (0, full_piece - piece), (0, 0)))

    order = lax.dynamic_index_in_dim(dealing[:, 0], p, 0, keepdims=False)
    length = lax.dynamic_index_in_dim(lengths[:, 0], p, 0, keepdims=False)
    first_long = length[0] == longest
    start = jnp.where(first_long, 0, jnp.where(length[1] == longest, length[0],
                                               length[0] + length[1]))
    bound = jnp.where(first_long, length[1], length[0]).reshape(1)
    short = group_rows - longest
    head_part = lax.dynamic_slice_in_dim(order, start, longest, 0)
    tail = jnp.where(jnp.arange(short) < start, order[:short], order[longest:])
    order = jnp.concatenate((head_part, tail))
    source, within = order // token_rows, order % token_rows
    idx = ((source % 2) * 2 + source // 2) * fsdp_count + within // piece
    idx = idx * full_piece + within % piece

    def half_cols(weight):
        return lax.dynamic_slice_in_dim(weight, c * part, part, 1)

    def half_ff(weight):
        split = weight.reshape(weight.shape[0], fsdp_count, 2, -1)
        return lax.dynamic_index_in_dim(split, c, 2, keepdims=False).reshape(weight.shape[0], -1)

    def gather(value, axis=0):
        return lax.all_gather(value, "fsdp", axis=axis, tiled=True)

    def line(value):
        return jnp.pad(value.astype(f32), ((0, 0), (0, lanes - value.shape[1])))

    small = jnp.concatenate([line(gain_attn[None]), line(gain_ff[None]), line(bias_table.T)])
    small = jnp.pad(small, ((0, 8 - small.shape[0]), (0, 0)))
    down_rows = w_down.shape[0] // 2
    weights = (
        jnp.concatenate([half_cols(w) for w in (w_query, w_key, w_value)], axis=1),
        w_out,
        jnp.concatenate([half_ff(w) for w in (w_gate, w_up)], axis=1),
        lax.dynamic_slice_in_dim(w_down, c * down_rows, down_rows, 0),
    )
    gathers = fsdp_count == 8 and all(w.shape[0] % 32 == 0 for w in weights)
    if not gathers:
        weights = tuple(gather(w) for w in weights)
    args = (bound, idx.reshape(-1, 1), small, pieces(tokens), pieces(cotangent))
    xs, cs, qkv, p_long, p_short, ctx, ctx32, linv, gains, w_qkv, *late = attend(
        fsdp_count, gathers, *args, *(weights if gathers else weights[:1]))
    wo, w_gu, wd = late if gathers else weights[1:]
    buckets = band_buckets()
    idx_row = idx.reshape(1, -1)
    output, grad_gu, grad_d, datt, dos, grad_o, grad_gain_ff = feed(
        fsdp_count, full_piece, idx_row, ctx, ctx32, linv, xs, cs, wo, gains, w_gu, wd)
    grad_tokens, small, *grads = back(
        fsdp_count, full_piece, gathers, idx_row, xs, gains, grad_gain_ff, w_qkv, datt,
        dos, qkv, p_long, p_short, (grad_gu, grad_d, grad_o))
    output, grad_tokens = (x[:, :, :piece].reshape(tokens.shape) for x in (output, grad_tokens))
    own_gain = width // fsdp_count
    f = lax.axis_index("fsdp")
    labels = bias_table.shape[0]
    bias_grad = lax.dynamic_slice_in_dim(small[:labels], s * local_heads, local_heads, 1)
    gain_grads = [
        lax.dynamic_slice_in_dim(
            small[first : first + width // lanes].reshape(-1), f * own_gain, own_gain, 0)
        for first in (labels, labels + 8)
    ]
    if not gathers:
        grads = scatter_rows(fsdp_count, c, (grad_gu, grad_d, grad_o, *grads))
    grad_gate, grad_up, grad_down, grad_out, grad_query, grad_key, grad_value = grads
    return (
        output, grad_tokens, gain_grads[0], grad_query, grad_key, grad_value, grad_out, bias_grad,
        gain_grads[1], grad_gate, grad_up, grad_down,
    )


def scatter_rows(fsdp_count, c, partial_grads):
    sibling = [(0, 1), (1, 0), (2, 3), (3, 2)]
    across = [(0, 2), (2, 0), (1, 3), (3, 1)]
    shares = [lax.psum_scatter(v, "fsdp", scatter_dimension=0, tiled=True) for v in partial_grads]
    shares = [v.astype(f32) + lax.ppermute(v, "sp", across).astype(f32) for v in shares]
    shares = [v.astype(bf16) for v in shares]
    others = [lax.ppermute(v, "sp", sibling) for v in shares]
    sides = [
        (jnp.where(c == 0, v, w).astype(f32), jnp.where(c == 0, w, v).astype(f32))
        for v, w in zip(shares, others)
    ]
    gu, down, out, *qkv = sides
    rows = gu[0].shape[0]
    ff = gu[0].shape[1] // 2

    def ff_cols(which):
        cut = [x[:, which * ff : (which + 1) * ff].reshape(rows, fsdp_count, 1, -1) for x in gu]
        return jnp.concatenate(cut, axis=2).reshape(rows, -1)

    def proj(kind):
        return jnp.concatenate(
            [pair[side][:, kind * lanes : (kind + 1) * lanes] for side in range(2) for pair in qkv],
            axis=1)

    return (ff_cols(0), ff_cols(1), jnp.concatenate(down), jnp.concatenate(out, axis=1),
            proj(0), proj(1), proj(2))


def solution(mesh):
    return jax.shard_map(
        shards,
        mesh=mesh,
        in_specs=(
            P(None, ("fsdp", "sp"), None), P(None, ("fsdp", "sp"), None),
            P(None, "fsdp", None), P(None, "fsdp", None),
            P("fsdp"), P("fsdp", None), P("fsdp", None), P("fsdp", None), P("fsdp", None),
            P(None, "sp"), P("fsdp"), P("fsdp", None), P("fsdp", None), P("fsdp", None),
        ),
        out_specs=(
            P(None, ("fsdp", "sp"), None), P(None, ("fsdp", "sp"), None),
            P("fsdp"), P("fsdp", None), P("fsdp", None), P("fsdp", None), P("fsdp", None),
            P(None, "sp"), P("fsdp"), P("fsdp", None), P("fsdp", None), P("fsdp", None),
        ),
        check_vma=False,
    )
```

```python
import functools
import math

import jax
import jax.numpy as jnp
from jax import lax
from jax.experimental import pallas as pl
from jax.experimental.pallas import tpu as pltpu
from jax.sharding import PartitionSpec as P

bucket_edges = (1, 2, 3, 4, 5, 6, 7, 8, 12, 16, 23, 32, 46, 64, 91)
epsilon = 1e-06
longest = 1024
lanes = 128
block = 256
far = 768
reach = 1792
MESH = pl.DeviceIdType.MESH
f32 = jnp.float32
bf16 = jnp.bfloat16
vmem_limit = 62 * 2**20


def nn(left, right):
    return jnp.dot(left, right, preferred_element_type=f32)


def nt(left, right):
    return lax.dot_general(left, right, (((1,), (1,)), ((), ())), preferred_element_type=f32)


def tn(left, right):
    return lax.dot_general(left, right, (((0,), (0,)), ((), ())), preferred_element_type=f32)


def iota(shape, dim):
    return lax.broadcasted_iota(jnp.int32, shape, dim)


def one_hot(column, row):
    return jnp.where(column == row, 1.0, 0.0).astype(bf16)


def inverse_rms(values):
    return lax.rsqrt(jnp.mean(values * values, axis=-1, keepdims=True) + epsilon)


def bucket_index(offset):
    distance = jnp.abs(offset)
    bucket_sum = jnp.where(offset > 0, 16, 0).astype(jnp.int32)
    for border in bucket_edges:
        bucket_sum = bucket_sum + (distance >= border).astype(jnp.int32)
    return bucket_sum


def band_buckets():
    shape = (3 * lanes, lanes)
    return bucket_index(iota(shape, 0) - lanes - iota(shape, 1))


def whole_spec(shape, space=pltpu.VMEM):
    return pl.BlockSpec(shape, lambda *_: (0,) * len(shape), memory_space=space,
                        pipeline_mode=pl.Buffered(1))


def place():
    f = lax.axis_index("fsdp")
    s = lax.axis_index("sp")
    return f, s // 2, s % 2


def device(f, p, c):
    return {"fsdp": f, "sp": 2 * p + c}


def signal(barrier, where):
    pl.semaphore_signal(barrier, inc=1, device_id=where, device_id_type=MESH)


def greet_all(fsdp_count):
    f, p, c = place()
    barrier = pltpu.get_barrier_semaphore()
    peers = 2 * fsdp_count
    mine = p * fsdp_count + f

    def greet(i, carry):
        k = lax.rem(mine + i, peers)
        signal(barrier, device(k % fsdp_count, k // fsdp_count, c))
        return carry

    lax.fori_loop(1, peers, greet, 0)
    signal(barrier, device(f, p, 1 - c))
    pl.semaphore_wait(barrier, peers)


def push(src, dst, send, recv, where):
    return pltpu.make_async_remote_copy(
        src_ref=src, dst_ref=dst, send_sem=send, recv_sem=recv, device_id=where,
        device_id_type=MESH)


def looped(first, last, body):
    def step(i, carry):
        body(i)
        return carry

    lax.fori_loop(first, last, step, 0)


class Dealing:
    def __init__(self, fsdp_count, src, dst, send, recv, pass_send, pass_recv, own):
        self.f, self.p, self.c = place()
        self.count = fsdp_count
        self.peers = 2 * fsdp_count
        self.mine = self.p * fsdp_count + self.f
        self.src, self.dst, self.send, self.recv = src, dst, send, recv
        self.pass_send, self.pass_recv, self.own = pass_send, pass_recv, own

    def source(self, k):
        return self.src.at[k // self.count, k % self.count] if len(self.src.shape) == 4 else self.src

    def out(self, k):
        where = device(k % self.count, k // self.count, self.c)
        return push(self.source(k), self.dst.at[self.c, self.p, self.f], self.send.at[k],
                    self.recv.at[self.mine], where)

    def come(self, k):
        where = device(k % self.count, k // self.count, self.c)
        return push(self.source(k), self.dst.at[self.c, k // self.count, k % self.count],
                    self.send.at[k], self.recv.at[k], where)

    def onward(self, k, side):
        here = self.dst.at[side, k // self.count, k % self.count]
        return push(here, here, self.pass_send.at[k], self.pass_recv.at[k],
                    device(self.f, self.p, 1 - self.c))

    def local(self):
        return pltpu.make_async_copy(
            self.source(self.mine), self.dst.at[self.c, self.p, self.f], self.own)

    def start(self):
        looped(1, self.peers, lambda i: self.out(lax.rem(self.mine + i, self.peers)).start())
        self.local().start()

    def forward(self):
        self.local().wait()
        self.onward(self.mine, self.c).start()

        def one(i):
            k = lax.rem(self.mine + self.peers - i, self.peers)
            self.come(k).wait_recv()
            self.onward(k, self.c).start()

        looped(1, self.peers, one)

    def sent(self):
        looped(1, self.peers, lambda i: self.out(lax.rem(self.mine + i, self.peers)).wait_send())

    def finish(self):
        looped(0, self.peers, lambda k: self.onward(k, 1 - self.c).wait_recv())

    def passed(self):
        looped(0, self.peers, lambda k: self.onward(k, self.c).wait_send())


class Gathering:
    def __init__(self, fsdp_count, srcs, dsts, sends, recvs, own):
        self.f, self.y, self.c = place()
        self.count = fsdp_count
        self.planes = fsdp_count // 2
        self.z, self.x = self.f // 2, self.f % 2
        self.srcs, self.dsts, self.sends, self.recvs, self.own = srcs, dsts, sends, recvs, own
        self.x_side = device(self.z * 2 + 1 - self.x, self.y, self.c)
        self.y_side = device(self.f, 1 - self.y, self.c)

    def rows(self, dst, f, k):
        total = dst.shape[0] // self.count
        quarter = total // 4
        return dst.at[pl.ds(pl.multiple_of(f * total + k * quarter, 8), quarter)]

    def copies(self, link, f, k, where, fresh=False):
        out = []
        for n, (src, dst) in enumerate(zip(self.srcs, self.dsts)):
            there = self.rows(dst, f, k)
            quarter = src.shape[0] // 4
            here = src.at[pl.ds(pl.multiple_of(k * quarter, 8), quarter)] if fresh else there
            out.append(push(here, there, self.sends.at[n, link, f, k], self.recvs.at[n, f, k],
                            where))
        return out

    def go(self, *args, **kw):
        for copy in self.copies(*args, **kw):
            copy.start()

    def arrived(self, f, k):
        for copy in self.copies(0, f, k, self.x_side):
            copy.wait_recv()

    def plane(self, j):
        return lax.rem(self.z + j, self.planes)

    def hop(self, z, k, up, fresh=False):
        to = self.z + 1 if up else self.z - 1
        where = device(2 * to + self.x, self.y, self.c)
        return self.copies(0 if up else 3, 2 * z + self.x, k, where, fresh)

    def hops(self, z, up, action, fresh=False):
        @pl.when(self.z + 1 < self.planes if up else self.z > 0)
        def _():
            for side in range(2):
                for copy in self.hop(z, 2 * self.y + side, up, fresh):
                    action(copy)

    def at(self, d, body):
        pl.when(self.z >= d)(lambda: body(self.z - d, True))
        pl.when(self.z + d < self.planes)(lambda: body(self.z + d, False))

    def local(self):
        return [
            pltpu.make_async_copy(
                src, dst.at[pl.ds(pl.multiple_of(self.f * src.shape[0], 8), src.shape[0])],
                self.own.at[n])
            for n, (src, dst) in enumerate(zip(self.srcs, self.dsts))
        ]

    def start_x(self):
        for copy in self.local():
            copy.start()
        for k in (2 * self.y, 2 * self.y + 1, 2 * (1 - self.y) + 1):
            self.go(1, self.f, k, self.x_side, fresh=True)

    def start_z(self):
        for up in (True, False):
            self.hops(self.z, up, lambda copy: copy.start(), fresh=True)

    def spread(self, d):
        def one(z, up):
            f = 2 * z + self.x
            for side in range(2):
                self.arrived(f, 2 * self.y + side)
            self.hops(z, up, lambda copy: copy.start())
            for side in range(2):
                k = 2 * self.y + side
                self.go(1, f, k, self.x_side)
                self.go(2, f, k, self.y_side)

        self.at(d, one)

    def turn(self, d):
        def one(z, up):
            f = 2 * z + 1 - self.x
            self.arrived(f, 2 * self.y)
            self.go(2, f, 2 * self.y, self.y_side)
            if d:
                f = 2 * z + self.x
                k = 2 * (1 - self.y) + 1
                self.arrived(f, k)
                self.go(1, f, k, self.x_side)

        if d:
            self.at(d, one)
        else:
            one(self.z, True)

    def finish(self):
        x, y = self.x, self.y
        for copy in self.local():
            copy.wait()

        def one(j):
            other = 2 * self.plane(j) + 1 - x
            self.arrived(other, 2 * y + 1)
            self.arrived(other, 2 * (1 - y) + 1)
            self.arrived(other, 2 * (1 - y))

        looped(0, self.planes, one)

        def two(j):
            self.arrived(2 * self.plane(j) + x, 2 * (1 - y))

        looped(1, self.planes, two)

        for k in (2 * y, 2 * y + 1, 2 * (1 - y) + 1):
            for copy in self.copies(1, self.f, k, self.x_side, fresh=True):
                copy.wait_send()

        def three(j):
            f = 2 * self.plane(j) + x
            for side in range(2):
                k = 2 * y + side
                for copy in (*self.copies(1, f, k, self.x_side),
                             *self.copies(2, f, k, self.y_side)):
                    copy.wait_send()
            for copy in self.copies(1, f, 2 * (1 - y) + 1, self.x_side):
                copy.wait_send()

        looped(1, self.planes, three)

        def four(j):
            for copy in self.copies(2, 2 * self.plane(j) + 1 - x, 2 * y, self.y_side):
                copy.wait_send()

        looped(0, self.planes, four)
        for up in (True, False):
            self.hops(self.z, up, lambda copy: copy.wait_send(), fresh=True)
        for d in range(1, self.planes):
            self.at(d, lambda z, up: self.hops(z, up, lambda copy: copy.wait_send()))


def build_diagonals(table_ref, band):
    left = jnp.broadcast_to(band[0:1, :], (lanes, lanes))
    right = jnp.broadcast_to(band[3 * lanes - 1 : 3 * lanes, :], (lanes, lanes))
    for half in range(2):
        cols = slice(half * lanes, (half + 1) * lanes)
        first = far - lanes + half * lanes
        for row in range(0, first, lanes):
            table_ref[row : row + lanes, cols] = left
        table_ref[first : first + 3 * lanes, cols] = band
        for row in range(first + 3 * lanes, reach, lanes):
            table_ref[row : row + lanes, cols] = right


def attend_kernel(
    fsdp_count, gathers, bound_ref, idx_ref, small_ref, tok_ref, cot_ref, *refs,
):
    if gathers:
        wq_src, wo_src, wgu_src, wd_src, *refs = refs
    else:
        w_given, *refs = refs
    (xs_out, cs_ref, qkv_out, pl_ref, ps_ref, ctx_ref, ctx32_out, linv_out, gains_ref, w_ref,
     *refs) = refs
    if gathers:
        wo_ref, wgu_ref, wd_ref, *refs = refs
    (xs_ref, qkv_ref, ctx32_ref, linv_ref, idx_col, leave,
     smalls, xa, ca, p_long, p_short, table, mask, band, km, vt, ctx_t, linv_t,
     deal_send, deal_recv, pass_send, pass_recv, own, ctx_send, ctx_recv, p_sem, *refs) = refs
    f, p, c = place()
    rows_all, width = xs_ref.shape
    part = width // 2
    pairs = part // lanes
    short = rows_all - longest
    half = lanes // 2
    sibling = device(f, p, 1 - c)

    greet_all(fsdp_count)
    deals = [
        Dealing(fsdp_count, src, dst, deal_send.at[n], deal_recv.at[n], pass_send.at[n],
                pass_recv.at[n], own.at[n])
        for n, (src, dst) in enumerate(((small_ref, smalls), (tok_ref, xa), (cot_ref, ca)))
    ]
    events = []
    deals[0].start()
    if gathers:
        sends_q, recvs_q, own_q, sends_r, recvs_r, own_r = refs
        first = Gathering(fsdp_count, (wq_src,), (w_ref,), sends_q, recvs_q, own_q)
        rest = Gathering(fsdp_count, (wo_src, wgu_src, wd_src), (wo_ref, wgu_ref, wd_ref),
                         sends_r, recvs_r, own_r)
        first.start_z()
        rest.start_z()
        first.start_x()
    deals[1].start()
    if gathers:
        rest.start_x()
        order = [(first.spread, 1), (rest.spread, 1), (first.turn, 0), (first.spread, 2),
                 (first.turn, 1), (rest.spread, 2), (first.spread, 3), (first.turn, 2)]
        for step, d in order:
            step(d)
    deals[0].forward()
    deals[0].finish()

    slice_width = width // fsdp_count

    def gain_of(k, total):
        row = iota((lanes, width), 0)
        spot = jnp.where((iota((lanes, width), 1) == k * slice_width + row) & (row < slice_width),
                         1.0, 0.0).astype(bf16)
        return total + nn(smalls[c, p, k].astype(bf16), spot)

    gains_ref[...] = lax.fori_loop(0, fsdp_count, gain_of, jnp.zeros((8, width), f32))

    wide = 4 * lanes
    place_of = iota((lanes, wide), 1)
    offset = jnp.where(place_of < wide // 2, -place_of, wide - place_of)
    chosen = jnp.where(bucket_index(offset) == iota((lanes, wide), 0), 1.0, 0.0).astype(bf16)
    for side in range(2):
        by_head = nn(smalls[side, c, f].astype(bf16), chosen)
        for h in range(pairs):
            line = jnp.broadcast_to(by_head[2 + h : 3 + h, :], (lanes, wide))
            for d in range(3):
                turned = pltpu.roll(line, d * lanes, 1, stride=1, stride_axis=0)
                band[side * pairs + h, d * lanes : (d + 1) * lanes, :] = turned[:, lanes : 2 * lanes]

    idx_col[...] = jnp.transpose(
        jnp.broadcast_to(idx_ref[...].astype(f32), (lanes, rows_all)))
    bound = bound_ref[0]
    inside = (iota((short, short), 0) < bound) == (iota((short, short), 1) < bound)
    mask[...] = jnp.where(inside, 0.0, -1e30)

    if gathers:
        first.turn(3)
    deals[1].forward()
    if gathers:
        rest.spread(3)
        events = [functools.partial(rest.turn, d) for d in range(4)]
    else:
        given = pltpu.make_async_copy(w_given, w_ref, own.at[3])
        given.start()
        given.wait()
    deals[2].start()
    deals[1].finish()
    if gathers:
        first.finish()

    xa_rows = xa.shape[0] * xa.shape[1] * xa.shape[2] * xa.shape[3]

    def arrive(i):
        rows = pl.ds(pl.multiple_of(i * block, block), block)
        chosen = one_hot(idx_col[rows, 0:1], iota((block, xa_rows), 1).astype(f32))
        return rows, chosen

    def tile(i):
        rows, chosen = arrive(i)
        x = nn(chosen, xa[...].reshape(xa_rows, width))
        xs_ref[rows, :] = x.astype(bf16)
        normed = (x * inverse_rms(x) * gains_ref[0:1, :]).astype(bf16)
        for k in range(3):
            cols = slice(k * part, (k + 1) * part)
            qkv_ref[rows, cols] = nn(normed, w_ref[:, cols]).astype(bf16)

    looped(0, rows_all // block, tile)
    leaving = [
        pltpu.make_async_copy(here, there, leave.at[n])
        for n, (here, there) in enumerate(((xs_ref, xs_out), (qkv_ref, qkv_out)))
    ]
    for copy in leaving:
        copy.start()

    def poll(count):
        for _ in range(count):
            if events:
                events.pop(0)()

    own_lane = iota((rows_all, lanes), 1) < half
    for pair in range(pairs):
        cols = [slice(kind * part + pair * lanes, kind * part + (pair + 1) * lanes)
                for kind in range(3)]
        keys = qkv_ref[:, cols[1]]
        vt[...] = jnp.transpose(qkv_ref[:, cols[2]].astype(f32)).astype(bf16)
        for h in range(2):
            build_diagonals(table, band[2 * pair + h])
            km[...] = jnp.where(own_lane == (h == 0), keys, jnp.zeros_like(keys))

            def strip(base, count, out_ref, masked, b):
                here = pl.ds(pl.multiple_of(base + b * block, block), block)
                logits = nt(km[base : base + count, :], qkv_ref[here, cols[0]])
                top_row = pl.multiple_of(far - b * block, block)
                logits = logits + table[pl.ds(top_row, count), :]
                spot = pl.ds(pl.multiple_of(b * block, block), block)
                if masked:
                    logits = logits + mask[:, spot]
                top = jnp.max(logits, axis=0, keepdims=True)
                weights = jnp.exp(logits - top)
                inv = 1.0 / jnp.sum(weights, axis=0, keepdims=True)
                low = weights.astype(bf16)
                spot = pl.ds(pl.multiple_of(h * count + b * block, block), block)
                out_ref[pair % 2, :, spot] = low
                part_rows = slice(h * half, (h + 1) * half)
                ctx_t[part_rows, here] = nn(vt[part_rows, base : base + count], low) * inv
                linv_t[part_rows, here] = jnp.broadcast_to(inv, (half, block))

            if h == 0 and pair >= 2:
                for copy in p_copies(p_long, p_short, pl_ref, ps_ref, p_sem, pair - 2):
                    copy.wait()
            looped(0, longest // block, functools.partial(strip, 0, longest, p_long, False))
            poll(1)
            looped(0, short // block, functools.partial(strip, longest, short, p_short, True))
            poll(1)
        context = jnp.transpose(ctx_t[...])
        spot = c * pairs + pair
        ctx32_ref[:, pair * lanes : (pair + 1) * lanes] = context
        ctx_ref[spot] = context.astype(bf16)
        linv_ref[:, pair * lanes : (pair + 1) * lanes] = jnp.transpose(linv_t[...])
        for n, (here, there) in enumerate(((ctx32_ref, ctx32_out), (linv_ref, linv_out))):
            spot_lanes = slice(pair * lanes, (pair + 1) * lanes)
            copy = pltpu.make_async_copy(here.at[:, spot_lanes], there.at[:, spot_lanes],
                                         leave.at[2 + 2 * pair + n])
            copy.start()
            leaving.append(copy)
        push(ctx_ref.at[spot], ctx_ref.at[spot], ctx_send.at[pair], ctx_recv.at[pair],
             sibling).start()
        for copy in p_copies(p_long, p_short, pl_ref, ps_ref, p_sem, pair):
            copy.start()
        if pair == pairs - 2:
            deals[2].forward()
    poll(len(events))
    deals[2].finish()

    def cot_tile(i):
        rows, chosen = arrive(i)
        cs_ref[rows, :] = nn(chosen, ca[...].reshape(xa_rows, width)).astype(bf16)

    looped(0, rows_all // block, cot_tile)
    for pair in range(pairs):
        spot = c * pairs + pair
        there = (1 - c) * pairs + pair
        push(ctx_ref.at[spot], ctx_ref.at[spot], ctx_send.at[pair], ctx_recv.at[pair],
             sibling).wait_send()
        push(ctx_ref.at[there], ctx_ref.at[there], ctx_send.at[pair], ctx_recv.at[pair],
             sibling).wait_recv()
    for pair in range(max(0, pairs - 2), pairs):
        for copy in p_copies(p_long, p_short, pl_ref, ps_ref, p_sem, pair):
            copy.wait()
    for copy in leaving:
        copy.wait()
    for deal in deals:
        deal.sent()
        deal.passed()
    if gathers:
        rest.finish()


def p_copies(p_long, p_short, pl_ref, ps_ref, sem, pair):
    return [
        pltpu.make_async_copy(p_long.at[pair % 2], pl_ref.at[pair], sem.at[0, pair]),
        pltpu.make_async_copy(p_short.at[pair % 2], ps_ref.at[pair], sem.at[1, pair]),
    ]


def attend(fsdp_count, gathers, bound, idx_row, small, tokens, cotangent, *weights):
    rows = idx_row.shape[1]
    piece, width = tokens.shape[2:]
    part = width // 2
    pairs = part // lanes
    short = rows - longest
    vm = pl.BlockSpec(memory_space=pltpu.VMEM)
    hbm = pl.BlockSpec(memory_space=pl.ANY)
    dma = pltpu.SemaphoreType.DMA
    arrivals = pltpu.VMEM((2, 2, fsdp_count, piece, width), bf16)
    full = [jax.ShapeDtypeStruct((w.shape[0] * fsdp_count, w.shape[1]), bf16) for w in weights]
    out_shape = [
        jax.ShapeDtypeStruct((rows, width), bf16),
        jax.ShapeDtypeStruct((rows, width), bf16),
        jax.ShapeDtypeStruct((rows, 3 * part), bf16),
        jax.ShapeDtypeStruct((pairs, longest, 2 * longest), bf16),
        jax.ShapeDtypeStruct((pairs, short, 2 * short), bf16),
        jax.ShapeDtypeStruct((2 * pairs, rows, lanes), bf16),
        jax.ShapeDtypeStruct((rows, part), f32),
        jax.ShapeDtypeStruct((rows, part), f32),
        jax.ShapeDtypeStruct((8, width), f32),
        jax.ShapeDtypeStruct((width, 3 * part), bf16),
    ]
    out_specs = [hbm, vm, hbm, hbm, hbm, vm, hbm, hbm, vm, vm]
    scratch = [
        pltpu.VMEM((rows, width), bf16),
        pltpu.VMEM((rows, 3 * part), bf16),
        pltpu.VMEM((rows, part), f32),
        pltpu.VMEM((rows, part), f32),
        pltpu.VMEM((rows, lanes), f32),
        dma((2 + 2 * pairs,)),
        pltpu.VMEM((2, 2, fsdp_count, 8, lanes), f32),
        arrivals, arrivals,
        pltpu.VMEM((2, longest, 2 * longest), bf16),
        pltpu.VMEM((2, short, 2 * short), bf16),
        pltpu.VMEM((reach, block), f32),
        pltpu.VMEM((short, short), f32),
        pltpu.VMEM((2 * pairs, 3 * lanes, lanes), f32),
        pltpu.VMEM((rows, lanes), bf16),
        pltpu.VMEM((lanes, rows), bf16),
        pltpu.VMEM((lanes, rows), f32),
        pltpu.VMEM((lanes, rows), f32),
        dma((3, 2 * fsdp_count)), dma((3, 2 * fsdp_count)), dma((3, 2 * fsdp_count)),
        dma((3, 2 * fsdp_count)), dma((4,)), dma((pairs,)), dma((pairs,)), dma((2, pairs)),
    ]
    if gathers:
        out_shape += full[1:]
        out_specs += [hbm] * 3
        scratch += [
            dma((1, 4, fsdp_count, 4)), dma((1, fsdp_count, 4)), dma((1,)),
            dma((3, 4, fsdp_count, 4)), dma((3, fsdp_count, 4)), dma((3,)),
        ]
    return pl.pallas_call(
        functools.partial(attend_kernel, fsdp_count, gathers),
        in_specs=[pl.BlockSpec(memory_space=pltpu.SMEM), vm, vm, hbm, hbm] + [hbm] * len(weights),
        out_specs=tuple(out_specs),
        out_shape=tuple(out_shape),
        scratch_shapes=scratch,
        compiler_params=pltpu.CompilerParams(
            vmem_limit_bytes=vmem_limit, collective_id=0, has_side_effects=True),
        name="attend",
    )(bound, idx_row, small, tokens, cotangent, *weights)


class Homing:
    def __init__(self, fsdp_count, src, dst, send, recv, own):
        self.f, self.p, self.c = place()
        self.count = fsdp_count
        self.src, self.dst, self.send, self.recv, self.own = src, dst, send, recv, own

    def out(self, q, g):
        return push(self.src.at[q, g], self.dst.at[self.p, self.f], self.send.at[q, g],
                    self.recv.at[self.p, self.f], device(g, q, self.c))

    def come(self, q, g):
        return push(self.src.at[q, g], self.dst.at[q, g], self.send.at[q, g],
                    self.recv.at[q, g], device(g, q, self.c))

    def local(self):
        return pltpu.make_async_copy(self.src.at[self.p, self.f], self.dst.at[self.p, self.f],
                                     self.own)

    def start(self, q):
        for i in range(1, self.count):
            self.out(q, lax.rem(self.f + i, self.count)).start()

    def start_other(self):
        self.out(1 - self.p, self.f).start()
        self.local().start()

    def finish(self):
        self.local().wait()
        self.come(1 - self.p, self.f).wait_recv()
        self.out(1 - self.p, self.f).wait_send()
        for q in range(2):

            def one(i, q=q):
                g = lax.rem(self.f + i, self.count)
                self.come(q, g).wait_recv()
                self.out(q, g).wait_send()

            looped(1, self.count, one)


class Returning:
    def __init__(self, idx_ref, rows_ref, given, taken, pass_send, pass_recv, home):
        self.f, self.p, self.c = place()
        self.idx_ref, self.rows_ref, self.given, self.taken = idx_ref, rows_ref, given, taken
        self.pass_send, self.pass_recv, self.home = pass_send, pass_recv, home
        self.count = taken.shape[1] * taken.shape[2]

    def unslot(self, side, q):
        chosen = one_hot(
            iota((self.count, self.rows_ref.shape[0]), 0) + (side * 2 + q) * self.count,
            self.idx_ref[...])
        return nn(chosen, self.rows_ref[...])

    def pass_over(self, q):
        return push(self.given.at[q], self.taken.at[q], self.pass_send.at[q],
                    self.pass_recv.at[q], device(self.f, self.p, 1 - self.c))

    def give(self):
        for q in range(2):
            self.given[q] = self.unslot(1 - self.c, q).astype(bf16).reshape(self.given.shape[1:])
            self.pass_over(q).start()

    def keep(self):
        for q in range(2):
            self.pass_over(q).wait_recv()
            other = self.taken[q].reshape(self.count, self.rows_ref.shape[1]).astype(f32)
            value = self.unslot(self.c, q) + other
            self.taken[q] = value.astype(bf16).reshape(self.taken.shape[1:])
            self.home.start(q)
        self.home.start_other()

    def finish(self):
        for q in range(2):
            self.pass_over(q).wait_send()
        self.home.finish()


def feed_kernel(
    fsdp_count, idx_ref, ctx_ref, ctx32_in, linv_in, xs_ref, cs_in, wo_ref, gains_ref, wgu_ref,
    wd_ref, output_ref, ggu_ref, gd_ref, datt_ref, dos_ref, go_ref, ggain_ref,
    out, mid, nff, hid, dgu, dn, dn_sib, given, taken, send, recv, pass_send, pass_recv,
    home_send, home_recv, own, ctx32_ref, linv_ref, cs_ref, late,
):
    rows_all, width = xs_ref.shape
    ff = wd_ref.shape[0]
    part = width // 2
    lift = math.sqrt(2 / math.pi)
    tiles = rows_all // block
    f, p, c = place()
    sibling = device(f, p, 1 - c)
    gain = gains_ref[1:2, :]
    half_cols = pl.ds(pl.multiple_of(c * part, lanes), part)
    comes = [
        pltpu.make_async_copy(there, here, late.at[n])
        for n, (there, here) in enumerate(
            ((cs_in, cs_ref), (ctx32_in, ctx32_ref), (linv_in, linv_ref)))
    ]
    for copy in comes:
        copy.start()
    home = Homing(fsdp_count, taken, output_ref, home_send, home_recv, own)
    rows_home = Returning(idx_ref, out, given, taken, pass_send, pass_recv, home)
    greet_all(fsdp_count)

    def exchange(i):
        rows = pl.ds(pl.multiple_of(i * block, block), block)
        return pltpu.make_async_remote_copy(
            src_ref=dn.at[rows, :], dst_ref=dn_sib.at[rows, :], send_sem=send.at[i],
            recv_sem=recv.at[i], device_id=sibling, device_id_type=MESH)

    def forward(i):
        rows = pl.ds(pl.multiple_of(i * block, block), block)
        mixed = jnp.concatenate([ctx_ref[n, rows, :] for n in range(ctx_ref.shape[0])], axis=1)
        middle = xs_ref[rows, :].astype(f32) + nn(mixed, wo_ref[...])
        mid[rows, :] = middle
        normed = (middle * inverse_rms(middle) * gain).astype(bf16)
        nff[rows, :] = normed
        gate = nn(normed, wgu_ref[:, :ff])
        up = nn(normed, wgu_ref[:, ff:])
        square = gate * gate
        bent = jnp.tanh(lift * gate * (1.0 + 0.044715 * square))
        halved = 0.5 * (1.0 + bent)
        gelu = gate * halved
        slope = halved + 0.5 * gate * (1.0 - bent * bent) * (
            lift * (1.0 + 3 * 0.044715 * square))
        hidden = (gelu * up).astype(bf16)
        hid[rows, :] = hidden
        dgu[rows, :ff] = (up * slope).astype(bf16)
        dgu[rows, ff:] = gelu.astype(bf16)
        out[rows, :] = (0.5 * middle + nn(hidden, wd_ref[...])).astype(bf16)

    def backward(i):
        rows = pl.ds(pl.multiple_of(i * block, block), block)
        d_hidden = nt(cs_ref[rows, :], wd_ref[...])
        d_gate = (d_hidden * dgu[rows, :ff].astype(f32)).astype(bf16)
        d_up = (d_hidden * dgu[rows, ff:].astype(f32)).astype(bf16)
        dgu[rows, :ff] = d_gate
        dgu[rows, ff:] = d_up
        dn[rows, :] = (nt(d_gate, wgu_ref[:, :ff]) + nt(d_up, wgu_ref[:, ff:])).astype(bf16)
        exchange(i).start()

    looped(0, tiles, forward)
    for copy in comes:
        copy.wait()
    rows_home.give()
    looped(0, 1, backward)
    rows_home.keep()
    looped(1, tiles, backward)

    def down(i, carry):
        cols = pl.ds(pl.multiple_of(i * block, block), block)
        gd_ref[cols, :] = tn(hid[:, cols], cs_ref[...]).astype(bf16)
        return carry

    lax.fori_loop(0, ff // block, down, 0)

    def settle(i, total):
        rows = pl.ds(pl.multiple_of(i * block, block), block)
        exchange(i).wait()
        mine = dn[rows, :].astype(f32)
        grad = mine + dn_sib[rows, :].astype(f32)
        middle = mid[rows, :]
        s = inverse_rms(middle)
        unit = middle * s
        scaled = gain * grad
        d_middle = cs_ref[rows, :].astype(f32) + s * (
            scaled - unit * jnp.mean(scaled * unit, axis=-1, keepdims=True))
        low = d_middle.astype(bf16)
        datt_ref[rows, :] = low
        d_context = nt(low, wo_ref[half_cols, :]).astype(bf16).astype(f32)
        scaled = (d_context * linv_ref[rows, :]).astype(bf16).astype(f32)
        against = scaled * ctx32_ref[rows, :]
        lane = iota((block, lanes), 1)
        for n in range(dos_ref.shape[0]):
            cols = slice((n // 2) * lanes, (n // 2 + 1) * lanes)
            mine_lanes = (lane < lanes // 2) == (n % 2 == 0)
            spare = lanes // 2 if n % 2 == 0 else 0
            delta = jnp.sum(jnp.where(mine_lanes, against[:, cols], 0.0), axis=1, keepdims=True)
            high = delta.astype(bf16).astype(f32)
            extra = jnp.where(lane == spare, -high,
                              jnp.where(lane == spare + 1, high - delta, 0.0))
            dos_ref[n, rows, :] = jnp.where(mine_lanes, scaled[:, cols], extra).astype(bf16)
        return total + jnp.sum(mine * unit, axis=0, keepdims=True)

    ggain_ref[...] = lax.fori_loop(0, tiles, settle, jnp.zeros((1, width), f32))
    for n in range(0, ctx_ref.shape[0], 2):
        mixed = jnp.concatenate((ctx_ref[n], ctx_ref[n + 1]), axis=1)
        go_ref[n * lanes : (n + 2) * lanes, :] = tn(mixed, datt_ref[:, half_cols]).astype(bf16)

    def gate_up(i, carry):
        cols = pl.ds(pl.multiple_of(i * block, block), block)
        ggu_ref[cols, :] = tn(nff[:, cols], dgu[...]).astype(bf16)
        return carry

    lax.fori_loop(0, width // block, gate_up, 0)
    rows_home.finish()


def feed(fsdp_count, piece, idx_row, ctx, ctx32, linv, xs, cs, w_out, gains, w_gu, w_down):
    rows, width = xs.shape
    ff = w_down.shape[0]
    part = width // 2
    shape = (2, fsdp_count, piece, width)
    dma = pltpu.SemaphoreType.DMA
    vm = pl.BlockSpec(memory_space=pltpu.VMEM)
    hbm = pl.BlockSpec(memory_space=pl.ANY)
    return pl.pallas_call(
        functools.partial(feed_kernel, fsdp_count),
        in_specs=[vm, vm, hbm, hbm, vm, hbm, vm, vm, vm, vm],
        out_specs=(hbm, *(vm,) * 6),
        out_shape=(
            jax.ShapeDtypeStruct(shape, bf16),
            jax.ShapeDtypeStruct((width, 2 * ff), bf16),
            jax.ShapeDtypeStruct((ff, width), bf16),
            jax.ShapeDtypeStruct((rows, width), bf16),
            jax.ShapeDtypeStruct((ctx.shape[0], rows, lanes), bf16),
            jax.ShapeDtypeStruct((width, part), bf16),
            jax.ShapeDtypeStruct((1, width), f32),
        ),
        scratch_shapes=[
            pltpu.VMEM((rows, width), bf16),
            pltpu.VMEM((rows, width), f32),
            pltpu.VMEM((rows, width), bf16),
            pltpu.VMEM((rows, ff), bf16),
            pltpu.VMEM((rows, 2 * ff), bf16),
            pltpu.VMEM((rows, width), bf16),
            pltpu.VMEM((rows, width), bf16),
            pltpu.VMEM(shape, bf16),
            pltpu.VMEM(shape, bf16),
            dma((rows // block,)), dma((rows // block,)), dma((2,)), dma((2,)),
            dma((2, fsdp_count)), dma((2, fsdp_count)), dma,
            pltpu.VMEM((rows, part), f32),
            pltpu.VMEM((rows, part), f32),
            pltpu.VMEM((rows, width), bf16),
            dma((3,)),
        ],
        compiler_params=pltpu.CompilerParams(
            vmem_limit_bytes=vmem_limit, collective_id=2, has_side_effects=True),
        name="feed",
    )(idx_row, ctx, ctx32, linv, xs, cs, w_out, gains, w_gu, w_down)


class Scattering:
    def __init__(self, fsdp_count, grads, in_y, in_x, turned, in_z, final, send, recv):
        self.f, self.y, self.c = place()
        self.count = fsdp_count
        self.planes = fsdp_count // 2
        self.z, self.x = self.f // 2, self.f % 2
        self.grads, self.in_y, self.in_x = grads, in_y, in_x
        self.turned, self.in_z, self.final = turned, in_z, final
        self.send, self.recv = send, recv
        self.x_side = device(self.z * 2 + 1 - self.x, self.y, self.c)
        self.y_side = device(self.f, 1 - self.y, self.c)
        self.sibling = device(self.f, self.y, 1 - self.c)

    def part(self, n, f, k):
        return self.grads[n].at[f * 4 + k]

    def plane(self, j):
        return lax.rem(self.z + j, self.planes)

    def order(self):
        return [*range(1, self.planes), 0]

    def move(self, n, kind, i, j, src, dst, where):
        return push(src, dst, self.send.at[n, kind, i, j], self.recv.at[n, kind, i, j], where)

    def along_y(self, n, z, x):
        return self.move(n, 0, z, x, self.part(n, 2 * z + x, 2 * (1 - self.y)),
                         self.in_y[n].at[z, x], self.y_side)

    def along_x(self, n, z, y):
        return self.move(n, 1, z, y, self.part(n, 2 * z + 1 - self.x, 2 * y + 1),
                         self.in_x[n].at[z, y], self.x_side)

    def turn(self, n, z, side):
        if side == 0:
            return self.move(n, 2, z, 0, self.in_y[n].at[z, 1 - self.x],
                             self.turned[n].at[z, 0], self.x_side)
        return self.move(n, 2, z, 1, self.in_x[n].at[z, 1 - self.y], self.turned[n].at[z, 1],
                         self.y_side)

    def summed(self, n, z, side):
        return (self.in_y[n].at[z, self.x], self.in_x[n].at[z, self.y])[side]

    def out_z(self, n, z, side):
        return push(self.summed(n, z, side), self.in_z[n].at[self.z, side],
                    self.send.at[n, 3, z, side], self.recv.at[n, 3, self.z, side],
                    device(2 * z + self.x, self.y, self.c))

    def come_z(self, n, z, side):
        return push(self.summed(n, z, side), self.in_z[n].at[z, side],
                    self.send.at[n, 3, z, side], self.recv.at[n, 3, z, side],
                    device(2 * z + self.x, self.y, self.c))

    def last_y(self, n, side, mine):
        y = self.y if mine else 1 - self.y
        here = self.final[n].at[self.c, 2 * y + side]
        return self.move(n, 4, 0, side, here, here, self.y_side)

    def last_core(self, n, mine):
        here = self.final[n].at[self.c if mine else 1 - self.c]
        return self.move(n, 5, 0, 0, here, here, self.sibling)

    def each(self, body):
        for n in range(len(self.grads)):
            body(n)

    def start(self, j):
        z = self.plane(j)
        for n in range(len(self.grads)):
            for k in range(2):
                self.along_y(n, z, k).start()
                self.along_x(n, z, k).start()

    def fold(self, j):
        z = self.plane(j)
        for n in range(len(self.grads)):
            for k in range(2):
                self.along_y(n, z, k).wait_recv()
                add_to(self.in_y[n].at[z, k], self.part(n, 2 * z + k, 2 * self.y))
            self.turn(n, z, 0).start()
            for k in range(2):
                self.along_x(n, z, k).wait_recv()
                add_to(self.in_x[n].at[z, k], self.part(n, 2 * z + self.x, 2 * k + 1))
            self.turn(n, z, 1).start()

    def plane_sum(self, j):
        z = self.plane(j)
        for n in range(len(self.grads)):
            for side in range(2):
                self.turn(n, z, side).wait_recv()
                add_to(self.summed(n, z, side), self.turned[n].at[z, side])
                if j:
                    self.out_z(n, z, side).start()

    def total(self):
        for n in range(len(self.grads)):
            for side in range(2):
                value = self.summed(n, self.z, side)[...].astype(f32)
                for j in range(1, self.planes):
                    z = self.plane(j)
                    self.come_z(n, z, side).wait_recv()
                    value = value + self.in_z[n][z, side].astype(f32)
                self.final[n][self.c, 2 * self.y + side] = value.astype(bf16)
                self.last_y(n, side, True).start()

    def share(self):
        for n in range(len(self.grads)):
            for side in range(2):
                self.last_y(n, side, False).wait_recv()
            self.last_core(n, True).start()

    def finish(self):
        for n in range(len(self.grads)):
            self.last_core(n, False).wait_recv()
            self.last_core(n, True).wait_send()
            for side in range(2):
                self.last_y(n, side, True).wait_send()
            for j in range(self.planes):
                z = self.plane(j)
                for k in range(2):
                    self.along_y(n, z, k).wait_send()
                    self.along_x(n, z, k).wait_send()
                    self.turn(n, z, k).wait_send()
                    if j:
                        self.out_z(n, z, k).wait_send()

    def steps(self, together):
        order = self.order()
        if together:
            return [
                lambda: [self.start(j) for j in order],
                lambda: [self.fold(j) for j in order],
                lambda: [self.plane_sum(j) for j in order],
                self.total, self.share,
            ]
        ahead = 2
        out = [lambda: [self.start(j) for j in order[:ahead]]]

        def fold(n):
            self.fold(order[n])
            if n + ahead < len(order):
                self.start(order[n + ahead])

        for n in range(len(order)):
            out.append(functools.partial(fold, n))
            if n:
                out.append(functools.partial(self.plane_sum, order[n - 1]))
        return out + [functools.partial(self.plane_sum, order[-1]), self.total, self.share]


def add_to(here, other):
    here[...] = (here[...].astype(f32) + other[...].astype(f32)).astype(bf16)


def back_kernel(
    fsdp_count, scatters, idx_ref, xs_ref, gains_ref, ggain_ref, w_ref, dos_ref, qkv_ref, datt_ref,
    pl_ref, ps_ref, *refs,
):
    if scatters:
        grads = refs[:3]
        refs = refs[3:]
    tokens_ref, small_ref, *refs = refs
    if scatters:
        outs, refs = refs[:7], refs[7:]
        gqkv_refs, refs = refs[:3], refs[3:]
    else:
        gqkv_refs, refs = refs[:3], refs[3:]
    (ybuf, normed, dqkv, table, qs, ds_l, ds_s, p_l, p_s, acc, va, kt, dq_t, given, taken,
     smalls, load, p_sem, pass_send, pass_recv, home_send, home_recv, own,
     small_send, small_recv, small_pass, small_back, *refs) = refs
    f, p, c = place()
    sibling = device(f, p, 1 - c)
    rows_all, width = xs_ref.shape
    part = width // 2
    pairs = part // lanes
    short = rows_all - longest
    half = lanes // 2
    gain_attn = gains_ref[0:1, :]

    def p_copies(head):
        pair, h = head // 2, head % 2
        return [
            pltpu.make_async_copy(pl_ref.at[pair, :, h * longest : (h + 1) * longest],
                                  p_l.at[h], p_sem.at[0, h]),
            pltpu.make_async_copy(ps_ref.at[pair, :, h * short : (h + 1) * short],
                                  p_s.at[h], p_sem.at[1, h]),
        ]

    for head in range(2):
        for copy in p_copies(head):
            copy.start()
    greet_all(fsdp_count)
    sets = []
    if scatters:
        for group in range(1 + pairs):
            arrays = grads if group == 0 else (gqkv_refs[group - 1],)
            count = len(arrays)
            bufs = [refs[k * count : (k + 1) * count] for k in range(5)]
            send, recv = refs[5 * count : 5 * count + 2]
            refs = refs[5 * count + 2 :]
            sets.append(Scattering(fsdp_count, arrays, *bufs, send, recv))
    steps = [group.steps(n > 0) for n, group in enumerate(sets)]

    def poll(*which):
        for n in which:
            if scatters and steps[n]:
                steps[n].pop(0)()

    places = {1: (0,), 4: (0,), 6: (0,), 8: (0,), 10: (0,), 12: (0,), 13: (0,), 14: (1,), 16: (0,), 17: (1,)}
    poll(0)

    home = Homing(fsdp_count, taken, tokens_ref, home_send, home_recv, own.at[0])
    rows_home = Returning(idx_ref, ybuf, given, taken, pass_send, pass_recv, home)

    def norm_tile(i):
        rows = pl.ds(pl.multiple_of(i * block, block), block)
        x = xs_ref[rows, :].astype(f32)
        normed[rows, :] = (x * inverse_rms(x) * gain_attn).astype(bf16)

    looped(0, rows_all // block, norm_tile)

    lane = iota((rows_all, lanes), 1)
    buckets = band_buckets()
    small_ref_rows = iota((lanes // 4, lanes), 1)
    bias = jnp.zeros((lanes // 4, lanes), f32)
    for pair in range(pairs):
        cols = [slice(kind * part + pair * lanes, kind * part + (pair + 1) * lanes)
                for kind in range(3)]
        queries = qkv_ref[:, cols[0]]
        keys = qkv_ref[:, cols[1]]
        values = qkv_ref[:, cols[2]]
        kt[...] = jnp.transpose(keys.astype(f32)).astype(bf16)
        for h in range(2):
            head = 2 * pair + h
            own_lanes = (lane < half) == (h == 0)
            spare = half if h == 0 else 0
            qs[...] = jnp.where(own_lanes, queries, jnp.zeros_like(queries))
            ones = jnp.where((lane == spare) | (lane == spare + 1), 1.0, 0.0)
            va[...] = jnp.where(own_lanes, values.astype(f32), ones).astype(bf16)
            table[...] = jnp.zeros_like(table)
            for copy in p_copies(head):
                copy.wait()

            def strip(base, count, p_buf, ds_buf, b):
                here = pl.ds(pl.multiple_of(base + b * block, block), block)
                spot = pl.ds(pl.multiple_of(b * block, block), block)
                d_weights = nt(va[base : base + count, :], dos_ref[head, here, :])
                d_logits = p_buf[h, :, spot].astype(f32) * d_weights
                window = pl.ds(pl.multiple_of(far - b * block, block), count)
                table[window, :] = table[window, :] + d_logits
                low = d_logits.astype(bf16)
                ds_buf[:, spot] = low
                part_rows = slice(h * half, (h + 1) * half)
                dq_t[part_rows, here] = nn(kt[part_rows, base : base + count], low)

            looped(0, longest // block, functools.partial(strip, 0, longest, p_l, ds_l))
            poll(*places.get(3 * head, ()))
            looped(0, short // block, functools.partial(strip, longest, short, p_s, ds_s))
            poll(*places.get(3 * head + 1, ()))
            for base, count, p_buf, ds_buf in ((0, longest, p_l, ds_l), (longest, short, p_s, ds_s)):
                rows = slice(base, base + count)
                clean = jnp.where(own_lanes[rows], dos_ref[head, rows, :].astype(f32), 0.0)
                d_value = nn(p_buf[h], clean.astype(bf16))
                d_key = nn(ds_buf[...], qs[rows, :])
                if h == 0:
                    acc[0, rows, :] = d_value
                    acc[1, rows, :] = d_key
                else:
                    dqkv[rows, cols[2]] = (acc[0, rows, :] + d_value).astype(bf16)
                    dqkv[rows, cols[1]] = (acc[1, rows, :] + d_key).astype(bf16)
            if head + 2 < 2 * pairs:
                for copy in p_copies(head + 2):
                    copy.start()
            before = far - lanes
            after = far + 3 * lanes
            band = table[before : before + 3 * lanes, :lanes] + table[far : far + 3 * lanes, lanes:]
            left = jnp.sum(table[:before, :lanes] + table[:before, lanes:], axis=0, keepdims=True)
            left = left + jnp.sum(table[before:far, lanes:], axis=0, keepdims=True)
            right = jnp.sum(table[after:, :lanes] + table[after:, lanes:], axis=0, keepdims=True)
            right = right + jnp.sum(table[after - lanes : after, :lanes], axis=0, keepdims=True)
            for label in range(lanes // 4):
                line = jnp.sum(jnp.where(buckets == label, band, 0.0), axis=0, keepdims=True)
                if label == 15:
                    line = line + left
                if label == 31:
                    line = line + right
                table[label : label + 1, :lanes] = line
            sums = jnp.sum(table[: lanes // 4, :lanes], axis=1, keepdims=True)
            bias = bias + jnp.where(small_ref_rows == c * 2 * pairs + head, sums, 0.0)
            poll(*places.get(3 * head + 2, ()))
        dqkv[:, cols[0]] = jnp.transpose(dq_t[...]).astype(bf16)
        for kind in range(3):
            grad = tn(normed[...], dqkv[:, cols[kind]])
            grad = grad.reshape(*gqkv_refs[pair].shape[:-1], lanes)
            gqkv_refs[pair][..., kind * lanes : (kind + 1) * lanes] = grad.astype(bf16)
        if pair == pairs - 1:
            reload = pltpu.make_async_copy(datt_ref, normed, load)
            reload.start()
        poll(1 + pair)

    def tile(i, total):
        rows = slice(i * block, (i + 1) * block)
        x = xs_ref[rows, :].astype(f32)
        s = inverse_rms(x)
        unit = x * s
        grad = nt(dqkv[rows, :], w_ref[...])
        scaled = gain_attn * grad
        y = 0.5 * normed[rows, :].astype(f32) + s * (
            scaled - unit * jnp.mean(scaled * unit, axis=-1, keepdims=True))
        ybuf[rows, :] = y.astype(bf16)
        return total + jnp.sum(grad * unit, axis=0, keepdims=True)

    grad_gain = jnp.zeros((1, width), f32)
    reload.wait()
    for i in range(rows_all // block):
        grad_gain = tile(i, grad_gain)
    rows_home.give()
    quarter = lanes // 4
    small_ref[0:quarter, :] = bias
    small_ref[quarter:, :] = jnp.zeros((small_ref.shape[0] - quarter, lanes), f32)
    for j in range(width // lanes):
        cols = slice(j * lanes, (j + 1) * lanes)
        small_ref[quarter + j : quarter + j + 1, :] = grad_gain[:, cols]
        row = quarter + 8 + j
        small_ref[row : row + 1, :] = ggain_ref[:, cols]
    dealt = Dealing(fsdp_count, small_ref, smalls, small_send, small_recv, small_pass, small_back,
                    own.at[1])
    dealt.start()
    rows_home.keep()
    poll(0, 2, 3, 1, 0, 2, 3, 1, 2, 3, 2, 3)
    dealt.forward()
    dealt.finish()
    dealt.sent()
    dealt.passed()

    def gather_small(k, total):
        return total + smalls[k // (2 * fsdp_count), (k // fsdp_count) % 2, k % fsdp_count]

    small_ref[...] = lax.fori_loop(0, 4 * fsdp_count, gather_small,
                                   jnp.zeros(small_ref.shape, f32))
    for group in sets:
        group.finish()
    if scatters:
        gate, up, down, out_w, query, key, value = outs
        gu, dn, wo = sets[0].final
        ff = gu.shape[3] // 2
        cut = ff // fsdp_count
        for k in range(4):
            for side in range(2):
                rows = gu.shape[2]
                rows = slice(k * rows, (k + 1) * rows)
                for g in range(fsdp_count):
                    there = slice((2 * g + side) * cut, (2 * g + side + 1) * cut)
                    gate[rows, there] = gu[side, k, :, g * cut : (g + 1) * cut].astype(f32)
                    up[rows, there] = gu[side, k, :, ff + g * cut : ff + (g + 1) * cut].astype(f32)
                many = dn.shape[2]
                first = (side * 4 + k) * many
                down[first : first + many, :] = dn[side, k].astype(f32)
                out_w[rows, side * part : (side + 1) * part] = wo[side, k].astype(f32)
                for pair in range(pairs):
                    [one] = sets[1 + pair].final
                    there = slice(side * part + pair * lanes, side * part + (pair + 1) * lanes)
                    for kind, ref in enumerate((query, key, value)):
                        ref[rows, there] = one[side, k, :, kind * lanes : (kind + 1) * lanes].astype(
                            f32)
    rows_home.finish()


def back(fsdp_count, piece, scatters, idx_row, xs, gains, ggain, w_qkv, datt, dos, qkv,
         p_long, p_short, grads):
    rows, width = xs.shape
    part = width // 2
    pairs = part // lanes
    short = rows - longest
    vm = pl.BlockSpec(memory_space=pltpu.VMEM)
    hbm = pl.BlockSpec(memory_space=pl.ANY)
    dma = pltpu.SemaphoreType.DMA
    shape = (2, fsdp_count, piece, width)
    own_rows = width // fsdp_count
    out_shape = [
        jax.ShapeDtypeStruct(shape, bf16), jax.ShapeDtypeStruct((48, lanes), f32),
    ]
    out_specs = [hbm, vm]
    if scatters:
        ff = grads[0].shape[1]
        out_shape += [jax.ShapeDtypeStruct((own_rows, ff), f32)] * 2
        out_shape += [jax.ShapeDtypeStruct((2 * grads[1].shape[0] // fsdp_count, width), f32)]
        out_shape += [jax.ShapeDtypeStruct((own_rows, width), f32)] * 4
        out_specs += [vm] * 7
    gqkv = [jax.ShapeDtypeStruct((width, 3 * lanes), bf16)] * pairs
    scratch = []
    if scatters:
        grads = tuple(g.reshape(4 * fsdp_count, -1, g.shape[1]) for g in grads)
        scratch = [pltpu.VMEM((4 * fsdp_count, own_rows // 4, 3 * lanes), bf16)] * pairs
    if not scatters:
        out_shape += gqkv
        out_specs += [vm] * pairs
    scratch += [
        pltpu.VMEM((rows, width), bf16),
        pltpu.VMEM((rows, width), bf16),
        pltpu.VMEM((rows, 3 * part), bf16),
        pltpu.VMEM((reach, block), f32),
        pltpu.VMEM((rows, lanes), bf16),
        pltpu.VMEM((longest, longest), bf16),
        pltpu.VMEM((short, short), bf16),
        pltpu.VMEM((2, longest, longest), bf16),
        pltpu.VMEM((2, short, short), bf16),
        pltpu.VMEM((2, rows, lanes), f32),
        pltpu.VMEM((rows, lanes), bf16),
        pltpu.VMEM((lanes, rows), bf16),
        pltpu.VMEM((lanes, rows), f32),
        pltpu.VMEM(shape, bf16),
        pltpu.VMEM(shape, bf16),
        pltpu.VMEM((2, 2, fsdp_count, 48, lanes), f32),
        dma, dma((2, 2)), dma((2,)), dma((2,)),
        dma((2, fsdp_count)), dma((2, fsdp_count)), dma((2,)),
        *[dma((2 * fsdp_count,))] * 4,
    ]
    if scatters:
        planes = fsdp_count // 2
        for quarters in ([g.shape[1:] for g in grads], *[[(own_rows // 4, 3 * lanes)]] * pairs):
            for lead in ((planes, 2), (planes, 2), (planes, 2), (planes, 2), (2, 4)):
                scratch += [pltpu.VMEM((*lead, *q), bf16) for q in quarters]
            scratch += [dma((len(quarters), 6, planes, 2))] * 2
    return pl.pallas_call(
        functools.partial(back_kernel, fsdp_count, scatters),
        in_specs=[vm] * 7 + [hbm] * 3 + [vm] * (len(grads) if scatters else 0),
        out_specs=tuple(out_specs),
        out_shape=tuple(out_shape),
        scratch_shapes=scratch,
        compiler_params=pltpu.CompilerParams(
            vmem_limit_bytes=vmem_limit, collective_id=1, has_side_effects=True),
        name="back",
    )(idx_row, xs, gains, ggain, w_qkv, dos, qkv, datt, p_long, p_short,
      *(grads if scatters else ()))


def shards(
    tokens, cotangent, lengths, dealing, gain_attn, w_query, w_key, w_value, w_out, bias_table,
    gain_ff, w_gate, w_up, w_down,
):
    fsdp_count = lax.axis_size("fsdp")
    sp_count = lax.axis_size("sp")
    micro_count, token_rows, width = tokens.shape
    piece = token_rows // fsdp_count
    group_rows = token_rows * sp_count
    local_heads = bias_table.shape[1]
    heads = local_heads * sp_count
    part = width // 2
    s = lax.axis_index("sp")
    p, c = s // 2, s % 2
    full_piece = -(-piece // 8) * 8

    def pieces(value):
        value = value.reshape(micro_count, fsdp_count, piece, width)
        return jnp.pad(value, ((0, 0), (0, 0), (0, full_piece - piece), (0, 0)))

    order = lax.dynamic_index_in_dim(dealing[:, 0], p, 0, keepdims=False)
    length = lax.dynamic_index_in_dim(lengths[:, 0], p, 0, keepdims=False)
    first_long = length[0] == longest
    start = jnp.where(first_long, 0, jnp.where(length[1] == longest, length[0],
                                               length[0] + length[1]))
    bound = jnp.where(first_long, length[1], length[0]).reshape(1)
    short = group_rows - longest
    head_part = lax.dynamic_slice_in_dim(order, start, longest, 0)
    tail = jnp.where(jnp.arange(short) < start, order[:short], order[longest:])
    order = jnp.concatenate((head_part, tail))
    source, within = order // token_rows, order % token_rows
    idx = ((source % 2) * 2 + source // 2) * fsdp_count + within // piece
    idx = idx * full_piece + within % piece

    def half_cols(weight):
        return lax.dynamic_slice_in_dim(weight, c * part, part, 1)

    def half_ff(weight):
        split = weight.reshape(weight.shape[0], fsdp_count, 2, -1)
        return lax.dynamic_index_in_dim(split, c, 2, keepdims=False).reshape(weight.shape[0], -1)

    def gather(value, axis=0):
        return lax.all_gather(value, "fsdp", axis=axis, tiled=True)

    def line(value):
        return jnp.pad(value.astype(f32), ((0, 0), (0, lanes - value.shape[1])))

    small = jnp.concatenate([line(gain_attn[None]), line(gain_ff[None]), line(bias_table.T)])
    small = jnp.pad(small, ((0, 8 - small.shape[0]), (0, 0)))
    down_rows = w_down.shape[0] // 2
    weights = (
        jnp.concatenate([half_cols(w) for w in (w_query, w_key, w_value)], axis=1),
        w_out,
        jnp.concatenate([half_ff(w) for w in (w_gate, w_up)], axis=1),
        lax.dynamic_slice_in_dim(w_down, c * down_rows, down_rows, 0),
    )
    gathers = fsdp_count == 8 and all(w.shape[0] % 32 == 0 for w in weights)
    if not gathers:
        weights = tuple(gather(w) for w in weights)
    idx_row = idx.reshape(1, -1)
    args = (bound, idx_row, small, pieces(tokens), pieces(cotangent))
    xs, cs, qkv, p_long, p_short, ctx, ctx32, linv, gains, w_qkv, *late = attend(
        fsdp_count, gathers, *args, *(weights if gathers else weights[:1]))
    wo, w_gu, wd = late if gathers else weights[1:]
    buckets = band_buckets()
    output, grad_gu, grad_d, datt, dos, grad_o, grad_gain_ff = feed(
        fsdp_count, full_piece, idx_row, ctx, ctx32, linv, xs, cs, wo, gains, w_gu, wd)
    grad_tokens, small, *grads = back(
        fsdp_count, full_piece, gathers, idx_row, xs, gains, grad_gain_ff, w_qkv, datt,
        dos, qkv, p_long, p_short, (grad_gu, grad_d, grad_o))
    output, grad_tokens = (x[:, :, :piece].reshape(tokens.shape) for x in (output, grad_tokens))
    own_gain = width // fsdp_count
    f = lax.axis_index("fsdp")
    labels = bias_table.shape[0]
    bias_grad = lax.dynamic_slice_in_dim(small[:labels], s * local_heads, local_heads, 1)
    gain_grads = [
        lax.dynamic_slice_in_dim(
            small[first : first + width // lanes].reshape(-1), f * own_gain, own_gain, 0)
        for first in (labels, labels + 8)
    ]
    if not gathers:
        grads = scatter_rows(fsdp_count, c, (grad_gu, grad_d, grad_o, *grads))
    grad_gate, grad_up, grad_down, grad_out, grad_query, grad_key, grad_value = grads
    return (
        output, grad_tokens, gain_grads[0], grad_query, grad_key, grad_value, grad_out, bias_grad,
        gain_grads[1], grad_gate, grad_up, grad_down,
    )


def scatter_rows(fsdp_count, c, partial_grads):
    sibling = [(0, 1), (1, 0), (2, 3), (3, 2)]
    across = [(0, 2), (2, 0), (1, 3), (3, 1)]
    shares = [lax.psum_scatter(v, "fsdp", scatter_dimension=0, tiled=True) for v in partial_grads]
    shares = [v.astype(f32) + lax.ppermute(v, "sp", across).astype(f32) for v in shares]
    shares = [v.astype(bf16) for v in shares]
    others = [lax.ppermute(v, "sp", sibling) for v in shares]
    sides = [
        (jnp.where(c == 0, v, w).astype(f32), jnp.where(c == 0, w, v).astype(f32))
        for v, w in zip(shares, others)
    ]
    gu, down, out, *qkv = sides
    rows = gu[0].shape[0]
    ff = gu[0].shape[1] // 2

    def ff_cols(which):
        cut = [x[:, which * ff : (which + 1) * ff].reshape(rows, fsdp_count, 1, -1) for x in gu]
        return jnp.concatenate(cut, axis=2).reshape(rows, -1)

    def proj(kind):
        return jnp.concatenate(
            [pair[side][:, kind * lanes : (kind + 1) * lanes] for side in range(2) for pair in qkv],
            axis=1)

    return (ff_cols(0), ff_cols(1), jnp.concatenate(down), jnp.concatenate(out, axis=1),
            proj(0), proj(1), proj(2))


def solution(mesh):
    return jax.shard_map(
        shards,
        mesh=mesh,
        in_specs=(
            P(None, ("fsdp", "sp"), None), P(None, ("fsdp", "sp"), None),
            P(None, "fsdp", None), P(None, "fsdp", None),
            P("fsdp"), P("fsdp", None), P("fsdp", None), P("fsdp", None), P("fsdp", None),
            P(None, "sp"), P("fsdp"), P("fsdp", None), P("fsdp", None), P("fsdp", None),
        ),
        out_specs=(
            P(None, ("fsdp", "sp"), None), P(None, ("fsdp", "sp"), None),
            P("fsdp"), P("fsdp", None), P("fsdp", None), P("fsdp", None), P("fsdp", None),
            P(None, "sp"), P("fsdp"), P("fsdp", None), P("fsdp", None), P("fsdp", None),
        ),
        check_vma=False,
    )
```

```python
import functools
import math

import jax
import jax.numpy as jnp
from jax import lax
from jax.experimental import pallas as pl
from jax.experimental.pallas import tpu as pltpu
from jax.sharding import PartitionSpec as P

bucket_edges = (1, 2, 3, 4, 5, 6, 7, 8, 12, 16, 23, 32, 46, 64, 91)
epsilon = 1e-06
longest = 1024
lanes = 128
block = 256
far = 768
reach = 1792
MESH = pl.DeviceIdType.MESH
f32 = jnp.float32
bf16 = jnp.bfloat16
vmem_limit = 62 * 2**20


def nn(left, right):
    return jnp.dot(left, right, preferred_element_type=f32)


def nt(left, right):
    return lax.dot_general(left, right, (((1,), (1,)), ((), ())), preferred_element_type=f32)


def tn(left, right):
    return lax.dot_general(left, right, (((0,), (0,)), ((), ())), preferred_element_type=f32)


def iota(shape, dim):
    return lax.broadcasted_iota(jnp.int32, shape, dim)


def one_hot(column, row):
    return jnp.where(column == row, 1.0, 0.0).astype(bf16)


def inverse_rms(values):
    return lax.rsqrt(jnp.mean(values * values, axis=-1, keepdims=True) + epsilon)


def bucket_index(offset):
    distance = jnp.abs(offset)
    bucket_sum = jnp.where(offset > 0, 16, 0).astype(jnp.int32)
    for border in bucket_edges:
        bucket_sum = bucket_sum + (distance >= border).astype(jnp.int32)
    return bucket_sum


def band_buckets():
    shape = (3 * lanes, lanes)
    return bucket_index(iota(shape, 0) - lanes - iota(shape, 1))


def whole_spec(shape, space=pltpu.VMEM):
    return pl.BlockSpec(shape, lambda *_: (0,) * len(shape), memory_space=space,
                        pipeline_mode=pl.Buffered(1))


def place():
    f = lax.axis_index("fsdp")
    s = lax.axis_index("sp")
    return f, s // 2, s % 2


def device(f, p, c):
    return {"fsdp": f, "sp": 2 * p + c}


def signal(barrier, where):
    pl.semaphore_signal(barrier, inc=1, device_id=where, device_id_type=MESH)


def greet_all(fsdp_count):
    f, p, c = place()
    barrier = pltpu.get_barrier_semaphore()
    peers = 2 * fsdp_count
    mine = p * fsdp_count + f

    def greet(i, carry):
        k = lax.rem(mine + i, peers)
        signal(barrier, device(k % fsdp_count, k // fsdp_count, c))
        return carry

    lax.fori_loop(1, peers, greet, 0)
    signal(barrier, device(f, p, 1 - c))
    pl.semaphore_wait(barrier, peers)


def push(src, dst, send, recv, where):
    return pltpu.make_async_remote_copy(
        src_ref=src, dst_ref=dst, send_sem=send, recv_sem=recv, device_id=where,
        device_id_type=MESH)


def looped(first, last, body):
    def step(i, carry):
        body(i)
        return carry

    lax.fori_loop(first, last, step, 0)


class Dealing:
    def __init__(self, fsdp_count, src, dst, send, recv, pass_send, pass_recv, own):
        self.f, self.p, self.c = place()
        self.count = fsdp_count
        self.peers = 2 * fsdp_count
        self.mine = self.p * fsdp_count + self.f
        self.src, self.dst, self.send, self.recv = src, dst, send, recv
        self.pass_send, self.pass_recv, self.own = pass_send, pass_recv, own

    def source(self, k):
        return self.src.at[k // self.count, k % self.count] if len(self.src.shape) == 4 else self.src

    def out(self, k):
        where = device(k % self.count, k // self.count, self.c)
        return push(self.source(k), self.dst.at[self.c, self.p, self.f], self.send.at[k],
                    self.recv.at[self.mine], where)

    def come(self, k):
        where = device(k % self.count, k // self.count, self.c)
        return push(self.source(k), self.dst.at[self.c, k // self.count, k % self.count],
                    self.send.at[k], self.recv.at[k], where)

    def onward(self, k, side):
        here = self.dst.at[side, k // self.count, k % self.count]
        return push(here, here, self.pass_send.at[k], self.pass_recv.at[k],
                    device(self.f, self.p, 1 - self.c))

    def local(self):
        return pltpu.make_async_copy(
            self.source(self.mine), self.dst.at[self.c, self.p, self.f], self.own)

    def start(self):
        looped(1, self.peers, lambda i: self.out(lax.rem(self.mine + i, self.peers)).start())
        self.local().start()

    def forward(self):
        self.local().wait()
        self.onward(self.mine, self.c).start()

        def one(i):
            k = lax.rem(self.mine + self.peers - i, self.peers)
            self.come(k).wait_recv()
            self.onward(k, self.c).start()

        looped(1, self.peers, one)

    def sent(self):
        looped(1, self.peers, lambda i: self.out(lax.rem(self.mine + i, self.peers)).wait_send())

    def finish(self):
        looped(0, self.peers, lambda k: self.onward(k, 1 - self.c).wait_recv())

    def passed(self):
        looped(0, self.peers, lambda k: self.onward(k, self.c).wait_send())


class Gathering:
    def __init__(self, fsdp_count, srcs, dsts, sends, recvs, own):
        self.f, self.y, self.c = place()
        self.count = fsdp_count
        self.planes = fsdp_count // 2
        self.z, self.x = self.f // 2, self.f % 2
        self.srcs, self.dsts, self.sends, self.recvs, self.own = srcs, dsts, sends, recvs, own
        self.x_side = device(self.z * 2 + 1 - self.x, self.y, self.c)
        self.y_side = device(self.f, 1 - self.y, self.c)

    def rows(self, dst, f, k):
        total = dst.shape[0] // self.count
        quarter = total // 4
        return dst.at[pl.ds(pl.multiple_of(f * total + k * quarter, 8), quarter)]

    def copies(self, link, f, k, where, fresh=False):
        out = []
        for n, (src, dst) in enumerate(zip(self.srcs, self.dsts)):
            there = self.rows(dst, f, k)
            quarter = src.shape[0] // 4
            here = src.at[pl.ds(pl.multiple_of(k * quarter, 8), quarter)] if fresh else there
            out.append(push(here, there, self.sends.at[n, link, f, k], self.recvs.at[n, f, k],
                            where))
        return out

    def go(self, *args, **kw):
        for copy in self.copies(*args, **kw):
            copy.start()

    def arrived(self, f, k):
        for copy in self.copies(0, f, k, self.x_side):
            copy.wait_recv()

    def plane(self, j):
        return lax.rem(self.z + j, self.planes)

    def hop(self, z, k, up, fresh=False):
        to = self.z + 1 if up else self.z - 1
        where = device(2 * to + self.x, self.y, self.c)
        return self.copies(0 if up else 3, 2 * z + self.x, k, where, fresh)

    def hops(self, z, up, action, fresh=False):
        @pl.when(self.z + 1 < self.planes if up else self.z > 0)
        def _():
            for side in range(2):
                for copy in self.hop(z, 2 * self.y + side, up, fresh):
                    action(copy)

    def at(self, d, body):
        pl.when(self.z >= d)(lambda: body(self.z - d, True))
        pl.when(self.z + d < self.planes)(lambda: body(self.z + d, False))

    def local(self):
        return [
            pltpu.make_async_copy(
                src, dst.at[pl.ds(pl.multiple_of(self.f * src.shape[0], 8), src.shape[0])],
                self.own.at[n])
            for n, (src, dst) in enumerate(zip(self.srcs, self.dsts))
        ]

    def start_x(self):
        for copy in self.local():
            copy.start()
        for k in (2 * self.y, 2 * self.y + 1, 2 * (1 - self.y) + 1):
            self.go(1, self.f, k, self.x_side, fresh=True)

    def start_z(self):
        for up in (True, False):
            self.hops(self.z, up, lambda copy: copy.start(), fresh=True)

    def spread(self, d):
        def one(z, up):
            f = 2 * z + self.x
            for side in range(2):
                self.arrived(f, 2 * self.y + side)
            self.hops(z, up, lambda copy: copy.start())
            for side in range(2):
                k = 2 * self.y + side
                self.go(1, f, k, self.x_side)
                self.go(2, f, k, self.y_side)

        self.at(d, one)

    def turn(self, d):
        def one(z, up):
            f = 2 * z + 1 - self.x
            self.arrived(f, 2 * self.y)
            self.go(2, f, 2 * self.y, self.y_side)
            if d:
                f = 2 * z + self.x
                k = 2 * (1 - self.y) + 1
                self.arrived(f, k)
                self.go(1, f, k, self.x_side)

        if d:
            self.at(d, one)
        else:
            one(self.z, True)

    def finish(self):
        x, y = self.x, self.y
        for copy in self.local():
            copy.wait()

        def one(j):
            other = 2 * self.plane(j) + 1 - x
            self.arrived(other, 2 * y + 1)
            self.arrived(other, 2 * (1 - y) + 1)
            self.arrived(other, 2 * (1 - y))

        looped(0, self.planes, one)

        def two(j):
            self.arrived(2 * self.plane(j) + x, 2 * (1 - y))

        looped(1, self.planes, two)

        for k in (2 * y, 2 * y + 1, 2 * (1 - y) + 1):
            for copy in self.copies(1, self.f, k, self.x_side, fresh=True):
                copy.wait_send()

        def three(j):
            f = 2 * self.plane(j) + x
            for side in range(2):
                k = 2 * y + side
                for copy in (*self.copies(1, f, k, self.x_side),
                             *self.copies(2, f, k, self.y_side)):
                    copy.wait_send()
            for copy in self.copies(1, f, 2 * (1 - y) + 1, self.x_side):
                copy.wait_send()

        looped(1, self.planes, three)

        def four(j):
            for copy in self.copies(2, 2 * self.plane(j) + 1 - x, 2 * y, self.y_side):
                copy.wait_send()

        looped(0, self.planes, four)
        for up in (True, False):
            self.hops(self.z, up, lambda copy: copy.wait_send(), fresh=True)
        for d in range(1, self.planes):
            self.at(d, lambda z, up: self.hops(z, up, lambda copy: copy.wait_send()))


def build_diagonals(table_ref, band):
    left = jnp.broadcast_to(band[0:1, :], (lanes, lanes))
    right = jnp.broadcast_to(band[3 * lanes - 1 : 3 * lanes, :], (lanes, lanes))
    for half in range(2):
        cols = slice(half * lanes, (half + 1) * lanes)
        first = far - lanes + half * lanes
        for row in range(0, first, lanes):
            table_ref[row : row + lanes, cols] = left
        table_ref[first : first + 3 * lanes, cols] = band
        for row in range(first + 3 * lanes, reach, lanes):
            table_ref[row : row + lanes, cols] = right


def attend_kernel(
    fsdp_count, gathers, bound_ref, idx_ref, small_ref, tok_ref, cot_ref, *refs,
):
    if gathers:
        wq_src, wo_src, wgu_src, wd_src, *refs = refs
    else:
        w_given, *refs = refs
    (xs_out, cs_ref, qkv_out, pl_ref, ps_ref, ctx_ref, ctx32_out, linv_out, gains_ref, w_ref,
     *refs) = refs
    if gathers:
        wo_ref, wgu_ref, wd_ref, *refs = refs
    (xs_ref, qkv_ref, ctx32_ref, linv_ref, idx_col, leave,
     smalls, xa, ca, p_long, p_short, table, mask, band, km, vt, ctx_t, linv_t,
     deal_send, deal_recv, pass_send, pass_recv, own, ctx_send, ctx_recv, p_sem, *refs) = refs
    f, p, c = place()
    rows_all, width = xs_ref.shape
    part = width // 2
    pairs = part // lanes
    short = rows_all - longest
    half = lanes // 2
    sibling = device(f, p, 1 - c)

    greet_all(fsdp_count)
    deals = [
        Dealing(fsdp_count, src, dst, deal_send.at[n], deal_recv.at[n], pass_send.at[n],
                pass_recv.at[n], own.at[n])
        for n, (src, dst) in enumerate(((small_ref, smalls), (tok_ref, xa), (cot_ref, ca)))
    ]
    events = []
    deals[0].start()
    if gathers:
        sends_q, recvs_q, own_q, sends_r, recvs_r, own_r = refs
        first = Gathering(fsdp_count, (wq_src,), (w_ref,), sends_q, recvs_q, own_q)
        rest = Gathering(fsdp_count, (wo_src, wgu_src, wd_src), (wo_ref, wgu_ref, wd_ref),
                         sends_r, recvs_r, own_r)
        first.start_z()
        rest.start_z()
        first.start_x()
    deals[1].start()
    if gathers:
        rest.start_x()
        order = [(first.spread, 1), (rest.spread, 1), (first.turn, 0), (first.spread, 2),
                 (first.turn, 1), (rest.spread, 2), (first.spread, 3), (first.turn, 2)]
        for step, d in order:
            step(d)
    deals[0].forward()
    deals[0].finish()

    slice_width = width // fsdp_count

    def gain_of(k, total):
        row = iota((lanes, width), 0)
        spot = jnp.where((iota((lanes, width), 1) == k * slice_width + row) & (row < slice_width),
                         1.0, 0.0).astype(bf16)
        return total + nn(smalls[c, p, k].astype(bf16), spot)

    gains_ref[...] = lax.fori_loop(0, fsdp_count, gain_of, jnp.zeros((8, width), f32))

    wide = 4 * lanes
    place_of = iota((lanes, wide), 1)
    offset = jnp.where(place_of < wide // 2, -place_of, wide - place_of)
    chosen = jnp.where(bucket_index(offset) == iota((lanes, wide), 0), 1.0, 0.0).astype(bf16)
    for side in range(2):
        by_head = nn(smalls[side, c, f].astype(bf16), chosen)
        for h in range(pairs):
            line = jnp.broadcast_to(by_head[2 + h : 3 + h, :], (lanes, wide))
            for d in range(3):
                turned = pltpu.roll(line, d * lanes, 1, stride=1, stride_axis=0)
                band[side * pairs + h, d * lanes : (d + 1) * lanes, :] = turned[:, lanes : 2 * lanes]

    idx_col[...] = jnp.transpose(
        jnp.broadcast_to(idx_ref[...].astype(f32), (lanes, rows_all)))
    bound = bound_ref[0]
    inside = (iota((short, short), 0) < bound) == (iota((short, short), 1) < bound)
    mask[...] = jnp.where(inside, 0.0, -1e30)

    if gathers:
        first.turn(3)
    deals[1].forward()
    if gathers:
        rest.spread(3)
        events = [functools.partial(rest.turn, d) for d in range(4)]
    else:
        given = pltpu.make_async_copy(w_given, w_ref, own.at[3])
        given.start()
        given.wait()
    deals[2].start()
    deals[1].finish()
    if gathers:
        first.finish()

    xa_rows = xa.shape[0] * xa.shape[1] * xa.shape[2] * xa.shape[3]

    def arrive(i):
        rows = pl.ds(pl.multiple_of(i * block, block), block)
        chosen = one_hot(idx_col[rows, 0:1], iota((block, xa_rows), 1).astype(f32))
        return rows, chosen

    def tile(i):
        rows, chosen = arrive(i)
        x = nn(chosen, xa[...].reshape(xa_rows, width))
        xs_ref[rows, :] = x.astype(bf16)
        normed = (x * inverse_rms(x) * gains_ref[0:1, :]).astype(bf16)
        for k in range(3):
            cols = slice(k * part, (k + 1) * part)
            qkv_ref[rows, cols] = nn(normed, w_ref[:, cols]).astype(bf16)

    looped(0, rows_all // block, tile)
    leaving = [
        pltpu.make_async_copy(here, there, leave.at[n])
        for n, (here, there) in enumerate(((xs_ref, xs_out), (qkv_ref, qkv_out)))
    ]
    for copy in leaving:
        copy.start()

    def poll(count):
        for _ in range(count):
            if events:
                events.pop(0)()

    own_lane = iota((rows_all, lanes), 1) < half
    for pair in range(pairs):
        cols = [slice(kind * part + pair * lanes, kind * part + (pair + 1) * lanes)
                for kind in range(3)]
        keys = qkv_ref[:, cols[1]]
        vt[...] = jnp.transpose(qkv_ref[:, cols[2]].astype(f32)).astype(bf16)
        for h in range(2):
            build_diagonals(table, band[2 * pair + h])
            km[...] = jnp.where(own_lane == (h == 0), keys, jnp.zeros_like(keys))

            def strip(base, count, out_ref, masked, b):
                here = pl.ds(pl.multiple_of(base + b * block, block), block)
                logits = nt(km[base : base + count, :], qkv_ref[here, cols[0]])
                top_row = pl.multiple_of(far - b * block, block)
                logits = logits + table[pl.ds(top_row, count), :]
                spot = pl.ds(pl.multiple_of(b * block, block), block)
                if masked:
                    logits = logits + mask[:, spot]
                top = jnp.max(logits, axis=0, keepdims=True)
                weights = jnp.exp(logits - top)
                inv = 1.0 / jnp.sum(weights, axis=0, keepdims=True)
                low = weights.astype(bf16)
                spot = pl.ds(pl.multiple_of(h * count + b * block, block), block)
                out_ref[pair % 2, :, spot] = low
                part_rows = slice(h * half, (h + 1) * half)
                ctx_t[part_rows, here] = nn(vt[part_rows, base : base + count], low) * inv
                linv_t[part_rows, here] = jnp.broadcast_to(inv, (half, block))

            if h == 0 and pair >= 2:
                for copy in p_copies(p_long, p_short, pl_ref, ps_ref, p_sem, pair - 2):
                    copy.wait()
            looped(0, longest // block, functools.partial(strip, 0, longest, p_long, False))
            poll(1)
            looped(0, short // block, functools.partial(strip, longest, short, p_short, True))
            poll(1)
        context = jnp.transpose(ctx_t[...])
        spot = c * pairs + pair
        ctx32_ref[:, pair * lanes : (pair + 1) * lanes] = context
        ctx_ref[spot] = context.astype(bf16)
        linv_ref[:, pair * lanes : (pair + 1) * lanes] = jnp.transpose(linv_t[...])
        for n, (here, there) in enumerate(((ctx32_ref, ctx32_out), (linv_ref, linv_out))):
            spot_lanes = slice(pair * lanes, (pair + 1) * lanes)
            copy = pltpu.make_async_copy(here.at[:, spot_lanes], there.at[:, spot_lanes],
                                         leave.at[2 + 2 * pair + n])
            copy.start()
            leaving.append(copy)
        push(ctx_ref.at[spot], ctx_ref.at[spot], ctx_send.at[pair], ctx_recv.at[pair],
             sibling).start()
        for copy in p_copies(p_long, p_short, pl_ref, ps_ref, p_sem, pair):
            copy.start()
        if pair == pairs - 2:
            deals[2].forward()
    poll(len(events))
    deals[2].finish()

    def cot_tile(i):
        rows, chosen = arrive(i)
        cs_ref[rows, :] = nn(chosen, ca[...].reshape(xa_rows, width)).astype(bf16)

    looped(0, rows_all // block, cot_tile)
    for pair in range(pairs):
        spot = c * pairs + pair
        there = (1 - c) * pairs + pair
        push(ctx_ref.at[spot], ctx_ref.at[spot], ctx_send.at[pair], ctx_recv.at[pair],
             sibling).wait_send()
        push(ctx_ref.at[there], ctx_ref.at[there], ctx_send.at[pair], ctx_recv.at[pair],
             sibling).wait_recv()
    for pair in range(max(0, pairs - 2), pairs):
        for copy in p_copies(p_long, p_short, pl_ref, ps_ref, p_sem, pair):
            copy.wait()
    for copy in leaving:
        copy.wait()
    for deal in deals:
        deal.sent()
        deal.passed()
    if gathers:
        rest.finish()


def p_copies(p_long, p_short, pl_ref, ps_ref, sem, pair):
    return [
        pltpu.make_async_copy(p_long.at[pair % 2], pl_ref.at[pair], sem.at[0, pair]),
        pltpu.make_async_copy(p_short.at[pair % 2], ps_ref.at[pair], sem.at[1, pair]),
    ]


def attend(fsdp_count, gathers, bound, idx_row, small, tokens, cotangent, *weights):
    rows = idx_row.shape[1]
    piece, width = tokens.shape[2:]
    part = width // 2
    pairs = part // lanes
    short = rows - longest
    vm = pl.BlockSpec(memory_space=pltpu.VMEM)
    hbm = pl.BlockSpec(memory_space=pl.ANY)
    dma = pltpu.SemaphoreType.DMA
    arrivals = pltpu.VMEM((2, 2, fsdp_count, piece, width), bf16)
    full = [jax.ShapeDtypeStruct((w.shape[0] * fsdp_count, w.shape[1]), bf16) for w in weights]
    out_shape = [
        jax.ShapeDtypeStruct((rows, width), bf16),
        jax.ShapeDtypeStruct((rows, width), bf16),
        jax.ShapeDtypeStruct((rows, 3 * part), bf16),
        jax.ShapeDtypeStruct((pairs, longest, 2 * longest), bf16),
        jax.ShapeDtypeStruct((pairs, short, 2 * short), bf16),
        jax.ShapeDtypeStruct((2 * pairs, rows, lanes), bf16),
        jax.ShapeDtypeStruct((rows, part), f32),
        jax.ShapeDtypeStruct((rows, part), f32),
        jax.ShapeDtypeStruct((8, width), f32),
        jax.ShapeDtypeStruct((width, 3 * part), bf16),
    ]
    out_specs = [hbm, vm, hbm, hbm, hbm, vm, hbm, hbm, vm, vm]
    scratch = [
        pltpu.VMEM((rows, width), bf16),
        pltpu.VMEM((rows, 3 * part), bf16),
        pltpu.VMEM((rows, part), f32),
        pltpu.VMEM((rows, part), f32),
        pltpu.VMEM((rows, lanes), f32),
        dma((2 + 2 * pairs,)),
        pltpu.VMEM((2, 2, fsdp_count, 8, lanes), f32),
        arrivals, arrivals,
        pltpu.VMEM((2, longest, 2 * longest), bf16),
        pltpu.VMEM((2, short, 2 * short), bf16),
        pltpu.VMEM((reach, block), f32),
        pltpu.VMEM((short, short), f32),
        pltpu.VMEM((2 * pairs, 3 * lanes, lanes), f32),
        pltpu.VMEM((rows, lanes), bf16),
        pltpu.VMEM((lanes, rows), bf16),
        pltpu.VMEM((lanes, rows), f32),
        pltpu.VMEM((lanes, rows), f32),
        dma((3, 2 * fsdp_count)), dma((3, 2 * fsdp_count)), dma((3, 2 * fsdp_count)),
        dma((3, 2 * fsdp_count)), dma((4,)), dma((pairs,)), dma((pairs,)), dma((2, pairs)),
    ]
    if gathers:
        out_shape += full[1:]
        out_specs += [hbm] * 3
        scratch += [
            dma((1, 4, fsdp_count, 4)), dma((1, fsdp_count, 4)), dma((1,)),
            dma((3, 4, fsdp_count, 4)), dma((3, fsdp_count, 4)), dma((3,)),
        ]
    return pl.pallas_call(
        functools.partial(attend_kernel, fsdp_count, gathers),
        in_specs=[pl.BlockSpec(memory_space=pltpu.SMEM), vm, vm, hbm, hbm] + [hbm] * len(weights),
        out_specs=tuple(out_specs),
        out_shape=tuple(out_shape),
        scratch_shapes=scratch,
        compiler_params=pltpu.CompilerParams(
            vmem_limit_bytes=vmem_limit, collective_id=0, has_side_effects=True),
        name="attend",
    )(bound, idx_row, small, tokens, cotangent, *weights)


class Homing:
    def __init__(self, fsdp_count, src, dst, send, recv, own):
        self.f, self.p, self.c = place()
        self.count = fsdp_count
        self.src, self.dst, self.send, self.recv, self.own = src, dst, send, recv, own

    def out(self, q, g):
        return push(self.src.at[q, g], self.dst.at[self.p, self.f], self.send.at[q, g],
                    self.recv.at[self.p, self.f], device(g, q, self.c))

    def come(self, q, g):
        return push(self.src.at[q, g], self.dst.at[q, g], self.send.at[q, g],
                    self.recv.at[q, g], device(g, q, self.c))

    def local(self):
        return pltpu.make_async_copy(self.src.at[self.p, self.f], self.dst.at[self.p, self.f],
                                     self.own)

    def start(self, q):
        for i in range(1, self.count):
            self.out(q, lax.rem(self.f + i, self.count)).start()

    def start_other(self):
        self.out(1 - self.p, self.f).start()
        self.local().start()

    def finish(self):
        self.local().wait()
        self.come(1 - self.p, self.f).wait_recv()
        self.out(1 - self.p, self.f).wait_send()
        for q in range(2):

            def one(i, q=q):
                g = lax.rem(self.f + i, self.count)
                self.come(q, g).wait_recv()
                self.out(q, g).wait_send()

            looped(1, self.count, one)


class Returning:
    def __init__(self, idx_ref, rows_ref, given, taken, pass_send, pass_recv, home):
        self.f, self.p, self.c = place()
        self.idx_ref, self.rows_ref, self.given, self.taken = idx_ref, rows_ref, given, taken
        self.pass_send, self.pass_recv, self.home = pass_send, pass_recv, home
        self.count = taken.shape[1] * taken.shape[2]

    def unslot(self, side, q):
        chosen = one_hot(
            iota((self.count, self.rows_ref.shape[0]), 0) + (side * 2 + q) * self.count,
            self.idx_ref[...])
        return nn(chosen, self.rows_ref[...])

    def pass_over(self, q):
        return push(self.given.at[q], self.taken.at[q], self.pass_send.at[q],
                    self.pass_recv.at[q], device(self.f, self.p, 1 - self.c))

    def give(self):
        for q in range(2):
            self.given[q] = self.unslot(1 - self.c, q).astype(bf16).reshape(self.given.shape[1:])
            self.pass_over(q).start()

    def keep(self):
        for q in range(2):
            self.pass_over(q).wait_recv()
            other = self.taken[q].reshape(self.count, self.rows_ref.shape[1]).astype(f32)
            value = self.unslot(self.c, q) + other
            self.taken[q] = value.astype(bf16).reshape(self.taken.shape[1:])
            self.home.start(q)
        self.home.start_other()

    def finish(self):
        for q in range(2):
            self.pass_over(q).wait_send()
        self.home.finish()


def feed_kernel(
    fsdp_count, idx_ref, ctx_ref, ctx32_in, linv_in, xs_ref, cs_in, wo_ref, gains_ref, wgu_ref,
    wd_ref, output_ref, ggu_ref, gd_out, datt_out, dos_out, go_ref, ggain_ref,
    out, mid, nff, hid, dgu, dn, dn_sib, given, taken, send, recv, pass_send, pass_recv,
    home_send, home_recv, own, ctx32_ref, linv_ref, cs_ref, late,
    gd_ref, datt_ref, dos_ref, leave,
):
    rows_all, width = xs_ref.shape
    ff = wd_ref.shape[0]
    part = width // 2
    lift = math.sqrt(2 / math.pi)
    tiles = rows_all // block
    f, p, c = place()
    sibling = device(f, p, 1 - c)
    gain = gains_ref[1:2, :]
    half_cols = pl.ds(pl.multiple_of(c * part, lanes), part)
    comes = [
        pltpu.make_async_copy(there, here, late.at[n])
        for n, (there, here) in enumerate(
            ((cs_in, cs_ref), (ctx32_in, ctx32_ref), (linv_in, linv_ref)))
    ]
    for copy in comes:
        copy.start()
    home = Homing(fsdp_count, taken, output_ref, home_send, home_recv, own)
    rows_home = Returning(idx_ref, out, given, taken, pass_send, pass_recv, home)
    greet_all(fsdp_count)

    def exchange(i):
        rows = pl.ds(pl.multiple_of(i * block, block), block)
        return pltpu.make_async_remote_copy(
            src_ref=dn.at[rows, :], dst_ref=dn_sib.at[rows, :], send_sem=send.at[i],
            recv_sem=recv.at[i], device_id=sibling, device_id_type=MESH)

    def forward(i):
        rows = pl.ds(pl.multiple_of(i * block, block), block)
        mixed = jnp.concatenate([ctx_ref[n, rows, :] for n in range(ctx_ref.shape[0])], axis=1)
        middle = xs_ref[rows, :].astype(f32) + nn(mixed, wo_ref[...])
        mid[rows, :] = middle
        normed = (middle * inverse_rms(middle) * gain).astype(bf16)
        nff[rows, :] = normed
        gate = nn(normed, wgu_ref[:, :ff])
        up = nn(normed, wgu_ref[:, ff:])
        square = gate * gate
        bent = jnp.tanh(lift * gate * (1.0 + 0.044715 * square))
        halved = 0.5 * (1.0 + bent)
        gelu = gate * halved
        slope = halved + 0.5 * gate * (1.0 - bent * bent) * (
            lift * (1.0 + 3 * 0.044715 * square))
        hidden = (gelu * up).astype(bf16)
        hid[rows, :] = hidden
        dgu[rows, :ff] = (up * slope).astype(bf16)
        dgu[rows, ff:] = gelu.astype(bf16)
        out[rows, :] = (0.5 * middle + nn(hidden, wd_ref[...])).astype(bf16)

    def backward(i):
        rows = pl.ds(pl.multiple_of(i * block, block), block)
        d_hidden = nt(cs_ref[rows, :], wd_ref[...])
        d_gate = (d_hidden * dgu[rows, :ff].astype(f32)).astype(bf16)
        d_up = (d_hidden * dgu[rows, ff:].astype(f32)).astype(bf16)
        dgu[rows, :ff] = d_gate
        dgu[rows, ff:] = d_up
        dn[rows, :] = (nt(d_gate, wgu_ref[:, :ff]) + nt(d_up, wgu_ref[:, ff:])).astype(bf16)
        exchange(i).start()

    looped(0, tiles, forward)
    for copy in comes:
        copy.wait()
    rows_home.give()
    looped(0, 1, backward)
    rows_home.keep()
    looped(1, tiles, backward)

    def down(i, carry):
        cols = pl.ds(pl.multiple_of(i * block, block), block)
        gd_ref[cols, :] = tn(hid[:, cols], cs_ref[...]).astype(bf16)
        return carry

    lax.fori_loop(0, ff // block, down, 0)
    leaving = [
        pltpu.make_async_copy(here, there, leave.at[n])
        for n, (here, there) in enumerate(
            ((gd_ref, gd_out), (datt_ref, datt_out), (dos_ref, dos_out)))
    ]
    leaving[0].start()

    def settle(i, total):
        rows = pl.ds(pl.multiple_of(i * block, block), block)
        exchange(i).wait()
        mine = dn[rows, :].astype(f32)
        grad = mine + dn_sib[rows, :].astype(f32)
        middle = mid[rows, :]
        s = inverse_rms(middle)
        unit = middle * s
        scaled = gain * grad
        d_middle = cs_ref[rows, :].astype(f32) + s * (
            scaled - unit * jnp.mean(scaled * unit, axis=-1, keepdims=True))
        low = d_middle.astype(bf16)
        datt_ref[rows, :] = low
        d_context = nt(low, wo_ref[half_cols, :]).astype(bf16).astype(f32)
        scaled = (d_context * linv_ref[rows, :]).astype(bf16).astype(f32)
        against = scaled * ctx32_ref[rows, :]
        lane = iota((block, lanes), 1)
        for n in range(dos_ref.shape[0]):
            cols = slice((n // 2) * lanes, (n // 2 + 1) * lanes)
            mine_lanes = (lane < lanes // 2) == (n % 2 == 0)
            spare = lanes // 2 if n % 2 == 0 else 0
            delta = jnp.sum(jnp.where(mine_lanes, against[:, cols], 0.0), axis=1, keepdims=True)
            high = delta.astype(bf16).astype(f32)
            extra = jnp.where(lane == spare, -high,
                              jnp.where(lane == spare + 1, high - delta, 0.0))
            dos_ref[n, rows, :] = jnp.where(mine_lanes, scaled[:, cols], extra).astype(bf16)
        return total + jnp.sum(mine * unit, axis=0, keepdims=True)

    ggain_ref[...] = lax.fori_loop(0, tiles, settle, jnp.zeros((1, width), f32))
    for copy in leaving[1:]:
        copy.start()
    for n in range(0, ctx_ref.shape[0], 2):
        mixed = jnp.concatenate((ctx_ref[n], ctx_ref[n + 1]), axis=1)
        go_ref[n * lanes : (n + 2) * lanes, :] = tn(mixed, datt_ref[:, half_cols]).astype(bf16)

    def gate_up(i, carry):
        cols = pl.ds(pl.multiple_of(i * block, block), block)
        ggu_ref[cols, :] = tn(nff[:, cols], dgu[...]).astype(bf16)
        return carry

    lax.fori_loop(0, width // block, gate_up, 0)
    rows_home.finish()
    for copy in leaving:
        copy.wait()


def feed(fsdp_count, piece, idx_row, ctx, ctx32, linv, xs, cs, w_out, gains, w_gu, w_down):
    rows, width = xs.shape
    ff = w_down.shape[0]
    part = width // 2
    shape = (2, fsdp_count, piece, width)
    dma = pltpu.SemaphoreType.DMA
    vm = pl.BlockSpec(memory_space=pltpu.VMEM)
    hbm = pl.BlockSpec(memory_space=pl.ANY)
    return pl.pallas_call(
        functools.partial(feed_kernel, fsdp_count),
        in_specs=[vm, vm, hbm, hbm, vm, hbm, vm, vm, vm, vm],
        out_specs=(hbm, vm, hbm, hbm, hbm, vm, vm),
        out_shape=(
            jax.ShapeDtypeStruct(shape, bf16),
            jax.ShapeDtypeStruct((width, 2 * ff), bf16),
            jax.ShapeDtypeStruct((ff, width), bf16),
            jax.ShapeDtypeStruct((rows, width), bf16),
            jax.ShapeDtypeStruct((ctx.shape[0], rows, lanes), bf16),
            jax.ShapeDtypeStruct((width, part), bf16),
            jax.ShapeDtypeStruct((1, width), f32),
        ),
        scratch_shapes=[
            pltpu.VMEM((rows, width), bf16),
            pltpu.VMEM((rows, width), f32),
            pltpu.VMEM((rows, width), bf16),
            pltpu.VMEM((rows, ff), bf16),
            pltpu.VMEM((rows, 2 * ff), bf16),
            pltpu.VMEM((rows, width), bf16),
            pltpu.VMEM((rows, width), bf16),
            pltpu.VMEM(shape, bf16),
            pltpu.VMEM(shape, bf16),
            dma((rows // block,)), dma((rows // block,)), dma((2,)), dma((2,)),
            dma((2, fsdp_count)), dma((2, fsdp_count)), dma,
            pltpu.VMEM((rows, part), f32),
            pltpu.VMEM((rows, part), f32),
            pltpu.VMEM((rows, width), bf16),
            dma((3,)),
            pltpu.VMEM((ff, width), bf16),
            pltpu.VMEM((rows, width), bf16),
            pltpu.VMEM((ctx.shape[0], rows, lanes), bf16),
            dma((3,)),
        ],
        compiler_params=pltpu.CompilerParams(
            vmem_limit_bytes=vmem_limit, collective_id=2, has_side_effects=True),
        name="feed",
    )(idx_row, ctx, ctx32, linv, xs, cs, w_out, gains, w_gu, w_down)


class Scattering:
    def __init__(self, fsdp_count, grads, in_y, in_x, turned, in_z, final, send, recv):
        self.f, self.y, self.c = place()
        self.count = fsdp_count
        self.planes = fsdp_count // 2
        self.z, self.x = self.f // 2, self.f % 2
        self.grads, self.in_y, self.in_x = grads, in_y, in_x
        self.turned, self.in_z, self.final = turned, in_z, final
        self.send, self.recv = send, recv
        self.x_side = device(self.z * 2 + 1 - self.x, self.y, self.c)
        self.y_side = device(self.f, 1 - self.y, self.c)
        self.sibling = device(self.f, self.y, 1 - self.c)

    def part(self, n, f, k):
        return self.grads[n].at[f * 4 + k]

    def plane(self, j):
        return lax.rem(self.z + j, self.planes)

    def order(self):
        return [*range(1, self.planes), 0]

    def move(self, n, kind, i, j, src, dst, where):
        return push(src, dst, self.send.at[n, kind, i, j], self.recv.at[n, kind, i, j], where)

    def along_y(self, n, z, x):
        return self.move(n, 0, z, x, self.part(n, 2 * z + x, 2 * (1 - self.y)),
                         self.in_y[n].at[z, x], self.y_side)

    def along_x(self, n, z, y):
        return self.move(n, 1, z, y, self.part(n, 2 * z + 1 - self.x, 2 * y + 1),
                         self.in_x[n].at[z, y], self.x_side)

    def turn(self, n, z, side):
        if side == 0:
            return self.move(n, 2, z, 0, self.in_y[n].at[z, 1 - self.x],
                             self.turned[n].at[z, 0], self.x_side)
        return self.move(n, 2, z, 1, self.in_x[n].at[z, 1 - self.y], self.turned[n].at[z, 1],
                         self.y_side)

    def summed(self, n, z, side):
        return (self.in_y[n].at[z, self.x], self.in_x[n].at[z, self.y])[side]

    def out_z(self, n, z, side):
        return push(self.summed(n, z, side), self.in_z[n].at[self.z, side],
                    self.send.at[n, 3, z, side], self.recv.at[n, 3, self.z, side],
                    device(2 * z + self.x, self.y, self.c))

    def come_z(self, n, z, side):
        return push(self.summed(n, z, side), self.in_z[n].at[z, side],
                    self.send.at[n, 3, z, side], self.recv.at[n, 3, z, side],
                    device(2 * z + self.x, self.y, self.c))

    def last_y(self, n, side, mine):
        y = self.y if mine else 1 - self.y
        here = self.final[n].at[self.c, 2 * y + side]
        return self.move(n, 4, 0, side, here, here, self.y_side)

    def last_core(self, n, mine):
        here = self.final[n].at[self.c if mine else 1 - self.c]
        return self.move(n, 5, 0, 0, here, here, self.sibling)

    def each(self, body):
        for n in range(len(self.grads)):
            body(n)

    def start(self, j):
        z = self.plane(j)
        for n in range(len(self.grads)):
            for k in range(2):
                self.along_y(n, z, k).start()
                self.along_x(n, z, k).start()

    def fold(self, j):
        z = self.plane(j)
        for n in range(len(self.grads)):
            for k in range(2):
                self.along_y(n, z, k).wait_recv()
                add_to(self.in_y[n].at[z, k], self.part(n, 2 * z + k, 2 * self.y))
            self.turn(n, z, 0).start()
            for k in range(2):
                self.along_x(n, z, k).wait_recv()
                add_to(self.in_x[n].at[z, k], self.part(n, 2 * z + self.x, 2 * k + 1))
            self.turn(n, z, 1).start()

    def plane_sum(self, j):
        z = self.plane(j)
        for n in range(len(self.grads)):
            for side in range(2):
                self.turn(n, z, side).wait_recv()
                add_to(self.summed(n, z, side), self.turned[n].at[z, side])
                if j:
                    self.out_z(n, z, side).start()

    def total(self):
        for n in range(len(self.grads)):
            for side in range(2):
                value = self.summed(n, self.z, side)[...].astype(f32)
                for j in range(1, self.planes):
                    z = self.plane(j)
                    self.come_z(n, z, side).wait_recv()
                    value = value + self.in_z[n][z, side].astype(f32)
                self.final[n][self.c, 2 * self.y + side] = value.astype(bf16)
                self.last_y(n, side, True).start()

    def share(self):
        for n in range(len(self.grads)):
            for side in range(2):
                self.last_y(n, side, False).wait_recv()
            self.last_core(n, True).start()

    def finish(self):
        for n in range(len(self.grads)):
            self.last_core(n, False).wait_recv()
            self.last_core(n, True).wait_send()
            for side in range(2):
                self.last_y(n, side, True).wait_send()
            for j in range(self.planes):
                z = self.plane(j)
                for k in range(2):
                    self.along_y(n, z, k).wait_send()
                    self.along_x(n, z, k).wait_send()
                    self.turn(n, z, k).wait_send()
                    if j:
                        self.out_z(n, z, k).wait_send()

    def steps(self, together):
        order = self.order()
        if together:
            return [
                lambda: [self.start(j) for j in order],
                lambda: [self.fold(j) for j in order],
                lambda: [self.plane_sum(j) for j in order],
                self.total, self.share,
            ]
        ahead = 2
        out = [lambda: [self.start(j) for j in order[:ahead]]]

        def fold(n):
            self.fold(order[n])
            if n + ahead < len(order):
                self.start(order[n + ahead])

        for n in range(len(order)):
            out.append(functools.partial(fold, n))
            if n:
                out.append(functools.partial(self.plane_sum, order[n - 1]))
        return out + [functools.partial(self.plane_sum, order[-1]), self.total, self.share]


def add_to(here, other):
    here[...] = (here[...].astype(f32) + other[...].astype(f32)).astype(bf16)


def back_kernel(
    fsdp_count, scatters, idx_ref, xs_ref, gains_ref, ggain_ref, w_in, dos_in, qkv_in, datt_ref,
    pl_ref, ps_ref, *refs,
):
    if scatters:
        grads = refs[:3]
        refs = refs[3:]
    tokens_ref, small_ref, *refs = refs
    if scatters:
        outs, refs = refs[:7], refs[7:]
        gqkv_refs, refs = refs[:3], refs[3:]
    else:
        gqkv_refs, refs = refs[:3], refs[3:]
    (w_ref, dos_ref, qkv_ref, late, ybuf, normed, dqkv, table, qs, ds_l, ds_s, p_l, p_s, acc, va, kt, dq_t, given, taken,
     smalls, load, p_sem, pass_send, pass_recv, home_send, home_recv, own,
     small_send, small_recv, small_pass, small_back, *refs) = refs
    f, p, c = place()
    sibling = device(f, p, 1 - c)
    rows_all, width = xs_ref.shape
    part = width // 2
    pairs = part // lanes
    short = rows_all - longest
    half = lanes // 2
    gain_attn = gains_ref[0:1, :]

    def p_copies(head):
        pair, h = head // 2, head % 2
        return [
            pltpu.make_async_copy(pl_ref.at[pair, :, h * longest : (h + 1) * longest],
                                  p_l.at[h], p_sem.at[0, h]),
            pltpu.make_async_copy(ps_ref.at[pair, :, h * short : (h + 1) * short],
                                  p_s.at[h], p_sem.at[1, h]),
        ]

    comes = [
        pltpu.make_async_copy(there, here, late.at[n])
        for n, (there, here) in enumerate(
            ((qkv_in, qkv_ref), (dos_in, dos_ref), (w_in, w_ref)))
    ]
    for copy in comes:
        copy.start()
    for head in range(2):
        for copy in p_copies(head):
            copy.start()
    greet_all(fsdp_count)
    sets = []
    if scatters:
        for group in range(1 + pairs):
            arrays = grads if group == 0 else (gqkv_refs[group - 1],)
            count = len(arrays)
            bufs = [refs[k * count : (k + 1) * count] for k in range(5)]
            send, recv = refs[5 * count : 5 * count + 2]
            refs = refs[5 * count + 2 :]
            sets.append(Scattering(fsdp_count, arrays, *bufs, send, recv))
    steps = [group.steps(n > 0) for n, group in enumerate(sets)]

    def poll(*which):
        for n in which:
            if scatters and steps[n]:
                steps[n].pop(0)()

    places = {1: (0,), 4: (0,), 6: (0,), 8: (0,), 10: (0,), 12: (0,), 13: (0,), 14: (1,), 16: (0,), 17: (1,)}
    poll(0)

    home = Homing(fsdp_count, taken, tokens_ref, home_send, home_recv, own.at[0])
    rows_home = Returning(idx_ref, ybuf, given, taken, pass_send, pass_recv, home)

    def norm_tile(i):
        rows = pl.ds(pl.multiple_of(i * block, block), block)
        x = xs_ref[rows, :].astype(f32)
        normed[rows, :] = (x * inverse_rms(x) * gain_attn).astype(bf16)

    looped(0, rows_all // block, norm_tile)
    for copy in comes:
        copy.wait()

    lane = iota((rows_all, lanes), 1)
    buckets = band_buckets()
    small_ref_rows = iota((lanes // 4, lanes), 1)
    bias = jnp.zeros((lanes // 4, lanes), f32)
    for pair in range(pairs):
        cols = [slice(kind * part + pair * lanes, kind * part + (pair + 1) * lanes)
                for kind in range(3)]
        queries = qkv_ref[:, cols[0]]
        keys = qkv_ref[:, cols[1]]
        values = qkv_ref[:, cols[2]]
        kt[...] = jnp.transpose(keys.astype(f32)).astype(bf16)
        for h in range(2):
            head = 2 * pair + h
            own_lanes = (lane < half) == (h == 0)
            spare = half if h == 0 else 0
            qs[...] = jnp.where(own_lanes, queries, jnp.zeros_like(queries))
            ones = jnp.where((lane == spare) | (lane == spare + 1), 1.0, 0.0)
            va[...] = jnp.where(own_lanes, values.astype(f32), ones).astype(bf16)
            table[...] = jnp.zeros_like(table)
            for copy in p_copies(head):
                copy.wait()

            def strip(base, count, p_buf, ds_buf, b):
                here = pl.ds(pl.multiple_of(base + b * block, block), block)
                spot = pl.ds(pl.multiple_of(b * block, block), block)
                d_weights = nt(va[base : base + count, :], dos_ref[head, here, :])
                d_logits = p_buf[h, :, spot].astype(f32) * d_weights
                window = pl.ds(pl.multiple_of(far - b * block, block), count)
                table[window, :] = table[window, :] + d_logits
                low = d_logits.astype(bf16)
                ds_buf[:, spot] = low
                part_rows = slice(h * half, (h + 1) * half)
                dq_t[part_rows, here] = nn(kt[part_rows, base : base + count], low)

            looped(0, longest // block, functools.partial(strip, 0, longest, p_l, ds_l))
            poll(*places.get(3 * head, ()))
            looped(0, short // block, functools.partial(strip, longest, short, p_s, ds_s))
            poll(*places.get(3 * head + 1, ()))
            for base, count, p_buf, ds_buf in ((0, longest, p_l, ds_l), (longest, short, p_s, ds_s)):
                rows = slice(base, base + count)
                clean = jnp.where(own_lanes[rows], dos_ref[head, rows, :].astype(f32), 0.0)
                d_value = nn(p_buf[h], clean.astype(bf16))
                d_key = nn(ds_buf[...], qs[rows, :])
                if h == 0:
                    acc[0, rows, :] = d_value
                    acc[1, rows, :] = d_key
                else:
                    dqkv[rows, cols[2]] = (acc[0, rows, :] + d_value).astype(bf16)
                    dqkv[rows, cols[1]] = (acc[1, rows, :] + d_key).astype(bf16)
            if head + 2 < 2 * pairs:
                for copy in p_copies(head + 2):
                    copy.start()
            before = far - lanes
            after = far + 3 * lanes
            band = table[before : before + 3 * lanes, :lanes] + table[far : far + 3 * lanes, lanes:]
            left = jnp.sum(table[:before, :lanes] + table[:before, lanes:], axis=0, keepdims=True)
            left = left + jnp.sum(table[before:far, lanes:], axis=0, keepdims=True)
            right = jnp.sum(table[after:, :lanes] + table[after:, lanes:], axis=0, keepdims=True)
            right = right + jnp.sum(table[after - lanes : after, :lanes], axis=0, keepdims=True)
            for label in range(lanes // 4):
                line = jnp.sum(jnp.where(buckets == label, band, 0.0), axis=0, keepdims=True)
                if label == 15:
                    line = line + left
                if label == 31:
                    line = line + right
                table[label : label + 1, :lanes] = line
            sums = jnp.sum(table[: lanes // 4, :lanes], axis=1, keepdims=True)
            bias = bias + jnp.where(small_ref_rows == c * 2 * pairs + head, sums, 0.0)
            poll(*places.get(3 * head + 2, ()))
        dqkv[:, cols[0]] = jnp.transpose(dq_t[...]).astype(bf16)
        for kind in range(3):
            grad = tn(normed[...], dqkv[:, cols[kind]])
            grad = grad.reshape(*gqkv_refs[pair].shape[:-1], lanes)
            gqkv_refs[pair][..., kind * lanes : (kind + 1) * lanes] = grad.astype(bf16)
        if pair == pairs - 1:
            reload = pltpu.make_async_copy(datt_ref, normed, load)
            reload.start()
        poll(1 + pair)

    def tile(i, total):
        rows = slice(i * block, (i + 1) * block)
        x = xs_ref[rows, :].astype(f32)
        s = inverse_rms(x)
        unit = x * s
        grad = nt(dqkv[rows, :], w_ref[...])
        scaled = gain_attn * grad
        y = 0.5 * normed[rows, :].astype(f32) + s * (
            scaled - unit * jnp.mean(scaled * unit, axis=-1, keepdims=True))
        ybuf[rows, :] = y.astype(bf16)
        return total + jnp.sum(grad * unit, axis=0, keepdims=True)

    grad_gain = jnp.zeros((1, width), f32)
    reload.wait()
    for i in range(rows_all // block):
        grad_gain = tile(i, grad_gain)
    rows_home.give()
    quarter = lanes // 4
    small_ref[0:quarter, :] = bias
    small_ref[quarter:, :] = jnp.zeros((small_ref.shape[0] - quarter, lanes), f32)
    for j in range(width // lanes):
        cols = slice(j * lanes, (j + 1) * lanes)
        small_ref[quarter + j : quarter + j + 1, :] = grad_gain[:, cols]
        row = quarter + 8 + j
        small_ref[row : row + 1, :] = ggain_ref[:, cols]
    dealt = Dealing(fsdp_count, small_ref, smalls, small_send, small_recv, small_pass, small_back,
                    own.at[1])
    dealt.start()
    rows_home.keep()
    poll(0, 2, 3, 1, 0, 2, 3, 1, 2, 3, 2, 3)
    dealt.forward()
    dealt.finish()
    dealt.sent()
    dealt.passed()

    def gather_small(k, total):
        return total + smalls[k // (2 * fsdp_count), (k // fsdp_count) % 2, k % fsdp_count]

    small_ref[...] = lax.fori_loop(0, 4 * fsdp_count, gather_small,
                                   jnp.zeros(small_ref.shape, f32))
    for group in sets:
        group.finish()
    if scatters:
        gate, up, down, out_w, query, key, value = outs
        gu, dn, wo = sets[0].final
        ff = gu.shape[3] // 2
        cut = ff // fsdp_count
        for k in range(4):
            for side in range(2):
                rows = gu.shape[2]
                rows = slice(k * rows, (k + 1) * rows)
                for g in range(fsdp_count):
                    there = slice((2 * g + side) * cut, (2 * g + side + 1) * cut)
                    gate[rows, there] = gu[side, k, :, g * cut : (g + 1) * cut].astype(f32)
                    up[rows, there] = gu[side, k, :, ff + g * cut : ff + (g + 1) * cut].astype(f32)
                many = dn.shape[2]
                first = (side * 4 + k) * many
                down[first : first + many, :] = dn[side, k].astype(f32)
                out_w[rows, side * part : (side + 1) * part] = wo[side, k].astype(f32)
                for pair in range(pairs):
                    [one] = sets[1 + pair].final
                    there = slice(side * part + pair * lanes, side * part + (pair + 1) * lanes)
                    for kind, ref in enumerate((query, key, value)):
                        ref[rows, there] = one[side, k, :, kind * lanes : (kind + 1) * lanes].astype(
                            f32)
    rows_home.finish()


def back(fsdp_count, piece, scatters, idx_row, xs, gains, ggain, w_qkv, datt, dos, qkv,
         p_long, p_short, grads):
    rows, width = xs.shape
    part = width // 2
    pairs = part // lanes
    short = rows - longest
    vm = pl.BlockSpec(memory_space=pltpu.VMEM)
    hbm = pl.BlockSpec(memory_space=pl.ANY)
    dma = pltpu.SemaphoreType.DMA
    shape = (2, fsdp_count, piece, width)
    own_rows = width // fsdp_count
    out_shape = [
        jax.ShapeDtypeStruct(shape, bf16), jax.ShapeDtypeStruct((48, lanes), f32),
    ]
    out_specs = [hbm, vm]
    if scatters:
        ff = grads[0].shape[1]
        out_shape += [jax.ShapeDtypeStruct((own_rows, ff), f32)] * 2
        out_shape += [jax.ShapeDtypeStruct((2 * grads[1].shape[0] // fsdp_count, width), f32)]
        out_shape += [jax.ShapeDtypeStruct((own_rows, width), f32)] * 4
        out_specs += [vm] * 7
    gqkv = [jax.ShapeDtypeStruct((width, 3 * lanes), bf16)] * pairs
    scratch = []
    if scatters:
        grads = tuple(g.reshape(4 * fsdp_count, -1, g.shape[1]) for g in grads)
        scratch = [pltpu.VMEM((4 * fsdp_count, own_rows // 4, 3 * lanes), bf16)] * pairs
    if not scatters:
        out_shape += gqkv
        out_specs += [vm] * pairs
    scratch += [
        pltpu.VMEM(w_qkv.shape, bf16),
        pltpu.VMEM(dos.shape, bf16),
        pltpu.VMEM(qkv.shape, bf16),
        dma((3,)),
        pltpu.VMEM((rows, width), bf16),
        pltpu.VMEM((rows, width), bf16),
        pltpu.VMEM((rows, 3 * part), bf16),
        pltpu.VMEM((reach, block), f32),
        pltpu.VMEM((rows, lanes), bf16),
        pltpu.VMEM((longest, longest), bf16),
        pltpu.VMEM((short, short), bf16),
        pltpu.VMEM((2, longest, longest), bf16),
        pltpu.VMEM((2, short, short), bf16),
        pltpu.VMEM((2, rows, lanes), f32),
        pltpu.VMEM((rows, lanes), bf16),
        pltpu.VMEM((lanes, rows), bf16),
        pltpu.VMEM((lanes, rows), f32),
        pltpu.VMEM(shape, bf16),
        pltpu.VMEM(shape, bf16),
        pltpu.VMEM((2, 2, fsdp_count, 48, lanes), f32),
        dma, dma((2, 2)), dma((2,)), dma((2,)),
        dma((2, fsdp_count)), dma((2, fsdp_count)), dma((2,)),
        *[dma((2 * fsdp_count,))] * 4,
    ]
    if scatters:
        planes = fsdp_count // 2
        for quarters in ([g.shape[1:] for g in grads], *[[(own_rows // 4, 3 * lanes)]] * pairs):
            for lead in ((planes, 2), (planes, 2), (planes, 2), (planes, 2), (2, 4)):
                scratch += [pltpu.VMEM((*lead, *q), bf16) for q in quarters]
            scratch += [dma((len(quarters), 6, planes, 2))] * 2
    return pl.pallas_call(
        functools.partial(back_kernel, fsdp_count, scatters),
        in_specs=[vm] * 4 + [hbm] * 6 + [vm] * (len(grads) if scatters else 0),
        out_specs=tuple(out_specs),
        out_shape=tuple(out_shape),
        scratch_shapes=scratch,
        compiler_params=pltpu.CompilerParams(
            vmem_limit_bytes=vmem_limit, collective_id=1, has_side_effects=True),
        name="back",
    )(idx_row, xs, gains, ggain, w_qkv, dos, qkv, datt, p_long, p_short,
      *(grads if scatters else ()))


def shards(
    tokens, cotangent, lengths, dealing, gain_attn, w_query, w_key, w_value, w_out, bias_table,
    gain_ff, w_gate, w_up, w_down,
):
    fsdp_count = lax.axis_size("fsdp")
    sp_count = lax.axis_size("sp")
    micro_count, token_rows, width = tokens.shape
    piece = token_rows // fsdp_count
    group_rows = token_rows * sp_count
    local_heads = bias_table.shape[1]
    heads = local_heads * sp_count
    part = width // 2
    s = lax.axis_index("sp")
    p, c = s // 2, s % 2
    full_piece = -(-piece // 8) * 8

    def pieces(value):
        value = value.reshape(micro_count, fsdp_count, piece, width)
        return jnp.pad(value, ((0, 0), (0, 0), (0, full_piece - piece), (0, 0)))

    order = lax.dynamic_index_in_dim(dealing[:, 0], p, 0, keepdims=False)
    length = lax.dynamic_index_in_dim(lengths[:, 0], p, 0, keepdims=False)
    first_long = length[0] == longest
    start = jnp.where(first_long, 0, jnp.where(length[1] == longest, length[0],
                                               length[0] + length[1]))
    bound = jnp.where(first_long, length[1], length[0]).reshape(1)
    short = group_rows - longest
    head_part = lax.dynamic_slice_in_dim(order, start, longest, 0)
    tail = jnp.where(jnp.arange(short) < start, order[:short], order[longest:])
    order = jnp.concatenate((head_part, tail))
    source, within = order // token_rows, order % token_rows
    idx = ((source % 2) * 2 + source // 2) * fsdp_count + within // piece
    idx = idx * full_piece + within % piece

    def half_cols(weight):
        return lax.dynamic_slice_in_dim(weight, c * part, part, 1)

    def half_ff(weight):
        split = weight.reshape(weight.shape[0], fsdp_count, 2, -1)
        return lax.dynamic_index_in_dim(split, c, 2, keepdims=False).reshape(weight.shape[0], -1)

    def gather(value, axis=0):
        return lax.all_gather(value, "fsdp", axis=axis, tiled=True)

    def line(value):
        return jnp.pad(value.astype(f32), ((0, 0), (0, lanes - value.shape[1])))

    small = jnp.concatenate([line(gain_attn[None]), line(gain_ff[None]), line(bias_table.T)])
    small = jnp.pad(small, ((0, 8 - small.shape[0]), (0, 0)))
    down_rows = w_down.shape[0] // 2
    weights = (
        jnp.concatenate([half_cols(w) for w in (w_query, w_key, w_value)], axis=1),
        w_out,
        jnp.concatenate([half_ff(w) for w in (w_gate, w_up)], axis=1),
        lax.dynamic_slice_in_dim(w_down, c * down_rows, down_rows, 0),
    )
    gathers = fsdp_count == 8 and all(w.shape[0] % 32 == 0 for w in weights)
    if not gathers:
        weights = tuple(gather(w) for w in weights)
    idx_row = idx.reshape(1, -1)
    args = (bound, idx_row, small, pieces(tokens), pieces(cotangent))
    xs, cs, qkv, p_long, p_short, ctx, ctx32, linv, gains, w_qkv, *late = attend(
        fsdp_count, gathers, *args, *(weights if gathers else weights[:1]))
    wo, w_gu, wd = late if gathers else weights[1:]
    buckets = band_buckets()
    output, grad_gu, grad_d, datt, dos, grad_o, grad_gain_ff = feed(
        fsdp_count, full_piece, idx_row, ctx, ctx32, linv, xs, cs, wo, gains, w_gu, wd)
    grad_tokens, small, *grads = back(
        fsdp_count, full_piece, gathers, idx_row, xs, gains, grad_gain_ff, w_qkv, datt,
        dos, qkv, p_long, p_short, (grad_gu, grad_d, grad_o))
    output, grad_tokens = (x[:, :, :piece].reshape(tokens.shape) for x in (output, grad_tokens))
    own_gain = width // fsdp_count
    f = lax.axis_index("fsdp")
    labels = bias_table.shape[0]
    bias_grad = lax.dynamic_slice_in_dim(small[:labels], s * local_heads, local_heads, 1)
    gain_grads = [
        lax.dynamic_slice_in_dim(
            small[first : first + width // lanes].reshape(-1), f * own_gain, own_gain, 0)
        for first in (labels, labels + 8)
    ]
    if not gathers:
        grads = scatter_rows(fsdp_count, c, (grad_gu, grad_d, grad_o, *grads))
    grad_gate, grad_up, grad_down, grad_out, grad_query, grad_key, grad_value = grads
    return (
        output, grad_tokens, gain_grads[0], grad_query, grad_key, grad_value, grad_out, bias_grad,
        gain_grads[1], grad_gate, grad_up, grad_down,
    )


def scatter_rows(fsdp_count, c, partial_grads):
    sibling = [(0, 1), (1, 0), (2, 3), (3, 2)]
    across = [(0, 2), (2, 0), (1, 3), (3, 1)]
    shares = [lax.psum_scatter(v, "fsdp", scatter_dimension=0, tiled=True) for v in partial_grads]
    shares = [v.astype(f32) + lax.ppermute(v, "sp", across).astype(f32) for v in shares]
    shares = [v.astype(bf16) for v in shares]
    others = [lax.ppermute(v, "sp", sibling) for v in shares]
    sides = [
        (jnp.where(c == 0, v, w).astype(f32), jnp.where(c == 0, w, v).astype(f32))
        for v, w in zip(shares, others)
    ]
    gu, down, out, *qkv = sides
    rows = gu[0].shape[0]
    ff = gu[0].shape[1] // 2

    def ff_cols(which):
        cut = [x[:, which * ff : (which + 1) * ff].reshape(rows, fsdp_count, 1, -1) for x in gu]
        return jnp.concatenate(cut, axis=2).reshape(rows, -1)

    def proj(kind):
        return jnp.concatenate(
            [pair[side][:, kind * lanes : (kind + 1) * lanes] for side in range(2) for pair in qkv],
            axis=1)

    return (ff_cols(0), ff_cols(1), jnp.concatenate(down), jnp.concatenate(out, axis=1),
            proj(0), proj(1), proj(2))


def solution(mesh):
    return jax.shard_map(
        shards,
        mesh=mesh,
        in_specs=(
            P(None, ("fsdp", "sp"), None), P(None, ("fsdp", "sp"), None),
            P(None, "fsdp", None), P(None, "fsdp", None),
            P("fsdp"), P("fsdp", None), P("fsdp", None), P("fsdp", None), P("fsdp", None),
            P(None, "sp"), P("fsdp"), P("fsdp", None), P("fsdp", None), P("fsdp", None),
        ),
        out_specs=(
            P(None, ("fsdp", "sp"), None), P(None, ("fsdp", "sp"), None),
            P("fsdp"), P("fsdp", None), P("fsdp", None), P("fsdp", None), P("fsdp", None),
            P(None, "sp"), P("fsdp"), P("fsdp", None), P("fsdp", None), P("fsdp", None),
        ),
        check_vma=False,
    )
```
